256 devices in a mesh: inst: 4 (over x_lo, core), space: 64 (over x_hi, z, y).
Axes of the slice: x: 4 (x_hi: 2, x_lo: 2; x = x_hi * 2 + x_lo), y: 4, z: 8, core: 2. Of those that a mesh axis runs over, the one named last changes fastest.
Arguments:
- flow_state: float32 [8, 5, 4096, 256], P('inst', None, 'space'), may hold values from -6 to 6
- flow_source: float32 [8, 5, 4096, 256], P('inst', None, 'space'), may hold values from -6 to 6
- pseudo_step: float32 [4096, 256], P('space'), may hold values from 0.03 to 0.12
- flux_jacobian: float32 [5, 5], replicated, may hold values from -2.5 to 2.5
- stator_donor: int32 [8, 4096], P('inst', 'space'), may hold values from 0 to 4095, as said below
- stator_weight: float32 [8, 4096], P('inst', 'space'), may hold values from 0 to 1
- rotor_donor: int32 [8, 4096], P('inst', 'space'), may hold values from 0 to 4095, as said below
- rotor_weight: float32 [8, 4096], P('inst', 'space'), may hold values from 0 to 1
Outputs:
- new_state: float32 [8, 5, 4096, 256], P('inst', None, 'space')
- residual: float32 [8, 5, 4096, 256], P('inst', None, 'space')
The draws below stay inside these ranges and needn't reach their ends.
Inputs may be any that keep to these rules, and one draw needn't show every extreme that they name: `stator_donor`: for each instance n the row holds the rotation j -> (j - shift_n) mod 4096 of the rows, so entry j is (j - stator_shift_n) mod 4096, where stator_shift_n is a shift of its own for each instance. `rotor_donor`: for each instance n the row holds the rotation j -> (j + shift_n) mod 4096 of the rows, so entry j is (j + rotor_shift_n) mod 4096, where rotor_shift_n is a shift of its own for each instance, independent of stator_shift_n.
All inputs are finite; a program needn't handle non-finite values.
Results may differ from the reference program's by a relative error of at most 0.0001.
Values sent between devices are 32-bit elements; how exact they have to be, the bound alone decides.
A program may use at most 128 MiB of HBM per device.

```python
import math
import jax
import jax.numpy as jnp
from jax import lax

NT = 8
VARS = 5
SWEEPS = 2
AX = 256
NC = 4096


def draw_stator_donor(key, part):
    key = jax.random.fold_in(key, 11)
    shifts = jax.random.randint(key, (NT, 1), 0, NC)
    rows = jnp.arange(NC, dtype=jnp.int32)[None, :]
    return ((rows - shifts) % NC).astype(jnp.int32)


def draw_rotor_donor(key, part):
    key = jax.random.fold_in(key, 23)
    shifts = jax.random.randint(key, (NT, 1), 0, NC)
    rows = jnp.arange(NC, dtype=jnp.int32)[None, :]
    return ((rows + shifts) % NC).astype(jnp.int32)


def block_levels(stream_key, shape, split, smallest, largest):
    level = 1.0
    for dim, shards_of in split:
        heights = jax.random.uniform(jax.random.fold_in(jax.random.fold_in(stream_key, 6), dim), (shards_of,), jnp.float32, smallest / len(split), largest / len(split))
        level = level * jnp.repeat(jnp.exp(heights), shape[dim] // shards_of).reshape((-1,) + (1,) * (len(shape) - 1 - dim))
    return level


def centred(rng, dims, spread, most, cuts=(), held_as=jnp.bfloat16):
    values = spread * jax.random.normal(rng, dims, jnp.float32)
    if cuts:
        values = values * block_levels(rng, dims, cuts, -0.22, 0.18)
    return jnp.clip(values, -most, most).astype(held_as)


def setup_inputs(seed: int = 0) -> dict:
    streams_of = jax.random.split(jax.random.key(seed), 9)
    flow_state = centred(streams_of[0], (NT, VARS, NC, AX), 1.0, 6.0, ((0, 4), (2, 64)), jnp.float32)
    flow_source = centred(streams_of[1], (NT, VARS, NC, AX), 1.0, 6.0, ((0, 4), (2, 64)), jnp.float32)
    pseudo_step = jnp.clip(jnp.exp(math.log(0.12) - 1.3862944 * jax.random.uniform(streams_of[2], (NC, AX), jnp.float32) ** block_levels(streams_of[2], (NC, AX), ((0, 64),), -0.2, 0.2)), 0.03, 0.12)
    flux_jacobian = centred(streams_of[3], (VARS, VARS), VARS ** -0.5, 2.5, (), jnp.float32)
    stator_donor = draw_stator_donor(jax.random.fold_in(streams_of[8], 71), 0)
    stator_weight = jnp.clip(1.0 * jax.random.uniform(streams_of[5], (NT, NC), jnp.float32) ** block_levels(streams_of[5], (NT, NC), ((0, 4), (1, 64)), -0.2, 0.2), 0.0, 1.0)
    rotor_donor = draw_rotor_donor(jax.random.fold_in(streams_of[8], 71), 0)
    rotor_weight = jnp.clip(1.0 * jax.random.uniform(streams_of[7], (NT, NC), jnp.float32) ** block_levels(streams_of[7], (NT, NC), ((0, 4), (1, 64)), -0.2, 0.2), 0.0, 1.0)
    return {"flow_state": flow_state, "flow_source": flow_source, "pseudo_step": pseudo_step, "flux_jacobian": flux_jacobian, "stator_donor": stator_donor, "stator_weight": stator_weight, "rotor_donor": rotor_donor, "rotor_weight": rotor_weight}


viscosity = 0.5


def spectral_table(count):
    rows = jnp.arange(count, dtype=jnp.int32)[:, None]
    columns = jnp.arange(count, dtype=jnp.int32)[None, :]
    gap = rows - columns
    parity = (1 - 2 * (gap % 2)).astype(jnp.float32)
    angle = (math.pi / count) * gap.astype(jnp.float32)
    sine = jnp.where(gap == 0, jnp.float32(1.0), jnp.sin(angle))
    value = 0.5 * parity * jnp.cos(angle) / sine
    return jnp.where(gap == 0, jnp.float32(0.0), value).astype(jnp.float32)


def interpolate(column, donor, weight):
    total = column.shape[2]
    first = jnp.take_along_axis(column, donor[:, None, :], axis=2)
    second = jnp.take_along_axis(column, ((donor + 1) % total)[:, None, :], axis=2)
    return (1.0 - weight)[:, None, :] * first + weight[:, None, :] * second


def spatial(flow, upper, lower, stator_in, rotor_in, flux_jacobian):
    half = flow.shape[3] // 2
    zero_col = jnp.zeros(flow.shape[:3] + (1,), jnp.float32)
    left_cells = jnp.concatenate([zero_col, flow[..., :-1]], axis=3).at[..., half].set(stator_in)
    right_cells = jnp.concatenate([flow[..., 1:], zero_col], axis=3).at[..., half - 1].set(rotor_in)
    convect = jnp.einsum("vw,nwca->nvca", flux_jacobian, flow - left_cells, precision=lax.Precision.HIGHEST)
    return convect + viscosity * (4.0 * flow - left_cells - right_cells - upper - lower)


def reference(flow_state, flow_source, pseudo_step, flux_jacobian, stator_donor, stator_weight, rotor_donor, rotor_weight):
    table = spectral_table(NT)
    flow = flow_state
    half = flow.shape[3] // 2
    residual = flow
    for sweep in range(SWEEPS):
        stator_in = interpolate(flow[..., half - 1], stator_donor, stator_weight)
        rotor_in = interpolate(flow[..., half], rotor_donor, rotor_weight)
        upper = jnp.roll(flow, 1, axis=2)
        lower = jnp.roll(flow, -1, axis=2)
        derivative = jnp.einsum("nm,mvca->nvca", table, flow, precision=lax.Precision.HIGHEST)
        residual = spatial(flow, upper, lower, stator_in, rotor_in, flux_jacobian) + derivative - flow_source
        flow = flow - pseudo_step[None, None] * residual
    return flow, residual
```

```python
import math

import jax
import jax.numpy as jnp
from jax import lax
from jax.experimental import pallas as pl
from jax.experimental.pallas import tpu as pltpu
from jax.sharding import PartitionSpec as P

MESH = pl.DeviceIdType.MESH
NT = 8
NV = 5
ROWS = 64
AX = 256
LANES = 128
CHUNK = 8
CHUNKS = ROWS // CHUNK
SX, SZ, SY = 2, 8, 4
SPACE = SX * SZ * SY
PLANE = SX * SY
VISCOSITY = 0.5


def spectral(gap):
    gap = gap % NT
    if gap == 0:
        return 0.0
    return 0.5 * (-1.0) ** gap * math.cos(math.pi * gap / NT) / math.sin(math.pi * gap / NT)


def kernel(
    flow_hbm, source_hbm, step_hbm, jac, stator_donor, stator_weight, rotor_donor, rotor_weight,
    state_hbm, resid_hbm,
    flow0, flow1, source, step, sib0, sib1, send0, send1, recv0, recv1, out_state, out_resid,
    corner, plane0, plane1, ring0, ring1, inflow,
    load_sem, out_sem, sib_ssem, sib_rsem, par_ssem, par_rsem, halo_ssem, halo_rsem,
    plane_ssem, plane_rsem, ring_ssem, ring_rsem,
):
    inst, space = lax.axis_index("inst"), lax.axis_index("space")
    pair, core = inst // 2, inst % 2
    x, z, y = space // (SZ * SY), (space // SY) % SZ, space % SY
    sibling = (pair * 2 + 1 - core, space)
    partner = ((1 - pair) * 2 + core, space)
    above = (inst, (space + SPACE - 1) % SPACE)
    below = (inst, (space + 1) % SPACE)
    slot = x * SY + y
    planes, rings = (plane0, plane1), (ring0, ring1)

    def plane_peer(k):
        other = (slot + k) % PLANE
        return other, (inst, (other // SY) * (SZ * SY) + z * SY + other % SY)

    def ring_peer(k):
        other = (z + k) % SZ
        return other, (inst, x * (SZ * SY) + other * SY + y)

    flow_in = pltpu.make_async_copy(flow_hbm, flow0.at[:, :, pl.ds(CHUNK, ROWS), :], load_sem.at[0])
    source_in = pltpu.make_async_copy(source_hbm, source, load_sem.at[1])
    step_in = pltpu.make_async_copy(step_hbm, step, load_sem.at[2])
    flow_in.start()
    source_in.start()
    step_in.start()

    barrier = pltpu.get_barrier_semaphore()
    greeted = [sibling, partner, above, below]
    greeted += [plane_peer(k)[1] for k in range(1, PLANE)]
    greeted += [ring_peer(k)[1] for k in range(1, SZ)]
    for device in greeted:
        pl.semaphore_signal(barrier, inc=1, device_id=device, device_id_type=MESH)

    lane = lax.broadcasted_iota(jnp.int32, (CHUNK, LANES), 1)
    low = lane < ROWS

    def scalars(table):
        return [[table(a - b) for b in range(2)] for a in range(2)]

    from_own = scalars(spectral)
    from_sib = scalars(lambda g: jnp.where(core == 0, spectral(g - 2), spectral(g + 2)).astype(jnp.float32))
    to_own = scalars(lambda g: spectral(g + 4))
    to_sib = scalars(lambda g: jnp.where(core == 0, spectral(g + 2), spectral(g + 6)).astype(jnp.float32))

    def remote(src, dst, ssem, rsem, device):
        return pltpu.make_async_remote_copy(
            src_ref=src, dst_ref=dst, send_sem=ssem, recv_sem=rsem, device_id=device, device_id_type=MESH
        )

    def rows_at(g):
        return pl.ds(pl.multiple_of(CHUNK + g * CHUNK, CHUNK), CHUNK)

    def sib_copy(sweep, g):
        flow, sib = (flow0, sib0) if sweep == 0 else (flow1, sib1)
        at = sweep * CHUNKS + g
        return remote(flow.at[:, :, rows_at(g), :], sib.at[g], sib_ssem.at[at], sib_rsem.at[at], sibling)

    def par_copy(sweep, g):
        send, recv = (send0, recv0) if sweep == 0 else (send1, recv1)
        at = sweep * CHUNKS + g
        return remote(send.at[g], recv.at[g], par_ssem.at[at], par_rsem.at[at], partner)

    def halo_copies(sweep):
        flow = flow0 if sweep == 0 else flow1
        first = flow.at[:, :, pl.ds(CHUNK, 1), :]
        last = flow.at[:, :, pl.ds(CHUNK + ROWS - 1, 1), :]
        before = flow.at[:, :, pl.ds(CHUNK - 1, 1), :]
        after = flow.at[:, :, pl.ds(CHUNK + ROWS, 1), :]
        up, down = 2 * sweep, 2 * sweep + 1
        return (
            remote(first, after, halo_ssem.at[up], halo_rsem.at[up], above),
            remote(last, before, halo_ssem.at[down], halo_rsem.at[down], below),
        )

    def plane_copy(sweep, k):
        _, device = plane_peer(k)
        mine = planes[sweep].at[slot]
        return remote(mine, mine, plane_ssem.at[sweep * PLANE + k], plane_rsem.at[sweep * PLANE + slot], device)

    def plane_arrival(sweep, k):
        other, device = plane_peer(k)
        theirs = planes[sweep].at[other]
        return remote(theirs, theirs, plane_ssem.at[sweep * PLANE + k], plane_rsem.at[sweep * PLANE + other], device)

    def ring_copy(sweep, k):
        _, device = ring_peer(k)
        mine = rings[sweep].at[z]
        return remote(mine, mine, ring_ssem.at[sweep * SZ + k], ring_rsem.at[sweep * SZ + z], device)

    def ring_arrival(sweep, k):
        other, device = ring_peer(k)
        theirs = rings[sweep].at[other]
        return remote(theirs, theirs, ring_ssem.at[sweep * SZ + k], ring_rsem.at[sweep * SZ + other], device)

    def extract(sweep):
        flow = flow0 if sweep == 0 else flow1

        def body(g, _):
            for n in range(2):
                total = jnp.zeros((CHUNK, LANES), jnp.float32)
                for c in range(2):
                    for v in range(NV):
                        tile = flow[n, v, rows_at(g), pl.ds(c * LANES, LANES)]
                        q = c * CHUNK + v
                        turned = pltpu.roll(tile, (q + 1) if c == 0 else q, axis=1)
                        total = jnp.where(lane == q, turned, total)
                corner[pl.ds(pl.multiple_of(n * ROWS + g * CHUNK, CHUNK), CHUNK), :] = total
            return 0

        lax.fori_loop(0, CHUNKS, body, 0)
        planes[sweep][slot] = corner[...].T[0 : 2 * CHUNK, :]

    def donor(c, n):
        return (stator_donor if c == 0 else rotor_donor)[n, 0]

    def forward(sweep):
        for c in range(2):
            for n in range(2):
                ahead = (donor(c, n) // ROWS + SPACE - space) % SPACE
                halves = []
                for d in (ahead, (ahead + 1) % SPACE):
                    dx, dz, dy = d // (SZ * SY), (d // SY) % SZ, d % SY
                    carry = (y + dy) // SY
                    wants = (z + 2 * SZ - dz - carry) % SZ
                    over = (wants + dz + carry) // SZ
                    pick = ((x + dx + over) % SX) * SY + (y + dy) % SY
                    halves.append(planes[sweep][pick, pl.ds(c * CHUNK, CHUNK), :])
                first, second = halves
                if n == 0:
                    both = jnp.where(low, first, pltpu.roll(second, ROWS, axis=1))
                else:
                    both = jnp.where(low, pltpu.roll(first, ROWS, axis=1), second)
                rings[sweep][z, pl.ds((c * 2 + n) * CHUNK, CHUNK), :] = both

    def interpolate(sweep):
        corner[...] = jnp.zeros_like(corner)
        for c in range(2):
            weights = stator_weight if c == 0 else rotor_weight
            for n in range(2):
                start = donor(c, n)
                block = start // ROWS
                group = pl.ds((c * 2 + n) * CHUNK, CHUNK)
                here = rings[sweep][(block // SY) % SZ, group, :]
                there = rings[sweep][((block + 1) // SY) % SZ, group, :]
                window = jnp.where(low, here, there)
                offset = start % ROWS
                first = pltpu.roll(window, (LANES - offset) % LANES, axis=1)
                second = pltpu.roll(window, LANES - 1 - offset, axis=1)
                weight = weights[pl.ds(n, 1), :]
                weight = jnp.concatenate([weight, weight], axis=1)
                corner[group, :] = (1.0 - weight) * first + weight * second
        inflow[...] = corner[...].T[0:ROWS, :]

    def mix(sweep, g):
        flow, sib, send = (flow0, sib0, send0) if sweep == 0 else (flow1, sib1, send1)
        for v in range(NV):
            for t in range(2):
                at = pl.ds(t * LANES, LANES)
                own = [flow[n, v, rows_at(g), at] for n in range(2)]
                other = [sib[g, n, v, :, at] for n in range(2)]
                for a in range(2):
                    send[g, a, v, :, at] = (
                        to_own[a][0] * own[0] + to_own[a][1] * own[1]
                        + (to_sib[a][0] * other[0] + to_sib[a][1] * other[1])
                    )

    jacobian = [[jac[v, w] for w in range(NV)] for v in range(NV)]

    def advance(sweep, g):
        flow, sib, recv = (flow0, sib0, recv0) if sweep == 0 else (flow1, sib1, recv1)
        here = pl.ds(pl.multiple_of(g * CHUNK, CHUNK), CHUNK)
        entering = inflow[here, :]
        for t in range(2):
            at = pl.ds(t * LANES, LANES)
            pace = step[here, at]
            centre = []
            for n in range(2):
                centre.append([flow[n, v, rows_at(g), at] for v in range(NV)])
            for n in range(2):
                diff, smooth = [], []
                for v in range(NV):
                    window = flow[n, v, pl.ds(pl.multiple_of(g * CHUNK, CHUNK), 3 * CHUNK), at]
                    upper = window[CHUNK - 1 : 2 * CHUNK - 1]
                    lower = window[CHUNK + 1 : 2 * CHUNK + 1]
                    f = centre[n][v]
                    left, right = pltpu.roll(f, 1, axis=1), pltpu.roll(f, LANES - 1, axis=1)
                    q = (1 - t) * 2 * CHUNK + n * CHUNK + v
                    if t == 0:
                        q = 2 * CHUNK + n * CHUNK + v
                        left = jnp.where(lane == 0, 0.0, left)
                        right = jnp.where(lane == LANES - 1, pltpu.roll(entering, LANES - 1 - q, axis=1), right)
                    else:
                        q = n * CHUNK + v
                        left = jnp.where(lane == 0, pltpu.roll(entering, (LANES - q) % LANES, axis=1), left)
                        right = jnp.where(lane == LANES - 1, 0.0, right)
                    diff.append(f - left)
                    smooth.append(VISCOSITY * (4.0 * f - left - right - upper - lower))
                for v in range(NV):
                    convect = jacobian[v][0] * diff[0]
                    for w in range(1, NV):
                        convect = convect + jacobian[v][w] * diff[w]
                    derivative = (
                        from_own[n][0] * centre[0][v] + from_own[n][1] * centre[1][v]
                        + (from_sib[n][0] * sib[g, 0, v, :, at] + from_sib[n][1] * sib[g, 1, v, :, at])
                        + recv[g, n, v, :, at]
                    )
                    residual = convect + smooth[v] + derivative - source[n, v, here, at]
                    new = centre[n][v] - pace * residual
                    if sweep == 0:
                        flow1[n, v, rows_at(g), at] = new
                    else:
                        out_state[g, n, v, :, at] = new
                        out_resid[g, n, v, :, at] = residual

    def loop(body):
        def wrapped(g, carry):
            body(g)
            return carry

        lax.fori_loop(0, CHUNKS, wrapped, 0)

    def out_copies(g):
        here = pl.ds(pl.multiple_of(g * CHUNK, CHUNK), CHUNK)
        return (
            pltpu.make_async_copy(out_state.at[g], state_hbm.at[:, :, here, :], out_sem.at[g]),
            pltpu.make_async_copy(out_resid.at[g], resid_hbm.at[:, :, here, :], out_sem.at[CHUNKS + g]),
        )

    flow_in.wait()
    extract(0)
    pl.semaphore_wait(barrier, len(greeted))

    def start_sib(g):
        sib_copy(0, g).start()

    loop(start_sib)
    for k in range(1, PLANE):
        plane_copy(0, k).start()
    for copy in halo_copies(0):
        copy.start()

    def first_mix(g):
        sib_copy(0, g).wait_recv()
        mix(0, g)
        par_copy(0, g).start()

    loop(first_mix)

    def interface(sweep):
        for k in range(1, PLANE):
            plane_arrival(sweep, k).wait_recv()
        forward(sweep)
        for k in range(1, SZ):
            ring_copy(sweep, k).start()
        for k in range(1, SZ):
            ring_arrival(sweep, k).wait_recv()
        interpolate(sweep)

    interface(0)
    for copy in halo_copies(0):
        copy.wait_recv()
    source_in.wait()
    step_in.wait()

    def second_mix(g):
        sib_copy(1, g).wait_recv()
        mix(1, g)
        par_copy(1, g).start()

    def first_sweep(g):
        par_copy(0, g).wait_recv()
        advance(0, g)
        sib_copy(1, g).start()

        @pl.when(g > 0)
        def _():
            second_mix(g - 1)

    loop(first_sweep)
    for copy in halo_copies(1):
        copy.start()
    extract(1)
    for k in range(1, PLANE):
        plane_copy(1, k).start()
    second_mix(CHUNKS - 1)
    interface(1)
    for copy in halo_copies(1):
        copy.wait_recv()

    def second_sweep(g):
        par_copy(1, g).wait_recv()
        advance(1, g)
        for copy in out_copies(g):
            copy.start()

    loop(second_sweep)

    def finish(g):
        for sweep in range(2):
            sib_copy(sweep, g).wait_send()
            par_copy(sweep, g).wait_send()
        for copy in out_copies(g):
            copy.wait()

    loop(finish)
    for sweep in range(2):
        for copy in halo_copies(sweep):
            copy.wait_send()
        for k in range(1, PLANE):
            plane_copy(sweep, k).wait_send()
        for k in range(1, SZ):
            ring_copy(sweep, k).wait_send()


def local(flow_state, flow_source, pseudo_step, flux_jacobian, stator_donor, stator_weight, rotor_donor, rotor_weight):
    f32 = jnp.float32
    block = (2, NV, ROWS, AX)
    padded = (2, NV, ROWS + 2 * CHUNK, AX)
    chunked = (CHUNKS, 2, NV, CHUNK, AX)
    anywhere = pl.BlockSpec(memory_space=pl.ANY)
    smem = pl.BlockSpec(memory_space=pltpu.SMEM)
    vmem = pl.BlockSpec(memory_space=pltpu.VMEM)
    dma = pltpu.SemaphoreType.DMA
    return pl.pallas_call(
        kernel,
        out_shape=(jax.ShapeDtypeStruct(block, f32), jax.ShapeDtypeStruct(block, f32)),
        in_specs=[anywhere, anywhere, anywhere, smem, smem, vmem, smem, vmem],
        out_specs=(anywhere, anywhere),
        scratch_shapes=[
            pltpu.VMEM(padded, f32),
            pltpu.VMEM(padded, f32),
            pltpu.VMEM(block, f32),
            pltpu.VMEM((ROWS, AX), f32),
            *[pltpu.VMEM(chunked, f32) for _ in range(8)],
            pltpu.VMEM((LANES, LANES), f32),
            *[pltpu.VMEM((PLANE, 2 * CHUNK, LANES), f32) for _ in range(2)],
            *[pltpu.VMEM((SZ, 4 * CHUNK, LANES), f32) for _ in range(2)],
            pltpu.VMEM((ROWS, LANES), f32),
            dma((3,)),
            dma((2 * CHUNKS,)),
            dma((2 * CHUNKS,)),
            dma((2 * CHUNKS,)),
            dma((2 * CHUNKS,)),
            dma((2 * CHUNKS,)),
            dma((4,)),
            dma((4,)),
            dma((2 * PLANE,)),
            dma((2 * PLANE,)),
            dma((2 * SZ,)),
            dma((2 * SZ,)),
        ],
        compiler_params=pltpu.CompilerParams(
            collective_id=0, has_side_effects=True, vmem_limit_bytes=24 * 2**20
        ),
    )(flow_state, flow_source, pseudo_step, flux_jacobian, stator_donor, stator_weight, rotor_donor, rotor_weight)


def solution(mesh):
    return jax.shard_map(
        local,
        mesh=mesh,
        in_specs=(
            P("inst", None, "space", None),
            P("inst", None, "space", None),
            P("space", None),
            P(),
            P("inst", "space"),
            P("inst", "space"),
            P("inst", "space"),
            P("inst", "space"),
        ),
        out_specs=(P("inst", None, "space", None), P("inst", None, "space", None)),
        check_vma=False,
    )
```

```python
import math

import jax
import jax.numpy as jnp
from jax import lax
from jax.experimental import pallas as pl
from jax.experimental.pallas import tpu as pltpu
from jax.sharding import PartitionSpec as P

MESH = pl.DeviceIdType.MESH
NT = 8
NV = 5
ROWS = 64
AX = 256
LANES = 128
CHUNK = 8
CHUNKS = ROWS // CHUNK
SX, SZ, SY = 2, 8, 4
SPACE = SX * SZ * SY
PLANE = SX * SY
VISCOSITY = 0.5
AT_PLANES, AT_RINGS, AT_HALOS = 3, 5, 6


def spectral(gap):
    gap = gap % NT
    if gap == 0:
        return 0.0
    return 0.5 * (-1.0) ** gap * math.cos(math.pi * gap / NT) / math.sin(math.pi * gap / NT)


def kernel(
    flow_hbm, source_hbm, step_hbm, *rest,
):
    *small_hbm, out_state, out_resid = rest[:7]
    body(flow_hbm, source_hbm, step_hbm, small_hbm, out_state, out_resid, *rest[7:])


def body(
    flow_hbm, source_hbm, step_hbm, small_hbm, out_state, out_resid,
    jac, stator_donor, stator_weight, rotor_donor, rotor_weight,
    flow0, flow1, source, step, sib0, sib1, send0, send1, recv0, recv1,
    corner, plane0, plane1, ring0, ring1, inflow, columns, remote_part,
    halo_out0, halo_out1, halo_in0, halo_in1,
    known, load_sem, sib_ssem, sib_rsem, par_ssem, par_rsem, halo_ssem, halo_rsem,
    plane_ssem, plane_rsem, ring_ssem, ring_rsem, column_ssem, column_rsem,
):
    inst, space = lax.axis_index("inst"), lax.axis_index("space")
    pair, core = inst // 2, inst % 2
    x, z, y = space // (SZ * SY), (space // SY) % SZ, space % SY
    sibling = (pair * 2 + 1 - core, space)
    partner = ((1 - pair) * 2 + core, space)
    diagonal = ((1 - pair) * 2 + 1 - core, space)
    across = (inst, (space + SPACE // 2) % SPACE)
    middle = ((1 - pair) * 2 + core, (space + SPACE // 2) % SPACE)
    above = (inst, (space + SPACE - 1) % SPACE)
    below = (inst, (space + 1) % SPACE)
    slot = x * SY + y
    planes, rings = (plane0, plane1), (ring0, ring1)

    def plane_peer(k):
        other = (slot + k) % PLANE
        return other, (inst, (other // SY) * (SZ * SY) + z * SY + other % SY)

    def ring_peer(k):
        other = (z + k) % SZ
        return other, (inst, x * (SZ * SY) + other * SY + y)

    flow_in = pltpu.make_async_copy(flow_hbm, flow0.at[:, :, pl.ds(CHUNK, ROWS), :], load_sem.at[0])
    source_in = pltpu.make_async_copy(source_hbm, source, load_sem.at[1])
    step_in = pltpu.make_async_copy(step_hbm, step, load_sem.at[2])
    flow_in.start()
    source_in.start()
    step_in.start()
    small = (jac, stator_donor, stator_weight, rotor_donor, rotor_weight)
    small_in = [
        pltpu.make_async_copy(src, dst, load_sem.at[3 + k]) for k, (src, dst) in enumerate(zip(small_hbm, small))
    ]
    for copy in small_in:
        copy.start()

    def on_line(k, along_y, along_z):
        out = []
        if along_y:
            out += [(y >= k, (inst, space - k)), (y < SY - k, (inst, space + k))]
        if along_z:
            out += [(z >= k, (inst, space - k * SY)), (z < SZ - k, (inst, space + k * SY))]
        return out

    always = space >= 0
    nearest = [(always, partner), (x != pair, middle)] + on_line(1, True, True)

    def tell(semaphore, devices):
        for exists, device in devices:

            @pl.when(exists)
            def _(device=device):
                pl.semaphore_signal(semaphore, inc=1, device_id=device, device_id_type=MESH)

    def hear(semaphore, devices):
        count = 0
        for exists, _ in devices:
            count = count + exists.astype(jnp.int32)
        pl.semaphore_wait(semaphore, count)

    rounds = [nearest, on_line(2, True, True), on_line(4, False, True) + [(always, across)]]
    barrier = pltpu.get_barrier_semaphore()
    greeted = [(always, sibling)] + nearest
    tell(barrier, greeted)

    lane = lax.broadcasted_iota(jnp.int32, (CHUNK, LANES), 1)
    low = lane < ROWS

    def scalars(table):
        return [[table(a - b) for b in range(2)] for a in range(2)]

    from_own = scalars(spectral)
    from_sib = scalars(lambda g: jnp.where(core == 0, spectral(g - 2), spectral(g + 2)).astype(jnp.float32))
    to_own = scalars(lambda g: spectral(g + 4))
    to_sib = scalars(lambda g: jnp.where(core == 0, spectral(g + 2), spectral(g + 6)).astype(jnp.float32))

    def remote(src, dst, ssem, rsem, device):
        return pltpu.make_async_remote_copy(
            src_ref=src, dst_ref=dst, send_sem=ssem, recv_sem=rsem, device_id=device, device_id_type=MESH
        )

    def rows_at(g):
        return pl.ds(pl.multiple_of(CHUNK + g * CHUNK, CHUNK), CHUNK)

    def sib_copy(sweep, g):
        flow, sib = (flow0, sib0) if sweep == 0 else (flow1, sib1)
        at = sweep * CHUNKS + g
        return remote(flow.at[:, :, rows_at(g), :], sib.at[g], sib_ssem.at[at], sib_rsem.at[at], sibling)

    def par_copy(sweep, g):
        send, recv = (send0, recv0) if sweep == 0 else (send1, recv1)
        at = sweep * CHUNKS + g
        return remote(send.at[g], recv.at[g], par_ssem.at[at], par_rsem.at[at], partner)

    halos_out, halos_in = (halo_out0, halo_out1), (halo_in0, halo_in1)

    def halo_copies(sweep):
        out, into = halos_out[sweep], halos_in[sweep]
        up, down = 2 * sweep, 2 * sweep + 1
        return (
            remote(out.at[0], into.at[1], halo_ssem.at[up], halo_rsem.at[up], above),
            remote(out.at[1], into.at[0], halo_ssem.at[down], halo_rsem.at[down], below),
        )

    def pack_halos(sweep):
        flow, out = (flow0 if sweep == 0 else flow1), halos_out[sweep]
        for side, row in enumerate((CHUNK, CHUNK + ROWS - 1)):
            for n in range(2):
                for v in range(NV):
                    out[side, n, pl.ds(v, 1), :] = flow[n, v, pl.ds(row, 1), :]

    def unpack_halos(sweep):
        flow, into = (flow0 if sweep == 0 else flow1), halos_in[sweep]
        for copy in halo_copies(sweep):
            copy.wait_recv()
        for side, row in enumerate((CHUNK - 1, CHUNK + ROWS)):
            for n in range(2):
                for v in range(NV):
                    flow[n, v, pl.ds(row, 1), :] = into[side, n, pl.ds(v, 1), :]

    def column_copies():
        mine = plane1.at[slot]
        return [
            remote(mine, columns.at[k], column_ssem.at[k], column_rsem.at[k], device)
            for k, device in enumerate((sibling, partner, diagonal))
        ]

    def plane_copy(sweep, k):
        _, device = plane_peer(k)
        mine = planes[sweep].at[slot]
        return remote(mine, mine, plane_ssem.at[sweep * PLANE + k], plane_rsem.at[sweep * PLANE + slot], device)

    def plane_arrival(sweep, k):
        other, device = plane_peer(k)
        theirs = planes[sweep].at[other]
        return remote(theirs, theirs, plane_ssem.at[sweep * PLANE + k], plane_rsem.at[sweep * PLANE + other], device)

    def ring_copy(sweep, k):
        _, device = ring_peer(k)
        mine = rings[sweep].at[z]
        return remote(mine, mine, ring_ssem.at[sweep * SZ + k], ring_rsem.at[sweep * SZ + z], device)

    def ring_arrival(sweep, k):
        other, device = ring_peer(k)
        theirs = rings[sweep].at[other]
        return remote(theirs, theirs, ring_ssem.at[sweep * SZ + k], ring_rsem.at[sweep * SZ + other], device)

    def extract(sweep):
        flow = flow0 if sweep == 0 else flow1

        def body(g, _):
            for n in range(2):
                total = jnp.zeros((CHUNK, LANES), jnp.float32)
                for c in range(2):
                    for v in range(NV):
                        tile = flow[n, v, rows_at(g), pl.ds(c * LANES, LANES)]
                        q = c * CHUNK + v
                        turned = pltpu.roll(tile, (q + 1) if c == 0 else q, axis=1)
                        total = jnp.where(lane == q, turned, total)
                corner[pl.ds(pl.multiple_of(n * ROWS + g * CHUNK, CHUNK), CHUNK), :] = total
            return 0

        lax.fori_loop(0, CHUNKS, body, 0)
        planes[sweep][slot] = corner[...].T[0 : 2 * CHUNK, :]

    def donor(c, n):
        return (stator_donor if c == 0 else rotor_donor)[n, 0]

    def forward(sweep):
        for c in range(2):
            for n in range(2):
                ahead = (donor(c, n) // ROWS + SPACE - space) % SPACE
                halves = []
                for d in (ahead, (ahead + 1) % SPACE):
                    dx, dz, dy = d // (SZ * SY), (d // SY) % SZ, d % SY
                    carry = (y + dy) // SY
                    wants = (z + 2 * SZ - dz - carry) % SZ
                    over = (wants + dz + carry) // SZ
                    pick = ((x + dx + over) % SX) * SY + (y + dy) % SY
                    halves.append(planes[sweep][pick, pl.ds(c * CHUNK, CHUNK), :])
                first, second = halves
                if n == 0:
                    both = jnp.where(low, first, pltpu.roll(second, ROWS, axis=1))
                else:
                    both = jnp.where(low, pltpu.roll(first, ROWS, axis=1), second)
                rings[sweep][z, pl.ds((c * 2 + n) * CHUNK, CHUNK), :] = both

    def interpolate(sweep):
        corner[...] = jnp.zeros_like(corner)
        for c in range(2):
            weights = stator_weight if c == 0 else rotor_weight
            for n in range(2):
                start = donor(c, n)
                block = start // ROWS
                group = pl.ds((c * 2 + n) * CHUNK, CHUNK)
                here = rings[sweep][(block // SY) % SZ, group, :]
                there = rings[sweep][((block + 1) // SY) % SZ, group, :]
                window = jnp.where(low, here, there)
                offset = start % ROWS
                first = pltpu.roll(window, (LANES - offset) % LANES, axis=1)
                second = pltpu.roll(window, LANES - 1 - offset, axis=1)
                weight = weights[pl.ds(n, 1), :]
                weight = jnp.concatenate([weight, weight], axis=1)
                corner[group, :] = (1.0 - weight) * first + weight * second
        inflow[...] = corner[...].T[0:ROWS, :]

    def mix(sweep, g):
        flow, sib, send = (flow0, sib0, send0) if sweep == 0 else (flow1, sib1, send1)
        for v in range(NV):
            for t in range(2):
                at = pl.ds(t * LANES, LANES)
                own = [flow[n, v, rows_at(g), at] for n in range(2)]
                other = [sib[g, n, v, :, at] for n in range(2)]
                for a in range(2):
                    send[g, a, v, :, at] = (
                        to_own[a][0] * own[0] + to_own[a][1] * own[1]
                        + (to_sib[a][0] * other[0] + to_sib[a][1] * other[1])
                    )

    def advance(sweep, g):
        flow, sib, recv = (flow0, sib0, recv0) if sweep == 0 else (flow1, sib1, recv1)
        here = pl.ds(pl.multiple_of(g * CHUNK, CHUNK), CHUNK)
        jacobian = [[jac[v, w] for w in range(NV)] for v in range(NV)]
        entering = inflow[here, :] if sweep == 1 else None
        for t in range(2):
            at = pl.ds(t * LANES, LANES)
            pace = step[here, at]
            edge = lane == (LANES - 1 if t == 0 else 0)
            centre = []
            for n in range(2):
                centre.append([flow[n, v, rows_at(g), at] for v in range(NV)])
            for n in range(2):
                if sweep == 1:
                    fixed = remote_part[pl.ds(pl.multiple_of(n * ROWS + g * CHUNK, CHUNK), CHUNK), :]
                diff, smooth = [], []
                for v in range(NV):
                    window = flow[n, v, pl.ds(pl.multiple_of(g * CHUNK, CHUNK), 3 * CHUNK), at]
                    upper = window[CHUNK - 1 : 2 * CHUNK - 1]
                    lower = window[CHUNK + 1 : 2 * CHUNK + 1]
                    f = centre[n][v]
                    left, right = pltpu.roll(f, 1, axis=1), pltpu.roll(f, LANES - 1, axis=1)
                    enter_left = enter_right = 0.0
                    if sweep == 1:
                        if t == 0:
                            enter_right = pltpu.roll(entering, LANES - 1 - (2 * CHUNK + n * CHUNK + v), axis=1)
                        else:
                            enter_left = pltpu.roll(entering, (LANES - n * CHUNK - v) % LANES, axis=1)
                    left = jnp.where(lane == 0, enter_left, left)
                    right = jnp.where(lane == LANES - 1, enter_right, right)
                    diff.append(f - left)
                    smooth.append(VISCOSITY * (4.0 * f - left - right - upper - lower))
                for v in range(NV):
                    convect = jacobian[v][0] * diff[0]
                    for w in range(1, NV):
                        convect = convect + jacobian[v][w] * diff[w]
                    others = (
                        from_sib[n][0] * sib[g, 0, v, :, at] + from_sib[n][1] * sib[g, 1, v, :, at]
                        + recv[g, n, v, :, at]
                    )
                    if sweep == 1:
                        turn = LANES - 1 - v if t == 0 else LANES - CHUNK - v
                        others = jnp.where(edge, pltpu.roll(fixed, turn, axis=1), others)
                    derivative = from_own[n][0] * centre[0][v] + from_own[n][1] * centre[1][v] + others
                    residual = convect + smooth[v] + derivative - source[n, v, here, at]
                    new = centre[n][v] - pace * residual
                    if sweep == 0:
                        flow1[n, v, rows_at(g), at] = new
                    else:
                        out_state[n, v, here, at] = new
                        out_resid[n, v, here, at] = residual

    def patch(g):
        here = pl.ds(pl.multiple_of(g * CHUNK, CHUNK), CHUNK)
        jacobian = [[jac[v, w] for w in range(NV)] for v in range(NV)]
        entering = inflow[here, :]
        for n in range(2):
            at = pl.ds(0, LANES)
            pace = jnp.where(lane == LANES - 1, step[here, at], 0.0)
            for v in range(NV):
                right = pltpu.roll(entering, LANES - 1 - (2 * CHUNK + n * CHUNK + v), axis=1)
                flow1[n, v, rows_at(g), at] = flow1[n, v, rows_at(g), at] + pace * (VISCOSITY * right)
            at = pl.ds(LANES, LANES)
            pace = jnp.where(lane == 0, step[here, at], 0.0)
            left = [pltpu.roll(entering, (LANES - n * CHUNK - v) % LANES, axis=1) for v in range(NV)]
            for v in range(NV):
                share = VISCOSITY * left[v]
                for w in range(NV):
                    share = share + jacobian[v][w] * left[w]
                flow1[n, v, rows_at(g), at] = flow1[n, v, rows_at(g), at] + pace * share

    def mix_columns():
        total = None
        for k, table in enumerate((from_sib, to_own, to_sib)):
            straight = columns[k]
            turned = pltpu.roll(straight, ROWS, axis=1)
            low2 = lax.broadcasted_iota(jnp.int32, (2 * CHUNK, LANES), 1) < ROWS
            same = jnp.where(low2, table[0][0], table[1][1])
            cross = jnp.where(low2, table[0][1], table[1][0])
            term = same * straight + cross * turned
            total = term if total is None else total + term
        corner[...] = jnp.zeros_like(corner)
        corner[pl.ds(0, 2 * CHUNK), :] = total
        remote_part[...] = corner[...].T

    def loop(body):
        def wrapped(g, carry):
            body(g)
            return carry

        lax.fori_loop(0, CHUNKS, wrapped, 0)

    def order(p):
        return (p + 1) % CHUNKS

    flow_in.wait()
    extract(0)
    pack_halos(0)
    hear(barrier, greeted)
    tell(known.at[0], rounds[0])
    loop(lambda p: sib_copy(0, order(p)).start())

    def first_mix(p):
        g = order(p)
        sib_copy(0, g).wait_recv()
        mix(0, g)
        par_copy(0, g).start()

    loop(first_mix)
    for copy in small_in:
        copy.wait()
    source_in.wait()
    step_in.wait()
    for k in range(2):
        hear(known.at[k], rounds[k])
        tell(known.at[k + 1], rounds[k + 1])

    def start_planes(sweep):
        for k in range(1, PLANE):
            plane_copy(sweep, k).start()

    def start_rings(sweep):
        for k in range(1, PLANE):
            plane_arrival(sweep, k).wait_recv()
        forward(sweep)
        for k in range(1, SZ):
            ring_copy(sweep, k).start()

    def finish_rings(sweep):
        for k in range(1, SZ):
            ring_arrival(sweep, k).wait_recv()
        interpolate(sweep)

    def second_mix(p):
        g = order(p)
        sib_copy(1, g).wait_recv()
        mix(1, g)
        par_copy(1, g).start()

    def first_sweep(p):
        g = order(p)

        @pl.when(p == AT_PLANES)
        def _():
            hear(known.at[2], rounds[2])
            start_planes(0)

        @pl.when(p == AT_RINGS)
        def _():
            start_rings(0)
            for copy in halo_copies(0):
                copy.start()

        @pl.when(p == AT_HALOS)
        def _():
            unpack_halos(0)

        par_copy(0, g).wait_recv()
        advance(0, g)
        sib_copy(1, g).start()

        @pl.when(p > 0)
        def _():
            second_mix(p - 1)

    loop(first_sweep)
    second_mix(CHUNKS - 1)
    finish_rings(0)
    loop(lambda p: sib_copy(1, order(p)).wait_send())
    loop(patch)
    extract(1)
    start_planes(1)
    pack_halos(1)
    for copy in halo_copies(1):
        copy.start()
    for copy in column_copies():
        copy.start()
    start_rings(1)
    unpack_halos(1)
    for copy in column_copies():
        copy.wait_recv()
    mix_columns()
    finish_rings(1)

    def second_sweep(p):
        g = order(p)
        par_copy(1, g).wait_recv()
        advance(1, g)

    loop(second_sweep)

    def finish(g):
        sib_copy(0, g).wait_send()
        for sweep in range(2):
            par_copy(sweep, g).wait_send()

    loop(finish)
    for copy in column_copies():
        copy.wait_send()
    for sweep in range(2):
        for copy in halo_copies(sweep):
            copy.wait_send()
        for k in range(1, PLANE):
            plane_copy(sweep, k).wait_send()
        for k in range(1, SZ):
            ring_copy(sweep, k).wait_send()


def store(state, resid, state_hbm, resid_hbm, sems):
    copies = [
        pltpu.make_async_copy(state, state_hbm, sems.at[0]),
        pltpu.make_async_copy(resid, resid_hbm, sems.at[1]),
    ]
    for copy in copies:
        copy.start()
    for copy in copies:
        copy.wait()


def local(flow_state, flow_source, pseudo_step, flux_jacobian, stator_donor, stator_weight, rotor_donor, rotor_weight):
    f32 = jnp.float32
    block = (2, NV, ROWS, AX)
    padded = (2, NV, ROWS + 2 * CHUNK, AX)
    chunked = (CHUNKS, 2, NV, CHUNK, AX)
    anywhere = pl.BlockSpec(memory_space=pltpu.HBM)
    vmem = pl.BlockSpec(memory_space=pltpu.VMEM)
    dma = pltpu.SemaphoreType.DMA
    regular = pltpu.SemaphoreType.REGULAR
    halo = (2, 2, NV, AX)
    args = (
        flow_state, flow_source, pseudo_step, flux_jacobian, stator_donor, stator_weight, rotor_donor, rotor_weight
    )
    state, resid = pl.pallas_call(
        kernel,
        out_shape=(pltpu.VMEM(block, f32), pltpu.VMEM(block, f32)),
        in_specs=[anywhere] * 8,
        out_specs=(vmem, vmem),
        scratch_shapes=[
            pltpu.SMEM((NV, NV), f32),
            pltpu.SMEM((2, ROWS), jnp.int32),
            pltpu.VMEM((2, ROWS), f32),
            pltpu.SMEM((2, ROWS), jnp.int32),
            pltpu.VMEM((2, ROWS), f32),
            pltpu.VMEM(padded, f32),
            pltpu.VMEM(padded, f32),
            pltpu.VMEM(block, f32),
            pltpu.VMEM((ROWS, AX), f32),
            *[pltpu.VMEM(chunked, f32) for _ in range(6)],
            pltpu.VMEM((LANES, LANES), f32),
            *[pltpu.VMEM((PLANE, 2 * CHUNK, LANES), f32) for _ in range(2)],
            *[pltpu.VMEM((SZ, 4 * CHUNK, LANES), f32) for _ in range(2)],
            pltpu.VMEM((ROWS, LANES), f32),
            pltpu.VMEM((3, 2 * CHUNK, LANES), f32),
            pltpu.VMEM((LANES, LANES), f32),
            *[pltpu.VMEM(halo, f32) for _ in range(4)],
            regular((3,)),
            dma((8,)),
            dma((2 * CHUNKS,)),
            dma((2 * CHUNKS,)),
            dma((2 * CHUNKS,)),
            dma((2 * CHUNKS,)),
            dma((4,)),
            dma((4,)),
            dma((2 * PLANE,)),
            dma((2 * PLANE,)),
            dma((2 * SZ,)),
            dma((2 * SZ,)),
            dma((3,)),
            dma((3,)),
        ],
        compiler_params=pltpu.CompilerParams(
            collective_id=0, has_side_effects=True, vmem_limit_bytes=24 * 2**20
        ),
    )(*[pltpu.with_memory_space_constraint(arg, pltpu.HBM) for arg in args])
    return pl.pallas_call(
        store,
        out_shape=(pltpu.HBM(block, f32), pltpu.HBM(block, f32)),
        in_specs=[vmem, vmem],
        out_specs=(anywhere, anywhere),
        scratch_shapes=[dma((2,))],
    )(
        pltpu.with_memory_space_constraint(state, pltpu.VMEM), pltpu.with_memory_space_constraint(resid, pltpu.VMEM)
    )


def solution(mesh):
    return jax.shard_map(
        local,
        mesh=mesh,
        in_specs=(
            P("inst", None, "space", None),
            P("inst", None, "space", None),
            P("space", None),
            P(),
            P("inst", "space"),
            P("inst", "space"),
            P("inst", "space"),
            P("inst", "space"),
        ),
        out_specs=(P("inst", None, "space", None), P("inst", None, "space", None)),
        check_vma=False,
    )
```

```python
import math

import jax
import jax.numpy as jnp
from jax import lax
from jax.experimental import pallas as pl
from jax.experimental.pallas import tpu as pltpu
from jax.sharding import PartitionSpec as P

MESH = pl.DeviceIdType.MESH
NT = 8
NV = 5
ROWS = 64
AX = 256
LANES = 128
CHUNK = 8
CHUNKS = ROWS // CHUNK
SX, SZ, SY = 2, 8, 4
SPACE = SX * SZ * SY
VISCOSITY = 0.5
AT_RINGS, AT_HALO_SENDS, AT_HALOS = 3, 5, 6
FIRST = 2


def spectral(gap):
    gap = gap % NT
    if gap == 0:
        return 0.0
    return 0.5 * (-1.0) ** gap * math.cos(math.pi * gap / NT) / math.sin(math.pi * gap / NT)


def kernel(
    flow_hbm, source_hbm, step_hbm, *rest,
):
    *small_hbm, out_state, out_resid = rest[:7]
    body(flow_hbm, source_hbm, step_hbm, small_hbm, out_state, out_resid, *rest[7:])


def body(
    flow_hbm, source_hbm, step_hbm, small_hbm, out_state, out_resid,
    jac, stator_donor, stator_weight, rotor_donor, rotor_weight,
    flow0, flow1, source, step, sib0, sib1, send0, send1, recv0, recv1,
    corner, plane0, plane1, ring0, ring1, cross, inflow, columns, remote_part,
    halo_out0, halo_out1, halo_in0, halo_in1,
    known, load_sem, sib_ssem, sib_rsem, par_ssem, par_rsem, halo_ssem, halo_rsem,
    plane_ssem, plane_rsem, ring_ssem, ring_rsem, cross_ssem, cross_rsem, column_ssem, column_rsem,
):
    inst, space = lax.axis_index("inst"), lax.axis_index("space")
    pair, core = inst // 2, inst % 2
    x, z, y = space // (SZ * SY), (space // SY) % SZ, space % SY
    sibling = (pair * 2 + 1 - core, space)
    partner = ((1 - pair) * 2 + core, space)
    diagonal = ((1 - pair) * 2 + 1 - core, space)
    across = (inst, (space + SPACE // 2) % SPACE)
    middle = ((1 - pair) * 2 + core, (space + SPACE // 2) % SPACE)
    above = (inst, (space + SPACE - 1) % SPACE)
    below = (inst, (space + 1) % SPACE)
    planes, rings = (plane0, plane1), (ring0, ring1)

    def plane_peer(k):
        other = (y + k) % SY
        return other, (inst, x * (SZ * SY) + z * SY + other)

    def ring_peer(k):
        other = (z + k) % SZ
        return other, (inst, x * (SZ * SY) + other * SY + y)

    flow_in = pltpu.make_async_copy(flow_hbm, flow0.at[:, :, pl.ds(CHUNK, ROWS), :], load_sem.at[0])
    source_in = pltpu.make_async_copy(source_hbm, source, load_sem.at[1])
    step_in = pltpu.make_async_copy(step_hbm, step, load_sem.at[2])
    flow_in.start()
    source_in.start()
    step_in.start()
    small = (jac, stator_donor, stator_weight, rotor_donor, rotor_weight)
    small_in = [
        pltpu.make_async_copy(src, dst, load_sem.at[3 + k]) for k, (src, dst) in enumerate(zip(small_hbm, small))
    ]
    for copy in small_in:
        copy.start()

    def on_line(k, along_y, along_z):
        out = []
        if along_y:
            out += [(y >= k, (inst, space - k)), (y < SY - k, (inst, space + k))]
        if along_z:
            out += [(z >= k, (inst, space - k * SY)), (z < SZ - k, (inst, space + k * SY))]
        return out

    always = space >= 0
    nearest = [(always, partner), (x != pair, middle)] + on_line(1, True, True)

    def tell(semaphore, devices):
        for exists, device in devices:

            @pl.when(exists)
            def _(device=device):
                pl.semaphore_signal(semaphore, inc=1, device_id=device, device_id_type=MESH)

    def hear(semaphore, devices):
        count = 0
        for exists, _ in devices:
            count = count + exists.astype(jnp.int32)
        pl.semaphore_wait(semaphore, count)

    rounds = [nearest, on_line(2, True, True), on_line(4, False, True), on_line(SZ - 1, False, True)]
    barrier = pltpu.get_barrier_semaphore()
    greeted = [(always, sibling)] + nearest
    tell(barrier, greeted)

    lane = lax.broadcasted_iota(jnp.int32, (CHUNK, LANES), 1)
    low = lax.broadcasted_iota(jnp.int32, (NV, LANES), 1) < ROWS

    def scalars(table):
        return [[table(a - b) for b in range(2)] for a in range(2)]

    from_own = scalars(spectral)
    from_sib = scalars(lambda g: jnp.where(core == 0, spectral(g - 2), spectral(g + 2)).astype(jnp.float32))
    to_own = scalars(lambda g: spectral(g + 4))
    to_sib = scalars(lambda g: jnp.where(core == 0, spectral(g + 2), spectral(g + 6)).astype(jnp.float32))

    def remote(src, dst, ssem, rsem, device):
        return pltpu.make_async_remote_copy(
            src_ref=src, dst_ref=dst, send_sem=ssem, recv_sem=rsem, device_id=device, device_id_type=MESH
        )

    def rows_at(g):
        return pl.ds(pl.multiple_of(CHUNK + g * CHUNK, CHUNK), CHUNK)

    def sib_copy(sweep, g):
        flow, sib = (flow0, sib0) if sweep == 0 else (flow1, sib1)
        at = sweep * CHUNKS + g
        return remote(flow.at[:, :, rows_at(g), :], sib.at[g], sib_ssem.at[at], sib_rsem.at[at], sibling)

    def par_copy(sweep, g):
        send, recv = (send0, recv0) if sweep == 0 else (send1, recv1)
        at = sweep * CHUNKS + g
        return remote(send.at[g], recv.at[g], par_ssem.at[at], par_rsem.at[at], partner)

    halos_out, halos_in = (halo_out0, halo_out1), (halo_in0, halo_in1)

    def halo_copies(sweep):
        out, into = halos_out[sweep], halos_in[sweep]
        up, down = 2 * sweep, 2 * sweep + 1
        return (
            remote(out.at[0], into.at[1], halo_ssem.at[up], halo_rsem.at[up], above),
            remote(out.at[1], into.at[0], halo_ssem.at[down], halo_rsem.at[down], below),
        )

    def pack_halos(sweep):
        flow, out = (flow0 if sweep == 0 else flow1), halos_out[sweep]
        for side, row in enumerate((CHUNK, CHUNK + ROWS - 1)):
            for n in range(2):
                for v in range(NV):
                    out[side, n, pl.ds(v, 1), :] = flow[n, v, pl.ds(row, 1), :]

    def unpack_halos(sweep):
        flow, into = (flow0 if sweep == 0 else flow1), halos_in[sweep]
        for copy in halo_copies(sweep):
            copy.wait_recv()
        for side, row in enumerate((CHUNK - 1, CHUNK + ROWS)):
            for n in range(2):
                for v in range(NV):
                    flow[n, v, pl.ds(row, 1), :] = into[side, n, pl.ds(v, 1), :]

    def column_copies():
        mine = plane1.at[y]
        return [
            remote(mine, columns.at[k], column_ssem.at[k], column_rsem.at[k], device)
            for k, device in enumerate((sibling, partner, diagonal))
        ]

    def plane_copy(sweep, k):
        _, device = plane_peer(k)
        mine = planes[sweep].at[y]
        return remote(mine, mine, plane_ssem.at[sweep * SY + k], plane_rsem.at[sweep * SY + y], device)

    def plane_arrival(sweep, k):
        other, device = plane_peer(k)
        theirs = planes[sweep].at[other]
        return remote(theirs, theirs, plane_ssem.at[sweep * SY + k], plane_rsem.at[sweep * SY + other], device)

    def cross_copy(sweep):
        mine = plane0.at[y, x] if sweep == 0 else cross.at[x]
        return remote(mine, mine, cross_ssem.at[sweep], cross_rsem.at[sweep], across)

    def cross_arrival(sweep):
        theirs = plane0.at[y, 1 - x] if sweep == 0 else cross.at[1 - x]
        return remote(theirs, theirs, cross_ssem.at[sweep], cross_rsem.at[sweep], across)

    def ring_copy(sweep, k):
        _, device = ring_peer(k)
        mine = rings[sweep].at[z]
        return remote(mine, mine, ring_ssem.at[sweep * SZ + k], ring_rsem.at[sweep * SZ + z], device)

    def ring_arrival(sweep, k):
        other, device = ring_peer(k)
        theirs = rings[sweep].at[other]
        return remote(theirs, theirs, ring_ssem.at[sweep * SZ + k], ring_rsem.at[sweep * SZ + other], device)

    def extract(sweep):
        flow = flow0 if sweep == 0 else flow1

        def body(g, _):
            for n in range(2):
                total = jnp.zeros((CHUNK, LANES), jnp.float32)
                for c in range(2):
                    for v in range(NV):
                        tile = flow[n, v, rows_at(g), pl.ds(c * LANES, LANES)]
                        q = c * CHUNK + v
                        turned = pltpu.roll(tile, (q + 1) if c == 0 else q, axis=1)
                        total = jnp.where(lane == q, turned, total)
                corner[pl.ds(pl.multiple_of(n * ROWS + g * CHUNK, CHUNK), CHUNK), :] = total
            return 0

        lax.fori_loop(0, CHUNKS, body, 0)
        turned = corner[...].T
        for c in range(2):
            found = turned[c * CHUNK : c * CHUNK + NV, :]
            if sweep == 0:
                plane0[y, x, c] = found
            else:
                plane1[y, c] = found

    def donor(c, n):
        return (stator_donor if c == 0 else rotor_donor)[n, 0]

    def forward(sweep):
        for c in range(2):
            for n in range(2):
                ahead = (donor(c, n) // ROWS + SPACE - space) % SPACE
                halves = []
                for d in (ahead, (ahead + 1) % SPACE):
                    dx, dz, dy = d // (SZ * SY), (d // SY) % SZ, d % SY
                    carry = (y + dy) // SY
                    wants = (z + 2 * SZ - dz - carry) % SZ
                    over = (wants + dz + carry) // SZ
                    if sweep == 0:
                        halves.append(plane0[(y + dy) % SY, (x + dx + over) % SX, c])
                    else:
                        halves.append(plane1[(y + dy) % SY, c])
                first, second = halves
                if n == 0:
                    both = jnp.where(low, first, pltpu.roll(second, ROWS, axis=1))
                else:
                    both = jnp.where(low, pltpu.roll(first, ROWS, axis=1), second)
                rings[sweep][z, c * 2 + n] = both

    def from_ring(sweep, c, n):
        block = donor(c, n) // ROWS
        here = rings[sweep][(block // SY) % SZ, c * 2 + n]
        there = rings[sweep][((block + 1) // SY) % SZ, c * 2 + n]
        return jnp.where(low, here, there)

    def pass_across():
        for c in range(2):
            for n in range(2):
                cross[x, c * 2 + n] = from_ring(1, c, n)

    def from_cross(c, n):
        block = donor(c, n) // ROWS
        here = cross[(block // (SZ * SY)) % SX, c * 2 + n]
        there = cross[((block + 1) // (SZ * SY)) % SX, c * 2 + n]
        return jnp.where(low, here, there)

    def interpolate(sweep):
        corner[...] = jnp.zeros_like(corner)
        for c in range(2):
            weights = stator_weight if c == 0 else rotor_weight
            for n in range(2):
                window = from_ring(sweep, c, n) if sweep == 0 else from_cross(c, n)
                offset = donor(c, n) % ROWS
                first = pltpu.roll(window, (LANES - offset) % LANES, axis=1)
                second = pltpu.roll(window, LANES - 1 - offset, axis=1)
                weight = weights[pl.ds(n, 1), :]
                weight = jnp.concatenate([weight, weight], axis=1)
                corner[pl.ds((c * 2 + n) * CHUNK, NV), :] = (1.0 - weight) * first + weight * second
        inflow[...] = corner[...].T[0:ROWS, :]

    def mix(sweep, g):
        flow, sib, send = (flow0, sib0, send0) if sweep == 0 else (flow1, sib1, send1)
        for v in range(NV):
            for t in range(2):
                at = pl.ds(t * LANES, LANES)
                own = [flow[n, v, rows_at(g), at] for n in range(2)]
                other = [sib[g, n, v, :, at] for n in range(2)]
                for a in range(2):
                    send[g, a, v, :, at] = (
                        to_own[a][0] * own[0] + to_own[a][1] * own[1]
                        + (to_sib[a][0] * other[0] + to_sib[a][1] * other[1])
                    )

    def advance(sweep, g):
        flow, sib, recv = (flow0, sib0, recv0) if sweep == 0 else (flow1, sib1, recv1)
        here = pl.ds(pl.multiple_of(g * CHUNK, CHUNK), CHUNK)
        jacobian = [[jac[v, w] for w in range(NV)] for v in range(NV)]
        for t in range(2):
            at = pl.ds(t * LANES, LANES)
            pace = step[here, at]
            edge = lane == (LANES - 1 if t == 0 else 0)
            centre = []
            for n in range(2):
                centre.append([flow[n, v, rows_at(g), at] for v in range(NV)])
            for n in range(2):
                diff, smooth = [], []
                for v in range(NV):
                    window = flow[n, v, pl.ds(pl.multiple_of(g * CHUNK, CHUNK), 3 * CHUNK), at]
                    upper = window[CHUNK - 1 : 2 * CHUNK - 1]
                    lower = window[CHUNK + 1 : 2 * CHUNK + 1]
                    f = centre[n][v]
                    left = jnp.where(lane == 0, 0.0, pltpu.roll(f, 1, axis=1))
                    right = jnp.where(lane == LANES - 1, 0.0, pltpu.roll(f, LANES - 1, axis=1))
                    diff.append(f - left)
                    smooth.append(VISCOSITY * (4.0 * f - left - right - upper - lower))
                for v in range(NV):
                    convect = jacobian[v][0] * diff[0]
                    for w in range(1, NV):
                        convect = convect + jacobian[v][w] * diff[w]
                    others = (
                        from_sib[n][0] * sib[g, 0, v, :, at] + from_sib[n][1] * sib[g, 1, v, :, at]
                        + recv[g, n, v, :, at]
                    )
                    if sweep == 1:
                        others = jnp.where(edge, 0.0, others)
                    derivative = from_own[n][0] * centre[0][v] + from_own[n][1] * centre[1][v] + others
                    residual = convect + smooth[v] + derivative - source[n, v, here, at]
                    new = centre[n][v] - pace * residual
                    if sweep == 0:
                        flow1[n, v, rows_at(g), at] = new
                    else:
                        out_state[n, v, here, at] = new
                        out_resid[n, v, here, at] = residual

    def patch(sweep, g):
        here = pl.ds(pl.multiple_of(g * CHUNK, CHUNK), CHUNK)
        jacobian = [[jac[v, w] for w in range(NV)] for v in range(NV)]
        entering = inflow[here, :]
        for n in range(2):
            if sweep == 1:
                fixed = remote_part[pl.ds(pl.multiple_of(n * ROWS + g * CHUNK, CHUNK), CHUNK), :]
            left = [pltpu.roll(entering, (LANES - n * CHUNK - v) % LANES, axis=1) for v in range(NV)]
            right = [pltpu.roll(entering, LANES - 1 - (2 * CHUNK + n * CHUNK + v), axis=1) for v in range(NV)]
            for t in range(2):
                at = pl.ds(t * LANES, LANES)
                edge = lane == (LANES - 1 if t == 0 else 0)
                pace = step[here, at]
                for v in range(NV):
                    if t == 0:
                        share = -VISCOSITY * right[v]
                    else:
                        share = -VISCOSITY * left[v]
                        for w in range(NV):
                            share = share - jacobian[v][w] * left[w]
                    if sweep == 0:
                        share = jnp.where(edge, share, 0.0)
                        flow1[n, v, rows_at(g), at] = flow1[n, v, rows_at(g), at] - pace * share
                    else:
                        turn = LANES - 1 - v if t == 0 else LANES - CHUNK - v
                        share = jnp.where(edge, share + pltpu.roll(fixed, turn, axis=1), 0.0)
                        out_state[n, v, here, at] = out_state[n, v, here, at] - pace * share
                        out_resid[n, v, here, at] = out_resid[n, v, here, at] + share

    def mix_columns():
        corner[...] = jnp.zeros_like(corner)
        for c in range(2):
            total = None
            for k, table in enumerate((from_sib, to_own, to_sib)):
                straight = columns[k, c]
                turned = pltpu.roll(straight, ROWS, axis=1)
                same = jnp.where(low, table[0][0], table[1][1])
                crossed = jnp.where(low, table[0][1], table[1][0])
                term = same * straight + crossed * turned
                total = term if total is None else total + term
            corner[pl.ds(c * CHUNK, NV), :] = total
        remote_part[...] = corner[...].T

    def loop(body, begin=0, end=CHUNKS):
        def wrapped(g, carry):
            body(g)
            return carry

        lax.fori_loop(begin, end, wrapped, 0)

    def order(p):
        return (p + 1) % CHUNKS

    flow_in.wait()
    extract(0)
    pack_halos(0)
    hear(barrier, greeted)
    tell(known.at[0], rounds[0])
    loop(lambda p: sib_copy(0, order(p)).start())

    def first_mix(p):
        g = order(p)
        sib_copy(0, g).wait_recv()
        mix(0, g)
        par_copy(0, g).start()

    loop(first_mix, 0, FIRST)
    hear(known.at[0], rounds[0])
    cross_copy(0).start()
    tell(known.at[1], rounds[1])
    loop(first_mix, FIRST, CHUNKS)
    for copy in small_in:
        copy.wait()
    source_in.wait()
    step_in.wait()
    hear(known.at[1], rounds[1])
    tell(known.at[2], rounds[2])
    cross_arrival(0).wait_recv()

    def start_planes(sweep):
        for k in range(1, SY):
            plane_copy(sweep, k).start()

    def start_rings(sweep):
        for k in range(1, SY):
            plane_arrival(sweep, k).wait_recv()
        forward(sweep)
        for k in range(1, SZ):
            ring_copy(sweep, k).start()

    def finish_rings(sweep):
        for k in range(1, SZ):
            ring_arrival(sweep, k).wait_recv()

    start_planes(0)

    def second_mix(p):
        g = order(p)
        sib_copy(1, g).wait_recv()
        mix(1, g)
        par_copy(1, g).start()

    def first_sweep(p):
        g = order(p)

        @pl.when(p == AT_RINGS)
        def _():
            hear(known.at[2], rounds[2])
            start_rings(0)
            tell(known.at[3], rounds[3])

        @pl.when(p == AT_HALO_SENDS)
        def _():
            for exists, _ in rounds[3]:

                @pl.when(exists)
                def _():
                    pl.semaphore_wait(known.at[3], 1)

            for copy in halo_copies(0):
                copy.start()

        @pl.when(p == AT_HALOS)
        def _():
            unpack_halos(0)

        par_copy(0, g).wait_recv()
        advance(0, g)
        sib_copy(1, g).start()

        @pl.when(p > 0)
        def _():
            second_mix(p - 1)

    loop(first_sweep)
    second_mix(CHUNKS - 1)
    finish_rings(0)
    interpolate(0)
    loop(lambda p: sib_copy(1, order(p)).wait_send())
    loop(lambda g: patch(0, g))
    extract(1)
    start_planes(1)
    pack_halos(1)
    for copy in halo_copies(1):
        copy.start()
    for copy in column_copies():
        copy.start()
    start_rings(1)
    unpack_halos(1)
    finish_rings(1)
    pass_across()
    cross_copy(1).start()

    def second_sweep(p):
        g = order(p)
        par_copy(1, g).wait_recv()
        advance(1, g)

    loop(second_sweep)
    for copy in column_copies():
        copy.wait_recv()
    mix_columns()
    cross_arrival(1).wait_recv()
    interpolate(1)
    loop(lambda g: patch(1, g))

    def finish(g):
        sib_copy(0, g).wait_send()
        for sweep in range(2):
            par_copy(sweep, g).wait_send()

    loop(finish)
    for copy in column_copies():
        copy.wait_send()
    for sweep in range(2):
        cross_copy(sweep).wait_send()
        for copy in halo_copies(sweep):
            copy.wait_send()
        for k in range(1, SY):
            plane_copy(sweep, k).wait_send()
        for k in range(1, SZ):
            ring_copy(sweep, k).wait_send()


def store(state, resid, state_hbm, resid_hbm, sems):
    copies = [
        pltpu.make_async_copy(state, state_hbm, sems.at[0]),
        pltpu.make_async_copy(resid, resid_hbm, sems.at[1]),
    ]
    for copy in copies:
        copy.start()
    for copy in copies:
        copy.wait()


def local(flow_state, flow_source, pseudo_step, flux_jacobian, stator_donor, stator_weight, rotor_donor, rotor_weight):
    f32 = jnp.float32
    block = (2, NV, ROWS, AX)
    padded = (2, NV, ROWS + 2 * CHUNK, AX)
    chunked = (CHUNKS, 2, NV, CHUNK, AX)
    anywhere = pl.BlockSpec(memory_space=pltpu.HBM)
    vmem = pl.BlockSpec(memory_space=pltpu.VMEM)
    dma = pltpu.SemaphoreType.DMA
    regular = pltpu.SemaphoreType.REGULAR
    halo = (2, 2, NV, AX)
    args = (
        flow_state, flow_source, pseudo_step, flux_jacobian, stator_donor, stator_weight, rotor_donor, rotor_weight
    )
    state, resid = pl.pallas_call(
        kernel,
        out_shape=(pltpu.VMEM(block, f32), pltpu.VMEM(block, f32)),
        in_specs=[anywhere] * 8,
        out_specs=(vmem, vmem),
        scratch_shapes=[
            pltpu.SMEM((NV, NV), f32),
            pltpu.SMEM((2, ROWS), jnp.int32),
            pltpu.VMEM((2, ROWS), f32),
            pltpu.SMEM((2, ROWS), jnp.int32),
            pltpu.VMEM((2, ROWS), f32),
            pltpu.VMEM(padded, f32),
            pltpu.VMEM(padded, f32),
            pltpu.VMEM(block, f32),
            pltpu.VMEM((ROWS, AX), f32),
            *[pltpu.VMEM(chunked, f32) for _ in range(6)],
            pltpu.VMEM((LANES, LANES), f32),
            pltpu.VMEM((SY, SX, 2, NV, LANES), f32),
            pltpu.VMEM((SY, 2, NV, LANES), f32),
            *[pltpu.VMEM((SZ, 4, NV, LANES), f32) for _ in range(2)],
            pltpu.VMEM((SX, 4, NV, LANES), f32),
            pltpu.VMEM((ROWS, LANES), f32),
            pltpu.VMEM((3, 2, NV, LANES), f32),
            pltpu.VMEM((LANES, LANES), f32),
            *[pltpu.VMEM(halo, f32) for _ in range(4)],
            regular((4,)),
            dma((8,)),
            dma((2 * CHUNKS,)),
            dma((2 * CHUNKS,)),
            dma((2 * CHUNKS,)),
            dma((2 * CHUNKS,)),
            dma((4,)),
            dma((4,)),
            dma((2 * SY,)),
            dma((2 * SY,)),
            dma((2 * SZ,)),
            dma((2 * SZ,)),
            dma((2,)),
            dma((2,)),
            dma((3,)),
            dma((3,)),
        ],
        compiler_params=pltpu.CompilerParams(
            collective_id=0, has_side_effects=True, vmem_limit_bytes=24 * 2**20
        ),
    )(*[pltpu.with_memory_space_constraint(arg, pltpu.HBM) for arg in args])
    return pl.pallas_call(
        store,
        out_shape=(pltpu.HBM(block, f32), pltpu.HBM(block, f32)),
        in_specs=[vmem, vmem],
        out_specs=(anywhere, anywhere),
        scratch_shapes=[dma((2,))],
    )(
        pltpu.with_memory_space_constraint(state, pltpu.VMEM), pltpu.with_memory_space_constraint(resid, pltpu.VMEM)
    )


def solution(mesh):
    return jax.shard_map(
        local,
        mesh=mesh,
        in_specs=(
            P("inst", None, "space", None),
            P("inst", None, "space", None),
            P("space", None),
            P(),
            P("inst", "space"),
            P("inst", "space"),
            P("inst", "space"),
            P("inst", "space"),
        ),
        out_specs=(P("inst", None, "space", None), P("inst", None, "space", None)),
        check_vma=False,
    )
```

```python
import math

import jax
import jax.numpy as jnp
from jax import lax
from jax.experimental import pallas as pl
from jax.experimental.pallas import tpu as pltpu
from jax.sharding import PartitionSpec as P

MESH = pl.DeviceIdType.MESH
NT = 8
NV = 5
ROWS = 64
AX = 256
LANES = 128
CHUNK = 8
CHUNKS = ROWS // CHUNK
SX, SZ, SY = 2, 8, 4
SPACE = SX * SZ * SY
LAYER = SZ * SY
VISCOSITY = 0.5
AT_RINGS, AT_HALO_SENDS, AT_HALOS = 3, 5, 6
FIRST = 2


def spectral(gap):
    gap = gap % NT
    if gap == 0:
        return 0.0
    return 0.5 * (-1.0) ** gap * math.cos(math.pi * gap / NT) / math.sin(math.pi * gap / NT)


def kernel(
    flow_hbm, source_hbm, step_hbm, *rest,
):
    *small_hbm, out_state, out_resid = rest[:7]
    body(flow_hbm, source_hbm, step_hbm, small_hbm, out_state, out_resid, *rest[7:])


def body(
    flow_hbm, source_hbm, step_hbm, small_hbm, out_state, out_resid,
    jac, stator_donor, stator_weight, rotor_donor, rotor_weight,
    flow0, flow1, source, step, sib0, sib1, send0, send1, recv0, recv1,
    corner, plane0, plane1, ring0, cross, columns, before, pace_lanes, share_lanes, share_rows,
    halo_out0, halo_out1, halo_in0, halo_in1,
    known, load_sem, sib_ssem, sib_rsem, par_ssem, par_rsem, halo_ssem, halo_rsem,
    plane_ssem, plane_rsem, ring_ssem, ring_rsem, layer_ssem, layer_rsem, cross_ssem, cross_rsem, column_ssem, column_rsem,
):
    inst, space = lax.axis_index("inst"), lax.axis_index("space")
    pair, core = inst // 2, inst % 2
    x, z, y = space // (SZ * SY), (space // SY) % SZ, space % SY
    sibling = (pair * 2 + 1 - core, space)
    partner = ((1 - pair) * 2 + core, space)
    diagonal = ((1 - pair) * 2 + 1 - core, space)
    across = (inst, (space + SPACE // 2) % SPACE)
    above = (inst, (space + SPACE - 1) % SPACE)
    below = (inst, (space + 1) % SPACE)
    place = space % LAYER

    def plane_peer(k):
        return inst, x * LAYER + z * SY + (y + k) % SY

    def ring_peer(k):
        return inst, x * LAYER + ((z + k) % SZ) * SY + y

    def layer_peer(k):
        return inst, x * LAYER + (place + k) % LAYER

    flow_in = pltpu.make_async_copy(flow_hbm, flow0.at[:, :, pl.ds(CHUNK, ROWS), :], load_sem.at[0])
    source_in = pltpu.make_async_copy(source_hbm, source, load_sem.at[1])
    step_in = pltpu.make_async_copy(step_hbm, step, load_sem.at[2])
    flow_in.start()
    source_in.start()
    step_in.start()
    small = (jac, stator_donor, stator_weight, rotor_donor, rotor_weight)
    small_in = [
        pltpu.make_async_copy(src, dst, load_sem.at[3 + k]) for k, (src, dst) in enumerate(zip(small_hbm, small))
    ]
    for copy in small_in:
        copy.start()

    def on_line(k):
        return [(z >= k, (inst, space - k * SY)), (z < SZ - k, (inst, space + k * SY))]

    always = space >= 0
    nearest = [(always, sibling), (always, partner), (always, across)]
    nearest += [(always, plane_peer(k)) for k in range(1, SY)] + on_line(1)

    def tell(semaphore, devices):
        for exists, device in devices:

            @pl.when(exists)
            def _(device=device):
                pl.semaphore_signal(semaphore, inc=1, device_id=device, device_id_type=MESH)

    def hear(semaphore, devices):
        count = 0
        for exists, _ in devices:
            count = count + exists.astype(jnp.int32)
        pl.semaphore_wait(semaphore, count)

    rounds = [on_line(1), on_line(2), on_line(4), on_line(SZ - 1)]
    barrier = pltpu.get_barrier_semaphore()
    tell(barrier, nearest)

    lane = lax.broadcasted_iota(jnp.int32, (CHUNK, LANES), 1)
    low = lax.broadcasted_iota(jnp.int32, (NV, LANES), 1) < ROWS

    def scalars(table):
        return [[table(a - b) for b in range(2)] for a in range(2)]

    from_own = scalars(spectral)
    from_sib = scalars(lambda g: jnp.where(core == 0, spectral(g - 2), spectral(g + 2)).astype(jnp.float32))
    to_own = scalars(lambda g: spectral(g + 4))
    to_sib = scalars(lambda g: jnp.where(core == 0, spectral(g + 2), spectral(g + 6)).astype(jnp.float32))

    def remote(src, dst, ssem, rsem, device):
        return pltpu.make_async_remote_copy(
            src_ref=src, dst_ref=dst, send_sem=ssem, recv_sem=rsem, device_id=device, device_id_type=MESH
        )

    def rows_at(g):
        return pl.ds(pl.multiple_of(CHUNK + g * CHUNK, CHUNK), CHUNK)

    def all_done(ref, semaphore):
        pltpu.make_async_copy(ref, ref, semaphore).wait()

    def sib_copy(sweep, g):
        flow, sib = (flow0, sib0) if sweep == 0 else (flow1, sib1)
        at = sweep * CHUNKS + g
        return remote(flow.at[:, :, rows_at(g), :], sib.at[g], sib_ssem.at[sweep], sib_rsem.at[at], sibling)

    def par_copy(sweep, g):
        send, recv = (send0, recv0) if sweep == 0 else (send1, recv1)
        at = sweep * CHUNKS + g
        return remote(send.at[g], recv.at[g], par_ssem.at[sweep], par_rsem.at[at], partner)

    halos_out, halos_in = (halo_out0, halo_out1), (halo_in0, halo_in1)

    def start_halos(sweep):
        out, into = halos_out[sweep], halos_in[sweep]
        remote(out.at[0], into.at[1], halo_ssem.at[sweep], halo_rsem.at[sweep], above).start()
        remote(out.at[1], into.at[0], halo_ssem.at[sweep], halo_rsem.at[sweep], below).start()

    def pack_halos(sweep):
        flow, out = (flow0 if sweep == 0 else flow1), halos_out[sweep]
        for side, row in enumerate((CHUNK, CHUNK + ROWS - 1)):
            for n in range(2):
                for v in range(NV):
                    out[side, n, pl.ds(v, 1), :] = flow[n, v, pl.ds(row, 1), :]

    def unpack_halos(sweep):
        flow, into = (flow0 if sweep == 0 else flow1), halos_in[sweep]
        all_done(into, halo_rsem.at[sweep])
        for side, row in enumerate((CHUNK - 1, CHUNK + ROWS)):
            for n in range(2):
                for v in range(NV):
                    flow[n, v, pl.ds(row, 1), :] = into[side, n, pl.ds(v, 1), :]

    def cross_copy(sweep):
        mine = plane0.at[y, x] if sweep == 0 else cross.at[x]
        return remote(mine, mine, cross_ssem.at[sweep], cross_rsem.at[sweep], across)

    def cross_arrival(sweep):
        theirs = plane0.at[y, 1 - x] if sweep == 0 else cross.at[1 - x]
        return remote(theirs, theirs, cross_ssem.at[sweep], cross_rsem.at[sweep], across)

    def start_planes():
        mine = plane0.at[y]
        for k in range(1, SY):
            remote(mine, mine, plane_ssem.at[0], plane_rsem.at[0], plane_peer(k)).start()

    def start_rings():
        mine = ring0.at[z]
        for k in range(1, SZ):
            remote(mine, mine, ring_ssem.at[0], ring_rsem.at[0], ring_peer(k)).start()

    def start_layer():
        mine = plane1.at[place]

        def start(k, carry):
            remote(mine, mine, layer_ssem.at[0], layer_rsem.at[0], layer_peer(k)).start()
            return carry

        lax.fori_loop(1, LAYER, start, 0)

    def start_columns():
        mine = plane1.at[place]
        for k, device in enumerate((sibling, partner, diagonal)):
            remote(mine, columns.at[k], column_ssem.at[0], column_rsem.at[0], device).start()

    def gather(sweep, g):
        flow = flow0 if sweep == 0 else flow1
        here = pl.ds(pl.multiple_of(g * CHUNK, CHUNK), CHUNK)
        for n in range(2):
            total = jnp.zeros((CHUNK, LANES), jnp.float32)
            for c in range(2):
                at = pl.ds(c * LANES, LANES)
                tiles = [flow[n, v, rows_at(g), at] for v in range(NV)]
                if sweep == 0:
                    tiles.append(step[here, at])
                for v, tile in enumerate(tiles):
                    q = c * CHUNK + v
                    total = jnp.where(lane == q, pltpu.roll(tile, (q + 1) if c == 0 else q, axis=1), total)
            corner[pl.ds(pl.multiple_of(n * ROWS + g * CHUNK, CHUNK), CHUNK), :] = total

    def turn(sweep):
        turned = corner[...].T
        for c in range(2):
            found = turned[c * CHUNK : c * CHUNK + NV, :]
            if sweep == 0:
                plane0[y, x, c] = found
                pace_lanes[c] = turned[c * CHUNK + NV : c * CHUNK + NV + 1, :]
            else:
                before[c] = found

    def donor(c, n):
        return (stator_donor if c == 0 else rotor_donor)[n, 0]

    def halves(first, second, n):
        if n == 0:
            return jnp.where(low, first, pltpu.roll(second, ROWS, axis=1))
        return jnp.where(low, pltpu.roll(first, ROWS, axis=1), second)

    def forward():
        for c in range(2):
            for n in range(2):
                ahead = (donor(c, n) // ROWS + SPACE - space) % SPACE
                found = []
                for d in (ahead, (ahead + 1) % SPACE):
                    dx, dz, dy = d // LAYER, (d // SY) % SZ, d % SY
                    carry = (y + dy) // SY
                    wants = (z + 2 * SZ - dz - carry) % SZ
                    over = (wants + dz + carry) // SZ
                    found.append(plane0[(y + dy) % SY, (x + dx + over) % SX, c])
                ring0[z, c * 2 + n] = halves(*found, n)

    def from_ring(c, n):
        block = donor(c, n) // ROWS
        here = ring0[(block // SY) % SZ, c * 2 + n]
        there = ring0[((block + 1) // SY) % SZ, c * 2 + n]
        return jnp.where(low, here, there)

    def pass_across():
        for c in range(2):
            for n in range(2):
                block = donor(c, n) // ROWS
                cross[x, c * 2 + n] = halves(plane1[block % LAYER, c], plane1[(block + 1) % LAYER, c], n)

    def from_cross(c, n):
        block = donor(c, n) // ROWS
        here = cross[(block // LAYER) % SX, c * 2 + n]
        there = cross[((block + 1) // LAYER) % SX, c * 2 + n]
        return jnp.where(low, here, there)

    def settle(sweep):
        entering = []
        for c in range(2):
            weights = stator_weight if c == 0 else rotor_weight
            values = []
            for n in range(2):
                window = from_ring(c, n) if sweep == 0 else from_cross(c, n)
                offset = donor(c, n) % ROWS
                first = pltpu.roll(window, (LANES - offset) % LANES, axis=1)
                second = pltpu.roll(window, LANES - 1 - offset, axis=1)
                weight = weights[pl.ds(n, 1), :]
                weight = jnp.concatenate([weight, weight], axis=1)
                values.append((1.0 - weight) * first + weight * second)
            entering.append(jnp.where(low, values[0], pltpu.roll(values[1], ROWS, axis=1)))
        stator, rotor = entering
        share_lanes[0] = -VISCOSITY * rotor
        share_lanes[1] = -VISCOSITY * stator
        for v in range(NV):
            total = share_lanes[1, pl.ds(v, 1), :]
            for w in range(NV):
                total = total - jac[v, w] * stator[w : w + 1, :]
            share_lanes[1, pl.ds(v, 1), :] = total
        if sweep == 1:
            for c in range(2):
                total = share_lanes[c]
                for k, table in enumerate((from_sib, to_own, to_sib)):
                    straight = columns[k, c]
                    turned = pltpu.roll(straight, ROWS, axis=1)
                    same = jnp.where(low, table[0][0], table[1][1])
                    crossed = jnp.where(low, table[0][1], table[1][0])
                    total = total + (same * straight + crossed * turned)
                share_lanes[c] = total

    def turn_share():
        corner[...] = jnp.zeros_like(corner)
        for t in range(2):
            corner[pl.ds(t * CHUNK, NV), :] = share_lanes[t]
        share_rows[...] = corner[...].T

    def mix(sweep, g):
        flow, sib, send = (flow0, sib0, send0) if sweep == 0 else (flow1, sib1, send1)
        for v in range(NV):
            for t in range(2):
                at = pl.ds(t * LANES, LANES)
                own = [flow[n, v, rows_at(g), at] for n in range(2)]
                other = [sib[g, n, v, :, at] for n in range(2)]
                for a in range(2):
                    send[g, a, v, :, at] = (
                        to_own[a][0] * own[0] + to_own[a][1] * own[1]
                        + (to_sib[a][0] * other[0] + to_sib[a][1] * other[1])
                    )

    def advance(sweep, g):
        flow, sib, recv = (flow0, sib0, recv0) if sweep == 0 else (flow1, sib1, recv1)
        here = pl.ds(pl.multiple_of(g * CHUNK, CHUNK), CHUNK)
        jacobian = [[jac[v, w] for w in range(NV)] for v in range(NV)]
        for t in range(2):
            at = pl.ds(t * LANES, LANES)
            pace = step[here, at]
            edge = lane == (LANES - 1 if t == 0 else 0)
            centre = []
            for n in range(2):
                centre.append([flow[n, v, rows_at(g), at] for v in range(NV)])
            for n in range(2):
                diff, smooth = [], []
                for v in range(NV):
                    window = flow[n, v, pl.ds(pl.multiple_of(g * CHUNK, CHUNK), 3 * CHUNK), at]
                    upper = window[CHUNK - 1 : 2 * CHUNK - 1]
                    lower = window[CHUNK + 1 : 2 * CHUNK + 1]
                    f = centre[n][v]
                    left = jnp.where(lane == 0, 0.0, pltpu.roll(f, 1, axis=1))
                    right = jnp.where(lane == LANES - 1, 0.0, pltpu.roll(f, LANES - 1, axis=1))
                    diff.append(f - left)
                    smooth.append(VISCOSITY * (4.0 * f - left - right - upper - lower))
                for v in range(NV):
                    convect = jacobian[v][0] * diff[0]
                    for w in range(1, NV):
                        convect = convect + jacobian[v][w] * diff[w]
                    others = (
                        from_sib[n][0] * sib[g, 0, v, :, at] + from_sib[n][1] * sib[g, 1, v, :, at]
                        + recv[g, n, v, :, at]
                    )
                    if sweep == 1:
                        others = jnp.where(edge, 0.0, others)
                    derivative = from_own[n][0] * centre[0][v] + from_own[n][1] * centre[1][v] + others
                    residual = convect + smooth[v] + derivative - source[n, v, here, at]
                    new = centre[n][v] - pace * residual
                    if sweep == 0:
                        flow1[n, v, rows_at(g), at] = new
                    else:
                        out_state[n, v, here, at] = new
                        out_resid[n, v, here, at] = residual

    def patch(sweep, g):
        here = pl.ds(pl.multiple_of(g * CHUNK, CHUNK), CHUNK)
        for n in range(2):
            shares = share_rows[pl.ds(pl.multiple_of(n * ROWS + g * CHUNK, CHUNK), CHUNK), :]
            for t in range(2):
                at = pl.ds(t * LANES, LANES)
                edge = lane == (LANES - 1 if t == 0 else 0)
                pace = step[here, at]
                for v in range(NV):
                    share = jnp.where(edge, pltpu.roll(shares, LANES - 1 - v if t == 0 else LANES - CHUNK - v, axis=1), 0.0)
                    if sweep == 0:
                        flow1[n, v, rows_at(g), at] = flow1[n, v, rows_at(g), at] - pace * share
                    else:
                        out_state[n, v, here, at] = out_state[n, v, here, at] - pace * share
                        out_resid[n, v, here, at] = out_resid[n, v, here, at] + share

    def loop(body, begin=0, end=CHUNKS):
        def wrapped(g, carry):
            body(g)
            return carry

        lax.fori_loop(begin, end, wrapped, 0)

    def order(p):
        return (p + 1) % CHUNKS

    step_in.wait()
    flow_in.wait()
    loop(lambda g: gather(0, g))
    turn(0)
    pack_halos(0)
    hear(barrier, nearest)
    cross_copy(0).start()
    tell(known.at[0], rounds[0])
    loop(lambda p: sib_copy(0, order(p)).start())

    def first_mix(p):
        g = order(p)
        sib_copy(0, g).wait_recv()
        mix(0, g)
        par_copy(0, g).start()

    loop(first_mix, 0, FIRST)
    hear(known.at[0], rounds[0])
    tell(known.at[1], rounds[1])
    loop(first_mix, FIRST, CHUNKS)
    for copy in small_in:
        copy.wait()
    source_in.wait()
    cross_arrival(0).wait_recv()
    start_planes()
    hear(known.at[1], rounds[1])
    tell(known.at[2], rounds[2])

    def second_mix(p):
        g = order(p)
        sib_copy(1, g).wait_recv()
        mix(1, g)
        par_copy(1, g).start()

    def first_sweep(p):
        g = order(p)

        @pl.when(p == AT_RINGS)
        def _():
            all_done(plane0.at[pl.ds(0, SY - 1)], plane_rsem.at[0])
            forward()
            hear(known.at[2], rounds[2])
            start_rings()
            tell(known.at[3], rounds[3])

        @pl.when(p == AT_HALO_SENDS)
        def _():
            for exists, _ in rounds[3]:

                @pl.when(exists)
                def _():
                    pl.semaphore_wait(known.at[3], 1)

            start_halos(0)

        @pl.when(p == AT_HALOS)
        def _():
            unpack_halos(0)

        par_copy(0, g).wait_recv()
        advance(0, g)
        sib_copy(1, g).start()
        gather(1, g)

        @pl.when(p > 0)
        def _():
            second_mix(p - 1)

    loop(first_sweep)
    turn(1)
    second_mix(CHUNKS - 1)
    all_done(ring0.at[pl.ds(0, SZ - 1)], ring_rsem.at[0])
    settle(0)
    for c in range(2):
        plane1[place, c] = before[c] - pace_lanes[c] * share_lanes[c]
    start_layer()
    start_columns()
    turn_share()
    all_done(sib1, sib_ssem.at[1])
    loop(lambda g: patch(0, g))
    pack_halos(1)
    start_halos(1)
    all_done(plane1.at[pl.ds(0, LAYER - 1)], layer_rsem.at[0])
    pass_across()
    cross_copy(1).start()
    unpack_halos(1)

    def second_sweep(p):
        g = order(p)
        par_copy(1, g).wait_recv()
        advance(1, g)

    loop(second_sweep)
    all_done(columns, column_rsem.at[0])
    cross_arrival(1).wait_recv()
    settle(1)
    turn_share()
    loop(lambda g: patch(1, g))

    all_done(sib0, sib_ssem.at[0])
    all_done(send0, par_ssem.at[0])
    all_done(send1, par_ssem.at[1])
    all_done(columns, column_ssem.at[0])
    all_done(plane0.at[pl.ds(0, SY - 1)], plane_ssem.at[0])
    all_done(ring0.at[pl.ds(0, SZ - 1)], ring_ssem.at[0])
    all_done(plane1.at[pl.ds(0, LAYER - 1)], layer_ssem.at[0])
    for sweep in range(2):
        cross_copy(sweep).wait_send()
        all_done(halos_out[sweep], halo_ssem.at[sweep])


def store(state, resid, state_hbm, resid_hbm, sems):
    copies = [
        pltpu.make_async_copy(state, state_hbm, sems.at[0]),
        pltpu.make_async_copy(resid, resid_hbm, sems.at[1]),
    ]
    for copy in copies:
        copy.start()
    for copy in copies:
        copy.wait()


def local(flow_state, flow_source, pseudo_step, flux_jacobian, stator_donor, stator_weight, rotor_donor, rotor_weight):
    f32 = jnp.float32
    block = (2, NV, ROWS, AX)
    padded = (2, NV, ROWS + 2 * CHUNK, AX)
    chunked = (CHUNKS, 2, NV, CHUNK, AX)
    anywhere = pl.BlockSpec(memory_space=pltpu.HBM)
    vmem = pl.BlockSpec(memory_space=pltpu.VMEM)
    dma = pltpu.SemaphoreType.DMA
    regular = pltpu.SemaphoreType.REGULAR
    halo = (2, 2, NV, AX)
    args = (
        flow_state, flow_source, pseudo_step, flux_jacobian, stator_donor, stator_weight, rotor_donor, rotor_weight
    )
    state, resid = pl.pallas_call(
        kernel,
        out_shape=(pltpu.VMEM(block, f32), pltpu.VMEM(block, f32)),
        in_specs=[anywhere] * 8,
        out_specs=(vmem, vmem),
        scratch_shapes=[
            pltpu.SMEM((NV, NV), f32),
            pltpu.SMEM((2, ROWS), jnp.int32),
            pltpu.VMEM((2, ROWS), f32),
            pltpu.SMEM((2, ROWS), jnp.int32),
            pltpu.VMEM((2, ROWS), f32),
            pltpu.VMEM(padded, f32),
            pltpu.VMEM(padded, f32),
            pltpu.VMEM(block, f32),
            pltpu.VMEM((ROWS, AX), f32),
            *[pltpu.VMEM(chunked, f32) for _ in range(6)],
            pltpu.VMEM((LANES, LANES), f32),
            pltpu.VMEM((SY, SX, 2, NV, LANES), f32),
            pltpu.VMEM((SZ * SY, 2, NV, LANES), f32),
            pltpu.VMEM((SZ, 4, NV, LANES), f32),
            pltpu.VMEM((SX, 4, NV, LANES), f32),
            pltpu.VMEM((3, 2, NV, LANES), f32),
            pltpu.VMEM((2, NV, LANES), f32),
            pltpu.VMEM((2, 1, LANES), f32),
            pltpu.VMEM((2, NV, LANES), f32),
            pltpu.VMEM((LANES, LANES), f32),
            *[pltpu.VMEM(halo, f32) for _ in range(4)],
            regular((4,)),
            dma((8,)),
            dma((2,)),
            dma((2 * CHUNKS,)),
            dma((2,)),
            dma((2 * CHUNKS,)),
            dma((2,)),
            dma((2,)),
            *[dma((1,)) for _ in range(6)],
            dma((2,)),
            dma((2,)),
            dma((1,)),
            dma((1,)),
        ],
        compiler_params=pltpu.CompilerParams(
            collective_id=0, has_side_effects=True, vmem_limit_bytes=24 * 2**20
        ),
    )(*[pltpu.with_memory_space_constraint(arg, pltpu.HBM) for arg in args])
    return pl.pallas_call(
        store,
        out_shape=(pltpu.HBM(block, f32), pltpu.HBM(block, f32)),
        in_specs=[vmem, vmem],
        out_specs=(anywhere, anywhere),
        scratch_shapes=[dma((2,))],
    )(
        pltpu.with_memory_space_constraint(state, pltpu.VMEM), pltpu.with_memory_space_constraint(resid, pltpu.VMEM)
    )


def solution(mesh):
    return jax.shard_map(
        local,
        mesh=mesh,
        in_specs=(
            P("inst", None, "space", None),
            P("inst", None, "space", None),
            P("space", None),
            P(),
            P("inst", "space"),
            P("inst", "space"),
            P("inst", "space"),
            P("inst", "space"),
        ),
        out_specs=(P("inst", None, "space", None), P("inst", None, "space", None)),
        check_vma=False,
    )
```

```python
import math

import jax
import jax.numpy as jnp
from jax import lax
from jax.experimental import pallas as pl
from jax.experimental.pallas import tpu as pltpu
from jax.sharding import PartitionSpec as P

MESH = pl.DeviceIdType.MESH
NT = 8
NV = 5
ROWS = 64
AX = 256
LANES = 128
CHUNK = 8
CHUNKS = ROWS // CHUNK
SX, SZ, SY = 2, 8, 4
SPACE = SX * SZ * SY
LAYER = SZ * SY
VISCOSITY = 0.5
AT_RINGS, AT_HALOS, AT_SETTLE = (3, 1), (5, 3), (6, 5)
AT_LAYER, AT_SECOND_HALOS = (6, 3), 6
FIRST = 2


def spectral(gap):
    gap = gap % NT
    if gap == 0:
        return 0.0
    return 0.5 * (-1.0) ** gap * math.cos(math.pi * gap / NT) / math.sin(math.pi * gap / NT)


def kernel(
    flow_hbm, source_hbm, step_hbm, *rest,
):
    *small_hbm, out_state, out_resid = rest[:7]
    body(flow_hbm, source_hbm, step_hbm, small_hbm, out_state, out_resid, *rest[7:])


def body(
    flow_hbm, source_hbm, step_hbm, small_hbm, out_state, out_resid,
    jac, stator_donor, stator_weight, rotor_donor, rotor_weight,
    flow0, flow1, source, step, sib0, sib1, send0, send1, recv0, recv1,
    corner, plane0, plane1, ring0, cross, columns0, columns1, before, pace_lanes, share_lanes, share_rows,
    halo_out0, halo_out1, halo_in0, halo_in1, relay, relay_sem,
    known, load_sem, sib_ssem, sib_rsem, par_ssem, par_rsem, halo_ssem, halo_rsem,
    plane_ssem, plane_rsem, ring_ssem, ring_rsem, layer_ssem, layer_rsem, cross_ssem, cross_rsem, column_ssem, column_rsem,
):
    inst, space = lax.axis_index("inst"), lax.axis_index("space")
    pair, core = inst // 2, inst % 2
    x, z, y = space // (SZ * SY), (space // SY) % SZ, space % SY
    sibling = (pair * 2 + 1 - core, space)
    partner = ((1 - pair) * 2 + core, space)
    diagonal = ((1 - pair) * 2 + 1 - core, space)
    across = (inst, (space + SPACE // 2) % SPACE)
    above = (inst, (space + SPACE - 1) % SPACE)
    below = (inst, (space + 1) % SPACE)
    place = space % LAYER

    def plane_peer(k):
        return inst, x * LAYER + z * SY + (y + k) % SY

    def ring_peer(k):
        return inst, x * LAYER + ((z + k) % SZ) * SY + y

    def layer_peer(k):
        return inst, x * LAYER + (place + k) % LAYER

    flow_in = pltpu.make_async_copy(flow_hbm, flow0.at[:, :, pl.ds(CHUNK, ROWS), :], load_sem.at[0])
    source_in = pltpu.make_async_copy(source_hbm, source, load_sem.at[1])
    step_in = pltpu.make_async_copy(step_hbm, step, load_sem.at[2])
    flow_in.start()
    source_in.start()
    step_in.start()
    small = (jac, stator_donor, stator_weight, rotor_donor, rotor_weight)
    small_in = [
        pltpu.make_async_copy(src, dst, load_sem.at[3 + k]) for k, (src, dst) in enumerate(zip(small_hbm, small))
    ]
    for copy in small_in:
        copy.start()

    def on_line(k):
        return [(z >= k, (inst, space - k * SY)), (z < SZ - k, (inst, space + k * SY))]

    always = space >= 0
    nearest = [(always, sibling), (always, partner), (always, across)]
    nearest += [(always, plane_peer(k)) for k in range(1, SY)] + on_line(1)

    def tell(semaphore, devices):
        for exists, device in devices:

            @pl.when(exists)
            def _(device=device):
                pl.semaphore_signal(semaphore, inc=1, device_id=device, device_id_type=MESH)

    def hear(semaphore, devices):
        count = 0
        for exists, _ in devices:
            count = count + exists.astype(jnp.int32)
        pl.semaphore_wait(semaphore, count)

    rounds = [on_line(1), on_line(2), on_line(4)]
    barrier = pltpu.get_barrier_semaphore()
    tell(barrier, nearest)

    lane = lax.broadcasted_iota(jnp.int32, (CHUNK, LANES), 1)
    low = lax.broadcasted_iota(jnp.int32, (NV, LANES), 1) < ROWS

    def scalars(table):
        return [[table(a - b) for b in range(2)] for a in range(2)]

    from_own = scalars(spectral)
    from_sib = scalars(lambda g: jnp.where(core == 0, spectral(g - 2), spectral(g + 2)).astype(jnp.float32))
    to_own = scalars(lambda g: spectral(g + 4))
    to_sib = scalars(lambda g: jnp.where(core == 0, spectral(g + 2), spectral(g + 6)).astype(jnp.float32))

    def remote(src, dst, ssem, rsem, device):
        return pltpu.make_async_remote_copy(
            src_ref=src, dst_ref=dst, send_sem=ssem, recv_sem=rsem, device_id=device, device_id_type=MESH
        )

    def rows_at(g):
        return pl.ds(pl.multiple_of(CHUNK + g * CHUNK, CHUNK), CHUNK)

    def all_done(ref, semaphore):
        pltpu.make_async_copy(ref, ref, semaphore).wait()

    def sib_copy(sweep, g):
        flow, sib = (flow0, sib0) if sweep == 0 else (flow1, sib1)
        at = sweep * CHUNKS + g
        return remote(flow.at[:, :, rows_at(g), :], sib.at[g], sib_ssem.at[sweep], sib_rsem.at[at], sibling)

    def par_copy(sweep, g):
        send, recv = (send0, recv0) if sweep == 0 else (send1, recv1)
        at = sweep * CHUNKS + g
        return remote(send.at[g], recv.at[g], par_ssem.at[sweep], par_rsem.at[at], partner)

    halos_out, halos_in = (halo_out0, halo_out1), (halo_in0, halo_in1)

    def send_row(sweep, row, into, device):
        remote(row, into, halo_ssem.at[sweep], halo_rsem.at[sweep], device).start()

    def start_halos(sweep):
        send_row(sweep, halos_out[sweep].at[0], halos_in[sweep].at[1], above)
        send_row(sweep, halos_out[sweep].at[1], halos_in[sweep].at[0], below)

    first_in_ring, last_in_ring = y == 0, y == SY - 1

    def start_first_halos():
        for side, stays, device in ((0, y > 0, above), (1, y < SY - 1, below)):

            @pl.when(stays)
            def _(side=side, device=device):
                send_row(0, halo_out0.at[side], halo_in0.at[1 - side], device)

            @pl.when(jnp.logical_not(stays))
            def _(side=side):
                other_end = plane_peer(SY - 1 if side == 0 else 1)
                remote(halo_out0.at[side], relay, halo_ssem.at[0], relay_sem.at[0], other_end).start()

    def pass_halos():
        for here, side, device in (
            (last_in_ring, 0, (inst, (space + SPACE - SY) % SPACE)),
            (first_in_ring, 1, (inst, (space + SY) % SPACE)),
        ):

            @pl.when(here)
            def _(side=side, device=device):
                all_done(relay, relay_sem.at[0])
                send_row(0, relay, halo_in0.at[1 - side], device)

    def pack_halos(sweep):
        flow, out = (flow0 if sweep == 0 else flow1), halos_out[sweep]
        for side, row in enumerate((CHUNK, CHUNK + ROWS - 1)):
            for n in range(2):
                for v in range(NV):
                    out[side, n, pl.ds(v, 1), :] = flow[n, v, pl.ds(row, 1), :]

    def unpack_halos(sweep):
        flow, into = (flow0 if sweep == 0 else flow1), halos_in[sweep]
        all_done(into, halo_rsem.at[sweep])
        for side, row in enumerate((CHUNK - 1, CHUNK + ROWS)):
            for n in range(2):
                for v in range(NV):
                    flow[n, v, pl.ds(row, 1), :] = into[side, n, pl.ds(v, 1), :]

    def cross_copy(sweep):
        mine = plane0.at[y, x] if sweep == 0 else cross.at[x]
        return remote(mine, mine, cross_ssem.at[sweep], cross_rsem.at[sweep], across)

    def cross_arrival(sweep):
        theirs = plane0.at[y, 1 - x] if sweep == 0 else cross.at[1 - x]
        return remote(theirs, theirs, cross_ssem.at[sweep], cross_rsem.at[sweep], across)

    def start_planes():
        mine = plane0.at[y]
        for k in range(1, SY):
            remote(mine, mine, plane_ssem.at[0], plane_rsem.at[0], plane_peer(k)).start()

    def start_rings():
        mine = ring0.at[z]
        for k in range(1, SZ):
            remote(mine, mine, ring_ssem.at[0], ring_rsem.at[0], ring_peer(k)).start()

    def start_layer():
        mine = plane1.at[place]

        def start(k, carry):
            remote(mine, mine, layer_ssem.at[0], layer_rsem.at[0], layer_peer(k)).start()
            return carry

        lax.fori_loop(1, LAYER, start, 0)

    def start_columns(sweep):
        mine = plane0.at[y, x] if sweep == 0 else plane1.at[place]
        for k, device in enumerate((sibling, partner, diagonal)):
            into = (columns0, columns1)[sweep].at[k]
            remote(mine, into, column_ssem.at[sweep], column_rsem.at[sweep], device).start()

    def to_lane(tiles, c, total):
        for v, tile in enumerate(tiles):
            q = c * CHUNK + v
            total = jnp.where(lane == q, pltpu.roll(tile, (q + 1) if c == 0 else q, axis=1), total)
        return total

    def corner_rows(n, g):
        return pl.ds(pl.multiple_of(n * ROWS + g * CHUNK, CHUNK), CHUNK)

    def gather(g):
        here = pl.ds(pl.multiple_of(g * CHUNK, CHUNK), CHUNK)
        for n in range(2):
            total = jnp.zeros((CHUNK, LANES), jnp.float32)
            for c in range(2):
                at = pl.ds(c * LANES, LANES)
                total = to_lane([flow0[n, v, rows_at(g), at] for v in range(NV)] + [step[here, at]], c, total)
            corner[corner_rows(n, g), :] = total

    def turn_first():
        turned = corner[...].T
        for c in range(2):
            plane0[y, x, c] = turned[c * CHUNK : c * CHUNK + NV, :]
            pace_lanes[c] = turned[c * CHUNK + NV : c * CHUNK + NV + 1, :]

    def turn_border():
        turned = corner[...].T
        for c in range(2):
            before[c] = turned[c * CHUNK : c * CHUNK + NV, :]

    def donor(c, n):
        return (stator_donor if c == 0 else rotor_donor)[n, 0]

    def halves(first, second, n):
        if n == 0:
            return jnp.where(low, first, pltpu.roll(second, ROWS, axis=1))
        return jnp.where(low, pltpu.roll(first, ROWS, axis=1), second)

    def forward():
        for c in range(2):
            for n in range(2):
                ahead = (donor(c, n) // ROWS + SPACE - space) % SPACE
                found = []
                for d in (ahead, (ahead + 1) % SPACE):
                    dx, dz, dy = d // LAYER, (d // SY) % SZ, d % SY
                    carry = (y + dy) // SY
                    wants = (z + 2 * SZ - dz - carry) % SZ
                    over = (wants + dz + carry) // SZ
                    found.append(plane0[(y + dy) % SY, (x + dx + over) % SX, c])
                ring0[z, c * 2 + n] = halves(*found, n)

    def from_ring(c, n):
        block = donor(c, n) // ROWS
        here = ring0[(block // SY) % SZ, c * 2 + n]
        there = ring0[((block + 1) // SY) % SZ, c * 2 + n]
        return jnp.where(low, here, there)

    def pass_across():
        for c in range(2):
            for n in range(2):
                block = donor(c, n) // ROWS
                cross[x, c * 2 + n] = halves(plane1[block % LAYER, c], plane1[(block + 1) % LAYER, c], n)

    def from_cross(c, n):
        block = donor(c, n) // ROWS
        here = cross[(block // LAYER) % SX, c * 2 + n]
        there = cross[((block + 1) // LAYER) % SX, c * 2 + n]
        return jnp.where(low, here, there)

    def settle(sweep):
        columns = (columns0, columns1)[sweep]
        entering = []
        for c in range(2):
            weights = stator_weight if c == 0 else rotor_weight
            values = []
            for n in range(2):
                window = from_ring(c, n) if sweep == 0 else from_cross(c, n)
                offset = donor(c, n) % ROWS
                first = pltpu.roll(window, (LANES - offset) % LANES, axis=1)
                second = pltpu.roll(window, LANES - 1 - offset, axis=1)
                weight = weights[pl.ds(n, 1), :]
                weight = jnp.concatenate([weight, weight], axis=1)
                values.append((1.0 - weight) * first + weight * second)
            entering.append(jnp.where(low, values[0], pltpu.roll(values[1], ROWS, axis=1)))
        stator, rotor = entering
        share_lanes[0] = -VISCOSITY * rotor
        share_lanes[1] = -VISCOSITY * stator
        for v in range(NV):
            total = share_lanes[1, pl.ds(v, 1), :]
            for w in range(NV):
                total = total - jac[v, w] * stator[w : w + 1, :]
            share_lanes[1, pl.ds(v, 1), :] = total
        for c in range(2):
            total = share_lanes[c]
            for k, table in enumerate((from_sib, to_own, to_sib)):
                straight = columns[k, c]
                turned = pltpu.roll(straight, ROWS, axis=1)
                same = jnp.where(low, table[0][0], table[1][1])
                crossed = jnp.where(low, table[0][1], table[1][0])
                total = total + (same * straight + crossed * turned)
            share_lanes[c] = total

    def turn_share():
        corner[...] = jnp.zeros_like(corner)
        for t in range(2):
            corner[pl.ds(t * CHUNK, NV), :] = share_lanes[t]
        share_rows[...] = corner[...].T

    def mix(sweep, g):
        flow, sib, send = (flow0, sib0, send0) if sweep == 0 else (flow1, sib1, send1)
        for v in range(NV):
            for t in range(2):
                at = pl.ds(t * LANES, LANES)
                own = [flow[n, v, rows_at(g), at] for n in range(2)]
                other = [sib[g, n, v, :, at] for n in range(2)]
                for a in range(2):
                    send[g, a, v, :, at] = (
                        to_own[a][0] * own[0] + to_own[a][1] * own[1]
                        + (to_sib[a][0] * other[0] + to_sib[a][1] * other[1])
                    )

    def inner(flow, g, t):
        here = pl.ds(pl.multiple_of(g * CHUNK, CHUNK), CHUNK)
        jacobian = [[jac[v, w] for w in range(NV)] for v in range(NV)]
        at = pl.ds(t * LANES, LANES)
        centre = [[flow[n, v, rows_at(g), at] for v in range(NV)] for n in range(2)]
        parts = []
        for n in range(2):
            diff, smooth = [], []
            for v in range(NV):
                window = flow[n, v, pl.ds(pl.multiple_of(g * CHUNK, CHUNK), 3 * CHUNK), at]
                upper = window[CHUNK - 1 : 2 * CHUNK - 1]
                lower = window[CHUNK + 1 : 2 * CHUNK + 1]
                f = centre[n][v]
                left = jnp.where(lane == 0, 0.0, pltpu.roll(f, 1, axis=1))
                right = jnp.where(lane == LANES - 1, 0.0, pltpu.roll(f, LANES - 1, axis=1))
                diff.append(f - left)
                smooth.append(VISCOSITY * (4.0 * f - left - right - upper - lower))
            row = []
            for v in range(NV):
                convect = jacobian[v][0] * diff[0]
                for w in range(1, NV):
                    convect = convect + jacobian[v][w] * diff[w]
                derivative = from_own[n][0] * centre[0][v] + from_own[n][1] * centre[1][v]
                row.append(convect + smooth[v] + derivative - source[n, v, here, at])
            parts.append(row)
        return centre, parts

    def border(g):
        here = pl.ds(pl.multiple_of(g * CHUNK, CHUNK), CHUNK)
        totals = [jnp.zeros((CHUNK, LANES), jnp.float32) for _ in range(2)]
        for t in range(2):
            pace = step[here, pl.ds(t * LANES, LANES)]
            centre, parts = inner(flow0, g, t)
            for n in range(2):
                totals[n] = to_lane([centre[n][v] - pace * parts[n][v] for v in range(NV)], t, totals[n])
        for n in range(2):
            corner[corner_rows(n, g), :] = totals[n]

    def advance(sweep, g):
        flow, sib, recv = (flow0, sib0, recv0) if sweep == 0 else (flow1, sib1, recv1)
        here = pl.ds(pl.multiple_of(g * CHUNK, CHUNK), CHUNK)
        for t in range(2):
            at = pl.ds(t * LANES, LANES)
            pace = step[here, at]
            edge = lane == (LANES - 1 if t == 0 else 0)
            centre, parts = inner(flow, g, t)
            for n in range(2):
                for v in range(NV):
                    others = (
                        from_sib[n][0] * sib[g, 0, v, :, at] + from_sib[n][1] * sib[g, 1, v, :, at]
                        + recv[g, n, v, :, at]
                    )
                    residual = parts[n][v] + jnp.where(edge, 0.0, others)
                    new = centre[n][v] - pace * residual
                    if sweep == 0:
                        flow1[n, v, rows_at(g), at] = new
                    else:
                        out_state[n, v, here, at] = new
                        out_resid[n, v, here, at] = residual

    def patch(sweep, g):
        here = pl.ds(pl.multiple_of(g * CHUNK, CHUNK), CHUNK)
        for n in range(2):
            shares = share_rows[corner_rows(n, g), :]
            for t in range(2):
                at = pl.ds(t * LANES, LANES)
                edge = lane == (LANES - 1 if t == 0 else 0)
                pace = step[here, at]
                for v in range(NV):
                    share = jnp.where(edge, pltpu.roll(shares, LANES - 1 - v if t == 0 else LANES - CHUNK - v, axis=1), 0.0)
                    if sweep == 0:
                        flow1[n, v, rows_at(g), at] = flow1[n, v, rows_at(g), at] - pace * share
                    else:
                        out_state[n, v, here, at] = out_state[n, v, here, at] - pace * share
                        out_resid[n, v, here, at] = out_resid[n, v, here, at] + share

    def loop(body, begin=0, end=CHUNKS):
        def wrapped(g, carry):
            body(g)
            return carry

        lax.fori_loop(begin, end, wrapped, 0)

    def order(p):
        return (p + 1) % CHUNKS

    step_in.wait()
    flow_in.wait()
    loop(gather)
    turn_first()
    pack_halos(0)
    hear(barrier, nearest)
    cross_copy(0).start()
    start_first_halos()
    tell(known.at[0], rounds[0])
    loop(lambda p: sib_copy(0, order(p)).start())

    def first_mix(p):
        g = order(p)
        sib_copy(0, g).wait_recv()
        mix(0, g)
        par_copy(0, g).start()

    loop(first_mix, 0, FIRST)
    start_columns(0)
    hear(known.at[0], rounds[0])
    tell(known.at[1], rounds[1])
    loop(first_mix, FIRST, CHUNKS)
    for copy in small_in:
        copy.wait()
    source_in.wait()
    cross_arrival(0).wait_recv()
    start_planes()
    hear(known.at[1], rounds[1])
    tell(known.at[2], rounds[2])
    loop(border, 1, CHUNKS - 1)

    def second_mix(p):
        g = order(p)
        sib_copy(1, g).wait_recv()
        mix(1, g)
        par_copy(1, g).start()

    def when(places):
        low_z, high_z = places
        return (z < SZ // 2).astype(jnp.int32) * (low_z - high_z) + high_z

    at_rings, at_halos, at_settle, at_layer = (when(a) for a in (AT_RINGS, AT_HALOS, AT_SETTLE, AT_LAYER))

    def first_sweep(p):
        g = order(p)

        @pl.when(p == at_rings)
        def _():
            hear(known.at[2], rounds[2])
            pass_halos()
            all_done(plane0.at[pl.ds(0, SY - 1)], plane_rsem.at[0])
            forward()
            start_rings()

        @pl.when(p == at_halos)
        def _():
            unpack_halos(0)
            border(0)
            border(CHUNKS - 1)
            turn_border()

        @pl.when(p == at_settle)
        def _():
            all_done(ring0.at[pl.ds(0, SZ - 1)], ring_rsem.at[0])
            all_done(columns0, column_rsem.at[0])
            settle(0)
            for c in range(2):
                plane1[place, c] = before[c] - pace_lanes[c] * share_lanes[c]
            start_layer()
            start_columns(1)
            turn_share()

        par_copy(0, g).wait_recv()
        advance(0, g)
        sib_copy(1, g).start()

        @pl.when(p > 0)
        def _():
            second_mix(p - 1)

    loop(first_sweep)
    second_mix(CHUNKS - 1)
    all_done(sib1, sib_ssem.at[1])
    loop(lambda g: patch(0, g))
    pack_halos(1)
    start_halos(1)

    def second_sweep(p):
        g = order(p)

        @pl.when(p == at_layer)
        def _():
            all_done(plane1.at[pl.ds(0, LAYER - 1)], layer_rsem.at[0])
            pass_across()
            cross_copy(1).start()

        @pl.when(p == AT_SECOND_HALOS)
        def _():
            unpack_halos(1)

        par_copy(1, g).wait_recv()
        advance(1, g)

    loop(second_sweep)
    all_done(columns1, column_rsem.at[1])
    cross_arrival(1).wait_recv()
    settle(1)
    turn_share()
    loop(lambda g: patch(1, g))

    all_done(sib0, sib_ssem.at[0])
    all_done(send0, par_ssem.at[0])
    all_done(send1, par_ssem.at[1])
    all_done(columns0, column_ssem.at[0])
    all_done(columns1, column_ssem.at[1])
    all_done(plane0.at[pl.ds(0, SY - 1)], plane_ssem.at[0])
    all_done(ring0.at[pl.ds(0, SZ - 1)], ring_ssem.at[0])
    all_done(plane1.at[pl.ds(0, LAYER - 1)], layer_ssem.at[0])
    for sweep in range(2):
        cross_copy(sweep).wait_send()
        all_done(halos_out[sweep], halo_ssem.at[sweep])

    @pl.when(jnp.logical_or(first_in_ring, last_in_ring))
    def _():
        all_done(relay, halo_ssem.at[0])


def store(state, resid, state_hbm, resid_hbm, sems):
    copies = [
        pltpu.make_async_copy(state, state_hbm, sems.at[0]),
        pltpu.make_async_copy(resid, resid_hbm, sems.at[1]),
    ]
    for copy in copies:
        copy.start()
    for copy in copies:
        copy.wait()


def local(flow_state, flow_source, pseudo_step, flux_jacobian, stator_donor, stator_weight, rotor_donor, rotor_weight):
    f32 = jnp.float32
    block = (2, NV, ROWS, AX)
    padded = (2, NV, ROWS + 2 * CHUNK, AX)
    chunked = (CHUNKS, 2, NV, CHUNK, AX)
    anywhere = pl.BlockSpec(memory_space=pltpu.HBM)
    vmem = pl.BlockSpec(memory_space=pltpu.VMEM)
    dma = pltpu.SemaphoreType.DMA
    regular = pltpu.SemaphoreType.REGULAR
    halo = (2, 2, NV, AX)
    args = (
        flow_state, flow_source, pseudo_step, flux_jacobian, stator_donor, stator_weight, rotor_donor, rotor_weight
    )
    state, resid = pl.pallas_call(
        kernel,
        out_shape=(pltpu.VMEM(block, f32), pltpu.VMEM(block, f32)),
        in_specs=[anywhere] * 8,
        out_specs=(vmem, vmem),
        scratch_shapes=[
            pltpu.SMEM((NV, NV), f32),
            pltpu.SMEM((2, ROWS), jnp.int32),
            pltpu.VMEM((2, ROWS), f32),
            pltpu.SMEM((2, ROWS), jnp.int32),
            pltpu.VMEM((2, ROWS), f32),
            pltpu.VMEM(padded, f32),
            pltpu.VMEM(padded, f32),
            pltpu.VMEM(block, f32),
            pltpu.VMEM((ROWS, AX), f32),
            *[pltpu.VMEM(chunked, f32) for _ in range(6)],
            pltpu.VMEM((LANES, LANES), f32),
            pltpu.VMEM((SY, SX, 2, NV, LANES), f32),
            pltpu.VMEM((SZ * SY, 2, NV, LANES), f32),
            pltpu.VMEM((SZ, 4, NV, LANES), f32),
            pltpu.VMEM((SX, 4, NV, LANES), f32),
            *[pltpu.VMEM((3, 2, NV, LANES), f32) for _ in range(2)],
            pltpu.VMEM((2, NV, LANES), f32),
            pltpu.VMEM((2, 1, LANES), f32),
            pltpu.VMEM((2, NV, LANES), f32),
            pltpu.VMEM((LANES, LANES), f32),
            *[pltpu.VMEM(halo, f32) for _ in range(4)],
            pltpu.VMEM(halo[1:], f32),
            dma((1,)),
            regular((3,)),
            dma((8,)),
            dma((2,)),
            dma((2 * CHUNKS,)),
            dma((2,)),
            dma((2 * CHUNKS,)),
            dma((2,)),
            dma((2,)),
            *[dma((1,)) for _ in range(6)],
            dma((2,)),
            dma((2,)),
            dma((2,)),
            dma((2,)),
        ],
        compiler_params=pltpu.CompilerParams(
            collective_id=0, has_side_effects=True, vmem_limit_bytes=24 * 2**20
        ),
    )(*[pltpu.with_memory_space_constraint(arg, pltpu.HBM) for arg in args])
    return pl.pallas_call(
        store,
        out_shape=(pltpu.HBM(block, f32), pltpu.HBM(block, f32)),
        in_specs=[vmem, vmem],
        out_specs=(anywhere, anywhere),
        scratch_shapes=[dma((2,))],
    )(
        pltpu.with_memory_space_constraint(state, pltpu.VMEM), pltpu.with_memory_space_constraint(resid, pltpu.VMEM)
    )


def solution(mesh):
    return jax.shard_map(
        local,
        mesh=mesh,
        in_specs=(
            P("inst", None, "space", None),
            P("inst", None, "space", None),
            P("space", None),
            P(),
            P("inst", "space"),
            P("inst", "space"),
            P("inst", "space"),
            P("inst", "space"),
        ),
        out_specs=(P("inst", None, "space", None), P("inst", None, "space", None)),
        check_vma=False,
    )
```

```python
import math

import jax
import jax.numpy as jnp
from jax import lax
from jax.experimental import pallas as pl
from jax.experimental.pallas import tpu as pltpu
from jax.sharding import PartitionSpec as P

MESH = pl.DeviceIdType.MESH
NT = 8
NV = 5
ROWS = 64
AX = 256
LANES = 128
CHUNK = 8
CHUNKS = ROWS // CHUNK
SX, SZ, SY = 2, 8, 4
SPACE = SX * SZ * SY
LAYER = SZ * SY
VISCOSITY = 0.5
AT_RINGS, AT_HALOS, AT_SETTLE = (3, 1), (5, 3), (6, 5)
AT_LAYER, AT_SECOND_HALOS = (4, 3), 6
AHEAD, PACE = (5, 3), 3
FIRST = 2


def spectral(gap):
    gap = gap % NT
    if gap == 0:
        return 0.0
    return 0.5 * (-1.0) ** gap * math.cos(math.pi * gap / NT) / math.sin(math.pi * gap / NT)


def kernel(
    flow_hbm, source_hbm, step_hbm, *rest,
):
    *small_hbm, out_state, out_resid = rest[:7]
    body(flow_hbm, source_hbm, step_hbm, small_hbm, out_state, out_resid, *rest[7:])


def body(
    flow_hbm, source_hbm, step_hbm, small_hbm, out_state, out_resid,
    jac, stator_donor, stator_weight, rotor_donor, rotor_weight,
    flow0, flow1, source, step, sib0, sib1, send0, send1, recv0, recv1,
    corner, plane0, plane1, ring0, cross, columns0, columns1, before, pace_lanes, share_lanes, share_rows,
    halo_out0, halo_out1, halo_in0, halo_in1, relay, relay_sem, raw, raw_ssem, raw_rsem,
    known, load_sem, sib_ssem, sib_rsem, par_ssem, par_rsem, halo_ssem, halo_rsem,
    plane_ssem, plane_rsem, ring_ssem, ring_rsem, layer_ssem, layer_rsem, cross_ssem, cross_rsem, column_ssem, column_rsem,
):
    inst, space = lax.axis_index("inst"), lax.axis_index("space")
    pair, core = inst // 2, inst % 2
    x, z, y = space // (SZ * SY), (space // SY) % SZ, space % SY
    sibling = (pair * 2 + 1 - core, space)
    partner = ((1 - pair) * 2 + core, space)
    diagonal = ((1 - pair) * 2 + 1 - core, space)
    across = (inst, (space + SPACE // 2) % SPACE)
    above = (inst, (space + SPACE - 1) % SPACE)
    below = (inst, (space + 1) % SPACE)
    place = space % LAYER

    def plane_peer(k):
        return inst, x * LAYER + z * SY + (y + k) % SY

    def ring_peer(k):
        return inst, x * LAYER + ((z + k) % SZ) * SY + y

    flow_in = pltpu.make_async_copy(flow_hbm, flow0.at[:, :, pl.ds(CHUNK, ROWS), :], load_sem.at[0])
    source_in = pltpu.make_async_copy(source_hbm, source, load_sem.at[1])
    step_in = pltpu.make_async_copy(step_hbm, step, load_sem.at[2])
    flow_in.start()
    source_in.start()
    step_in.start()
    small = (jac, stator_donor, stator_weight, rotor_donor, rotor_weight)
    small_in = [
        pltpu.make_async_copy(src, dst, load_sem.at[3 + k]) for k, (src, dst) in enumerate(zip(small_hbm, small))
    ]
    for copy in small_in:
        copy.start()

    def on_line(k):
        return [(z >= k, (inst, space - k * SY)), (z < SZ - k, (inst, space + k * SY))]

    always = space >= 0
    nearest = [(always, sibling), (always, partner), (always, across)]
    nearest += [(always, plane_peer(k)) for k in range(1, SY)] + on_line(1)

    def tell(semaphore, devices):
        for exists, device in devices:

            @pl.when(exists)
            def _(device=device):
                pl.semaphore_signal(semaphore, inc=1, device_id=device, device_id_type=MESH)

    def hear(semaphore, devices):
        count = 0
        for exists, _ in devices:
            count = count + exists.astype(jnp.int32)
        pl.semaphore_wait(semaphore, count)

    rounds = [on_line(1), on_line(2), on_line(4)]
    barrier = pltpu.get_barrier_semaphore()
    tell(barrier, nearest)

    lane = lax.broadcasted_iota(jnp.int32, (CHUNK, LANES), 1)
    low = lax.broadcasted_iota(jnp.int32, (NV, LANES), 1) < ROWS

    def scalars(table):
        return [[table(a - b) for b in range(2)] for a in range(2)]

    from_own = scalars(spectral)
    from_sib = scalars(lambda g: jnp.where(core == 0, spectral(g - 2), spectral(g + 2)).astype(jnp.float32))
    to_own = scalars(lambda g: spectral(g + 4))
    to_sib = scalars(lambda g: jnp.where(core == 0, spectral(g + 2), spectral(g + 6)).astype(jnp.float32))

    def remote(src, dst, ssem, rsem, device):
        return pltpu.make_async_remote_copy(
            src_ref=src, dst_ref=dst, send_sem=ssem, recv_sem=rsem, device_id=device, device_id_type=MESH
        )

    def rows_at(g):
        return pl.ds(pl.multiple_of(CHUNK + g * CHUNK, CHUNK), CHUNK)

    def order(p):
        return (p + 1) % CHUNKS

    def all_done(ref, semaphore):
        pltpu.make_async_copy(ref, ref, semaphore).wait()

    def sib_copy(sweep, g):
        flow, sib = (flow0, sib0) if sweep == 0 else (flow1, sib1)
        at = sweep * CHUNKS + g
        return remote(flow.at[:, :, rows_at(g), :], sib.at[g], sib_ssem.at[sweep], sib_rsem.at[at], sibling)

    def par_copy(sweep, g):
        send, recv = (send0, recv0) if sweep == 0 else (send1, recv1)
        at = sweep * CHUNKS + g
        return remote(send.at[g], recv.at[g], par_ssem.at[sweep], par_rsem.at[at], partner)

    def raw_copy():
        mine = flow0.at[:, :, rows_at(order(0)), :]
        return remote(mine, raw.at[0], raw_ssem.at[0], raw_rsem.at[0], partner)

    def raw_pass():
        return remote(raw.at[0], raw.at[1], raw_ssem.at[1], raw_rsem.at[1], sibling)

    halos_out, halos_in = (halo_out0, halo_out1), (halo_in0, halo_in1)

    def send_row(sweep, row, into, device):
        remote(row, into, halo_ssem.at[sweep], halo_rsem.at[sweep], device).start()

    def start_halos(sweep):
        send_row(sweep, halos_out[sweep].at[0], halos_in[sweep].at[1], above)
        send_row(sweep, halos_out[sweep].at[1], halos_in[sweep].at[0], below)

    first_in_ring, last_in_ring = y == 0, y == SY - 1

    def start_first_halos():
        for side, stays, device in ((0, y > 0, above), (1, y < SY - 1, below)):

            @pl.when(stays)
            def _(side=side, device=device):
                send_row(0, halo_out0.at[side], halo_in0.at[1 - side], device)

            @pl.when(jnp.logical_not(stays))
            def _(side=side):
                other_end = plane_peer(SY - 1 if side == 0 else 1)
                remote(halo_out0.at[side], relay, halo_ssem.at[0], relay_sem.at[0], other_end).start()

    def pass_halos():
        for here, side, device in (
            (last_in_ring, 0, (inst, (space + SPACE - SY) % SPACE)),
            (first_in_ring, 1, (inst, (space + SY) % SPACE)),
        ):

            @pl.when(here)
            def _(side=side, device=device):
                all_done(relay, relay_sem.at[0])
                send_row(0, relay, halo_in0.at[1 - side], device)

    def pack_halos(sweep):
        flow, out = (flow0 if sweep == 0 else flow1), halos_out[sweep]
        for side, row in enumerate((CHUNK, CHUNK + ROWS - 1)):
            for n in range(2):
                for v in range(NV):
                    out[side, n, pl.ds(v, 1), :] = flow[n, v, pl.ds(row, 1), :]

    def unpack_halos(sweep):
        flow, into = (flow0 if sweep == 0 else flow1), halos_in[sweep]
        all_done(into, halo_rsem.at[sweep])
        for side, row in enumerate((CHUNK - 1, CHUNK + ROWS)):
            for n in range(2):
                for v in range(NV):
                    flow[n, v, pl.ds(row, 1), :] = into[side, n, pl.ds(v, 1), :]

    def cross_copy(sweep):
        mine = plane0.at[y, x] if sweep == 0 else cross.at[x]
        return remote(mine, mine, cross_ssem.at[sweep], cross_rsem.at[sweep], across)

    def cross_arrival(sweep):
        theirs = plane0.at[y, 1 - x] if sweep == 0 else cross.at[1 - x]
        return remote(theirs, theirs, cross_ssem.at[sweep], cross_rsem.at[sweep], across)

    def start_planes():
        mine = plane0.at[y]
        for k in range(1, SY):
            remote(mine, mine, plane_ssem.at[0], plane_rsem.at[0], plane_peer(k)).start()

    def start_rings():
        mine = ring0.at[z]
        for k in range(1, SZ):
            remote(mine, mine, ring_ssem.at[0], ring_rsem.at[0], ring_peer(k)).start()

    def start_layer():
        mine = plane1.at[place]

        def start(k, carry):
            other = k + (k >= place).astype(jnp.int32)
            remote(mine, mine, layer_ssem.at[0], layer_rsem.at[0], (inst, x * LAYER + other)).start()
            return carry

        lax.fori_loop(0, LAYER - 1, start, 0)

    def start_columns(sweep):
        mine = plane0.at[y, x] if sweep == 0 else plane1.at[place]
        for k, device in enumerate((sibling, partner, diagonal)):
            into = (columns0, columns1)[sweep].at[k]
            remote(mine, into, column_ssem.at[sweep], column_rsem.at[sweep], device).start()

    def to_lane(tiles, c, total):
        for v, tile in enumerate(tiles):
            q = c * CHUNK + v
            total = jnp.where(lane == q, pltpu.roll(tile, (q + 1) if c == 0 else q, axis=1), total)
        return total

    def corner_rows(n, g):
        return pl.ds(pl.multiple_of(n * ROWS + g * CHUNK, CHUNK), CHUNK)

    def gather(g):
        here = pl.ds(pl.multiple_of(g * CHUNK, CHUNK), CHUNK)
        for n in range(2):
            total = jnp.zeros((CHUNK, LANES), jnp.float32)
            for c in range(2):
                at = pl.ds(c * LANES, LANES)
                total = to_lane([flow0[n, v, rows_at(g), at] for v in range(NV)] + [step[here, at]], c, total)
            corner[corner_rows(n, g), :] = total

    def turn_first():
        turned = corner[...].T
        for c in range(2):
            plane0[y, x, c] = turned[c * CHUNK : c * CHUNK + NV, :]
            pace_lanes[c] = turned[c * CHUNK + NV : c * CHUNK + NV + 1, :]

    def turn_border():
        turned = corner[...].T
        for c in range(2):
            before[c] = turned[c * CHUNK : c * CHUNK + NV, :]

    def donor(c, n):
        return (stator_donor if c == 0 else rotor_donor)[n, 0]

    def halves(first, second, n):
        if n == 0:
            return jnp.where(low, first, pltpu.roll(second, ROWS, axis=1))
        return jnp.where(low, pltpu.roll(first, ROWS, axis=1), second)

    def forward():
        for c in range(2):
            for n in range(2):
                ahead = (donor(c, n) // ROWS + SPACE - space) % SPACE
                found = []
                for d in (ahead, (ahead + 1) % SPACE):
                    dx, dz, dy = d // LAYER, (d // SY) % SZ, d % SY
                    carry = (y + dy) // SY
                    wants = (z + 2 * SZ - dz - carry) % SZ
                    over = (wants + dz + carry) // SZ
                    found.append(plane0[(y + dy) % SY, (x + dx + over) % SX, c])
                ring0[z, c * 2 + n] = halves(*found, n)

    def from_ring(c, n):
        block = donor(c, n) // ROWS
        here = ring0[(block // SY) % SZ, c * 2 + n]
        there = ring0[((block + 1) // SY) % SZ, c * 2 + n]
        return jnp.where(low, here, there)

    def pass_across():
        for c in range(2):
            for n in range(2):
                block = donor(c, n) // ROWS
                cross[x, c * 2 + n] = halves(plane1[block % LAYER, c], plane1[(block + 1) % LAYER, c], n)

    def from_cross(c, n):
        block = donor(c, n) // ROWS
        here = cross[(block // LAYER) % SX, c * 2 + n]
        there = cross[((block + 1) // LAYER) % SX, c * 2 + n]
        return jnp.where(low, here, there)

    def sum_columns(sweep):
        columns = (columns0, columns1)[sweep]
        sums = []
        for c in range(2):
            total = None
            for k, table in enumerate((from_sib, to_own, to_sib)):
                straight = columns[k, c]
                turned = pltpu.roll(straight, ROWS, axis=1)
                same = jnp.where(low, table[0][0], table[1][1])
                crossed = jnp.where(low, table[0][1], table[1][0])
                term = same * straight + crossed * turned
                total = term if total is None else total + term
            sums.append(total)
        return sums

    def settle(sweep, remote_sum):
        entering = []
        for c in range(2):
            weights = stator_weight if c == 0 else rotor_weight
            values = []
            for n in range(2):
                window = from_ring(c, n) if sweep == 0 else from_cross(c, n)
                offset = donor(c, n) % ROWS
                first = pltpu.roll(window, (LANES - offset) % LANES, axis=1)
                second = pltpu.roll(window, LANES - 1 - offset, axis=1)
                weight = weights[pl.ds(n, 1), :]
                weight = jnp.concatenate([weight, weight], axis=1)
                values.append((1.0 - weight) * first + weight * second)
            entering.append(jnp.where(low, values[0], pltpu.roll(values[1], ROWS, axis=1)))
        stator, rotor = entering
        share_lanes[0] = -VISCOSITY * rotor
        share_lanes[1] = -VISCOSITY * stator
        for v in range(NV):
            total = share_lanes[1, pl.ds(v, 1), :]
            for w in range(NV):
                total = total - jac[v, w] * stator[w : w + 1, :]
            share_lanes[1, pl.ds(v, 1), :] = total
        for c in range(2):
            share_lanes[c] = share_lanes[c] + remote_sum[c]

    def turn_share():
        corner[...] = jnp.zeros_like(corner)
        for t in range(2):
            corner[pl.ds(t * CHUNK, NV), :] = share_lanes[t]
        share_rows[...] = corner[...].T

    def spread(own, other, into):
        for v in range(NV):
            for t in range(2):
                at = pl.ds(t * LANES, LANES)
                ours, theirs = [own(n, v, at) for n in range(2)], [other(n, v, at) for n in range(2)]
                for a in range(2):
                    into[a, v, :, at] = (
                        to_own[a][0] * ours[0] + to_own[a][1] * ours[1]
                        + (to_sib[a][0] * theirs[0] + to_sib[a][1] * theirs[1])
                    )

    def mix(sweep, g):
        flow, sib, send = (flow0, sib0, send0) if sweep == 0 else (flow1, sib1, send1)
        spread(lambda n, v, at: flow[n, v, rows_at(g), at], lambda n, v, at: sib[g, n, v, :, at], send.at[g])

    def mix_raw():
        spread(lambda n, v, at: raw[0, n, v, :, at], lambda n, v, at: raw[1, n, v, :, at], recv0.at[order(0)])

    def inner(flow, g, t):
        here = pl.ds(pl.multiple_of(g * CHUNK, CHUNK), CHUNK)
        jacobian = [[jac[v, w] for w in range(NV)] for v in range(NV)]
        at = pl.ds(t * LANES, LANES)
        centre = [[flow[n, v, rows_at(g), at] for v in range(NV)] for n in range(2)]
        parts = []
        for n in range(2):
            diff, smooth = [], []
            for v in range(NV):
                window = flow[n, v, pl.ds(pl.multiple_of(g * CHUNK, CHUNK), 3 * CHUNK), at]
                upper = window[CHUNK - 1 : 2 * CHUNK - 1]
                lower = window[CHUNK + 1 : 2 * CHUNK + 1]
                f = centre[n][v]
                left = jnp.where(lane == 0, 0.0, pltpu.roll(f, 1, axis=1))
                right = jnp.where(lane == LANES - 1, 0.0, pltpu.roll(f, LANES - 1, axis=1))
                diff.append(f - left)
                smooth.append(VISCOSITY * (4.0 * f - left - right - upper - lower))
            row = []
            for v in range(NV):
                convect = jacobian[v][0] * diff[0]
                for w in range(1, NV):
                    convect = convect + jacobian[v][w] * diff[w]
                derivative = from_own[n][0] * centre[0][v] + from_own[n][1] * centre[1][v]
                row.append(convect + smooth[v] + derivative - source[n, v, here, at])
            parts.append(row)
        return centre, parts

    def border(g):
        here = pl.ds(pl.multiple_of(g * CHUNK, CHUNK), CHUNK)
        totals = [jnp.zeros((CHUNK, LANES), jnp.float32) for _ in range(2)]
        for t in range(2):
            pace = step[here, pl.ds(t * LANES, LANES)]
            centre, parts = inner(flow0, g, t)
            for n in range(2):
                totals[n] = to_lane([centre[n][v] - pace * parts[n][v] for v in range(NV)], t, totals[n])
        for n in range(2):
            corner[corner_rows(n, g), :] = totals[n]

    def advance(sweep, g):
        flow, sib, recv = (flow0, sib0, recv0) if sweep == 0 else (flow1, sib1, recv1)
        here = pl.ds(pl.multiple_of(g * CHUNK, CHUNK), CHUNK)
        for t in range(2):
            at = pl.ds(t * LANES, LANES)
            pace = step[here, at]
            edge = lane == (LANES - 1 if t == 0 else 0)
            centre, parts = inner(flow, g, t)
            for n in range(2):
                for v in range(NV):
                    others = (
                        from_sib[n][0] * sib[g, 0, v, :, at] + from_sib[n][1] * sib[g, 1, v, :, at]
                        + recv[g, n, v, :, at]
                    )
                    residual = parts[n][v] + jnp.where(edge, 0.0, others)
                    new = centre[n][v] - pace * residual
                    if sweep == 0:
                        flow1[n, v, rows_at(g), at] = new
                    else:
                        out_state[n, v, here, at] = new
                        out_resid[n, v, here, at] = residual

    def patch(sweep, g):
        here = pl.ds(pl.multiple_of(g * CHUNK, CHUNK), CHUNK)
        for n in range(2):
            shares = share_rows[corner_rows(n, g), :]
            for t in range(2):
                at = pl.ds(t * LANES, LANES)
                edge = lane == (LANES - 1 if t == 0 else 0)
                pace = step[here, at]
                for v in range(NV):
                    share = jnp.where(edge, pltpu.roll(shares, LANES - 1 - v if t == 0 else LANES - CHUNK - v, axis=1), 0.0)
                    if sweep == 0:
                        flow1[n, v, rows_at(g), at] = flow1[n, v, rows_at(g), at] - pace * share
                    else:
                        out_state[n, v, here, at] = out_state[n, v, here, at] - pace * share
                        out_resid[n, v, here, at] = out_resid[n, v, here, at] + share

    def loop(body, begin=0, end=CHUNKS):
        def wrapped(g, carry):
            body(g)
            return carry

        lax.fori_loop(begin, end, wrapped, 0)

    step_in.wait()
    flow_in.wait()
    loop(gather)
    turn_first()
    pack_halos(0)
    hear(barrier, nearest)
    cross_copy(0).start()
    raw_copy().start()
    loop(lambda p: sib_copy(0, order(p)).start())
    tell(known.at[0], rounds[0])
    start_first_halos()

    def first_mix(p):
        g = order(p)
        sib_copy(0, g).wait_recv()
        mix(0, g)
        par_copy(0, g).start()

    loop(first_mix, 1, FIRST)
    start_columns(0)
    hear(known.at[0], rounds[0])
    tell(known.at[1], rounds[1])
    loop(first_mix, FIRST, CHUNKS)
    for copy in small_in:
        copy.wait()
    source_in.wait()
    cross_arrival(0).wait_recv()
    start_planes()
    hear(known.at[1], rounds[1])
    tell(known.at[2], rounds[2])
    loop(border, 1, CHUNKS - 1)
    raw_copy().wait_recv()
    raw_pass().start()

    def when(places):
        low_z, high_z = places
        return (1 - z // (SZ // 2)) * (low_z - high_z) + high_z

    at_rings, at_halos, at_settle, at_layer = (when(a) for a in (AT_RINGS, AT_HALOS, AT_SETTLE, AT_LAYER))
    ahead = when(AHEAD)

    def second_mix(p):
        g = order(p)
        sib_copy(1, g).wait_recv()
        mix(1, g)

        @pl.when(p < ahead)
        def _():
            par_copy(1, g).start()

    def first_sweep(p):
        g = order(p)

        @pl.when(p == at_rings)
        def _():
            hear(known.at[2], rounds[2])
            pass_halos()
            all_done(plane0.at[pl.ds(0, SY - 1)], plane_rsem.at[0])
            forward()
            start_rings()

        @pl.when(p == at_halos)
        def _():
            unpack_halos(0)
            border(0)
            border(CHUNKS - 1)
            turn_border()

        @pl.when(p == at_settle)
        def _():
            all_done(columns0, column_rsem.at[0])
            remote_sum = sum_columns(0)
            all_done(ring0.at[pl.ds(0, SZ - 1)], ring_rsem.at[0])
            settle(0, remote_sum)
            for c in range(2):
                plane1[place, c] = before[c] - pace_lanes[c] * share_lanes[c]
            start_layer()
            start_columns(1)
            turn_share()

        @pl.when(p == 0)
        def _():
            sib_copy(0, g).wait_recv()
            raw_pass().wait_recv()
            mix_raw()

        @pl.when(p > 0)
        def _():
            par_copy(0, g).wait_recv()

        advance(0, g)
        sib_copy(1, g).start()

        @pl.when(p > 0)
        def _():
            second_mix(p - 1)

    loop(first_sweep)
    second_mix(CHUNKS - 1)
    all_done(sib1, sib_ssem.at[1])
    loop(lambda g: patch(0, g))
    pack_halos(1)
    start_halos(1)

    def second_sweep(p):
        g = order(p)

        @pl.when(p == at_layer)
        def _():
            all_done(plane1.at[pl.ds(0, LAYER - 1)], layer_rsem.at[0])
            pass_across()
            cross_copy(1).start()

        @pl.when(p == AT_SECOND_HALOS)
        def _():
            unpack_halos(1)

        par_copy(1, g).wait_recv()

        @pl.when(jnp.logical_and(p + PACE >= ahead, p + PACE < CHUNKS))
        def _():
            par_copy(1, order(p + PACE)).start()

        advance(1, g)

    loop(second_sweep)
    all_done(columns1, column_rsem.at[1])
    remote_sum = sum_columns(1)
    cross_arrival(1).wait_recv()
    settle(1, remote_sum)
    turn_share()
    loop(lambda g: patch(1, g))

    all_done(sib0, sib_ssem.at[0])
    all_done(send0.at[pl.ds(0, CHUNKS - 1)], par_ssem.at[0])
    raw_copy().wait_send()
    raw_pass().wait_send()
    all_done(send1, par_ssem.at[1])
    all_done(columns0, column_ssem.at[0])
    all_done(columns1, column_ssem.at[1])
    all_done(plane0.at[pl.ds(0, SY - 1)], plane_ssem.at[0])
    all_done(ring0.at[pl.ds(0, SZ - 1)], ring_ssem.at[0])
    all_done(plane1.at[pl.ds(0, LAYER - 1)], layer_ssem.at[0])
    for sweep in range(2):
        cross_copy(sweep).wait_send()
        all_done(halos_out[sweep], halo_ssem.at[sweep])

    @pl.when(jnp.logical_or(first_in_ring, last_in_ring))
    def _():
        all_done(relay, halo_ssem.at[0])


def store(state, resid, state_hbm, resid_hbm, sems):
    copies = [
        pltpu.make_async_copy(state, state_hbm, sems.at[0]),
        pltpu.make_async_copy(resid, resid_hbm, sems.at[1]),
    ]
    for copy in copies:
        copy.start()
    for copy in copies:
        copy.wait()


def local(flow_state, flow_source, pseudo_step, flux_jacobian, stator_donor, stator_weight, rotor_donor, rotor_weight):
    f32 = jnp.float32
    block = (2, NV, ROWS, AX)
    padded = (2, NV, ROWS + 2 * CHUNK, AX)
    chunked = (CHUNKS, 2, NV, CHUNK, AX)
    anywhere = pl.BlockSpec(memory_space=pltpu.HBM)
    vmem = pl.BlockSpec(memory_space=pltpu.VMEM)
    dma = pltpu.SemaphoreType.DMA
    regular = pltpu.SemaphoreType.REGULAR
    halo = (2, 2, NV, AX)
    args = (
        flow_state, flow_source, pseudo_step, flux_jacobian, stator_donor, stator_weight, rotor_donor, rotor_weight
    )
    state, resid = pl.pallas_call(
        kernel,
        out_shape=(pltpu.VMEM(block, f32), pltpu.VMEM(block, f32)),
        in_specs=[anywhere] * 8,
        out_specs=(vmem, vmem),
        scratch_shapes=[
            pltpu.SMEM((NV, NV), f32),
            pltpu.SMEM((2, ROWS), jnp.int32),
            pltpu.VMEM((2, ROWS), f32),
            pltpu.SMEM((2, ROWS), jnp.int32),
            pltpu.VMEM((2, ROWS), f32),
            pltpu.VMEM(padded, f32),
            pltpu.VMEM(padded, f32),
            pltpu.VMEM(block, f32),
            pltpu.VMEM((ROWS, AX), f32),
            *[pltpu.VMEM(chunked, f32) for _ in range(6)],
            pltpu.VMEM((LANES, LANES), f32),
            pltpu.VMEM((SY, SX, 2, NV, LANES), f32),
            pltpu.VMEM((SZ * SY, 2, NV, LANES), f32),
            pltpu.VMEM((SZ, 4, NV, LANES), f32),
            pltpu.VMEM((SX, 4, NV, LANES), f32),
            *[pltpu.VMEM((3, 2, NV, LANES), f32) for _ in range(2)],
            pltpu.VMEM((2, NV, LANES), f32),
            pltpu.VMEM((2, 1, LANES), f32),
            pltpu.VMEM((2, NV, LANES), f32),
            pltpu.VMEM((LANES, LANES), f32),
            *[pltpu.VMEM(halo, f32) for _ in range(4)],
            pltpu.VMEM(halo[1:], f32),
            dma((1,)),
            pltpu.VMEM((2, *chunked[1:]), f32),
            dma((2,)),
            dma((2,)),
            regular((3,)),
            dma((8,)),
            dma((2,)),
            dma((2 * CHUNKS,)),
            dma((2,)),
            dma((2 * CHUNKS,)),
            dma((2,)),
            dma((2,)),
            *[dma((1,)) for _ in range(6)],
            dma((2,)),
            dma((2,)),
            dma((2,)),
            dma((2,)),
        ],
        compiler_params=pltpu.CompilerParams(
            collective_id=0, has_side_effects=True, vmem_limit_bytes=24 * 2**20
        ),
    )(*[pltpu.with_memory_space_constraint(arg, pltpu.HBM) for arg in args])
    return pl.pallas_call(
        store,
        out_shape=(pltpu.HBM(block, f32), pltpu.HBM(block, f32)),
        in_specs=[vmem, vmem],
        out_specs=(anywhere, anywhere),
        scratch_shapes=[dma((2,))],
    )(
        pltpu.with_memory_space_constraint(state, pltpu.VMEM), pltpu.with_memory_space_constraint(resid, pltpu.VMEM)
    )


def solution(mesh):
    return jax.shard_map(
        local,
        mesh=mesh,
        in_specs=(
            P("inst", None, "space", None),
            P("inst", None, "space", None),
            P("space", None),
            P(),
            P("inst", "space"),
            P("inst", "space"),
            P("inst", "space"),
            P("inst", "space"),
        ),
        out_specs=(P("inst", None, "space", None), P("inst", None, "space", None)),
        check_vma=False,
    )
```

```python
import math

import jax
import jax.numpy as jnp
from jax import lax
from jax.experimental import pallas as pl
from jax.experimental.pallas import tpu as pltpu
from jax.sharding import PartitionSpec as P

MESH = pl.DeviceIdType.MESH
NT = 8
NV = 5
ROWS = 64
AX = 256
LANES = 128
CHUNK = 8
CHUNKS = ROWS // CHUNK
SX, SZ, SY = 2, 8, 4
SPACE = SX * SZ * SY
LAYER = SZ * SY
VISCOSITY = 0.5
AT_RINGS, AT_HALOS, AT_SETTLE = (3, 1), (5, 3), (6, 5)
AT_LAYER, AT_SECOND_HALOS = (4, 3), 6
AHEAD, PACE = (5, 3), 3
FIRST = 2


def spectral(gap):
    gap = gap % NT
    if gap == 0:
        return 0.0
    return 0.5 * (-1.0) ** gap * math.cos(math.pi * gap / NT) / math.sin(math.pi * gap / NT)


def kernel(
    flow_hbm, source_hbm, step_hbm, *rest,
):
    *small_hbm, out_state, out_resid = rest[:7]
    body(flow_hbm, source_hbm, step_hbm, small_hbm, out_state, out_resid, *rest[7:])


def body(
    flow_hbm, source_hbm, step_hbm, small_hbm, out_state, out_resid,
    jac, stator_donor, stator_weight, rotor_donor, rotor_weight,
    flow0, flow1, source, step, sib0, sib1, send0, send1, recv0, recv1,
    corner, plane0, plane1, ring0, cross, columns0, columns1, before, pace_lanes, share_lanes, share_rows,
    halo_out0, halo_out1, halo_in0, halo_in1, relay, relay_sem, raw, raw_ssem, raw_rsem,
    known, load_sem, sib_ssem, sib_rsem, par_ssem, par_rsem, halo_ssem, halo_rsem,
    plane_ssem, plane_rsem, ring_ssem, ring_rsem, layer_ssem, layer_rsem, cross_ssem, cross_rsem, column_ssem, column_rsem,
):
    inst, space = lax.axis_index("inst"), lax.axis_index("space")
    pair, core = inst // 2, inst % 2
    x, z, y = space // (SZ * SY), (space // SY) % SZ, space % SY
    sibling = (pair * 2 + 1 - core, space)
    partner = ((1 - pair) * 2 + core, space)
    diagonal = ((1 - pair) * 2 + 1 - core, space)
    across = (inst, (space + SPACE // 2) % SPACE)
    above = (inst, (space + SPACE - 1) % SPACE)
    below = (inst, (space + 1) % SPACE)
    place = space % LAYER

    def plane_peer(k):
        return inst, x * LAYER + z * SY + (y + k) % SY

    def ring_peer(k):
        return inst, x * LAYER + ((z + k) % SZ) * SY + y

    flow_in = pltpu.make_async_copy(flow_hbm, flow0.at[:, :, pl.ds(CHUNK, ROWS), :], load_sem.at[0])
    source_in = pltpu.make_async_copy(source_hbm, source, load_sem.at[1])
    step_in = pltpu.make_async_copy(step_hbm, step, load_sem.at[2])
    flow_in.start()
    source_in.start()
    step_in.start()
    small = (jac, stator_donor, stator_weight, rotor_donor, rotor_weight)
    small_in = [
        pltpu.make_async_copy(src, dst, load_sem.at[3 + k]) for k, (src, dst) in enumerate(zip(small_hbm, small))
    ]
    for copy in small_in:
        copy.start()

    def on_line(k):
        return [(z >= k, (inst, space - k * SY)), (z < SZ - k, (inst, space + k * SY))]

    always = space >= 0
    nearest = [(always, sibling), (always, partner), (always, across)]
    nearest += [(always, plane_peer(k)) for k in range(1, SY)] + on_line(1)

    def tell(semaphore, devices):
        for exists, device in devices:

            @pl.when(exists)
            def _(device=device):
                pl.semaphore_signal(semaphore, inc=1, device_id=device, device_id_type=MESH)

    def hear(semaphore, devices):
        count = 0
        for exists, _ in devices:
            count = count + exists.astype(jnp.int32)
        pl.semaphore_wait(semaphore, count)

    rounds = [on_line(1), on_line(2), on_line(4)]
    barrier = pltpu.get_barrier_semaphore()
    tell(barrier, nearest)

    lane = lax.broadcasted_iota(jnp.int32, (CHUNK, LANES), 1)
    low = lax.broadcasted_iota(jnp.int32, (NV, LANES), 1) < ROWS

    def scalars(table):
        return [[table(a - b) for b in range(2)] for a in range(2)]

    from_own = scalars(spectral)
    from_sib = scalars(lambda g: jnp.where(core == 0, spectral(g - 2), spectral(g + 2)).astype(jnp.float32))
    to_own = scalars(lambda g: spectral(g + 4))
    to_sib = scalars(lambda g: jnp.where(core == 0, spectral(g + 2), spectral(g + 6)).astype(jnp.float32))

    def remote(src, dst, ssem, rsem, device):
        return pltpu.make_async_remote_copy(
            src_ref=src, dst_ref=dst, send_sem=ssem, recv_sem=rsem, device_id=device, device_id_type=MESH
        )

    def rows_at(g):
        return pl.ds(pl.multiple_of(CHUNK + g * CHUNK, CHUNK), CHUNK)

    def order(p):
        return (p + 1) % CHUNKS

    def all_done(ref, semaphore):
        pltpu.make_async_copy(ref, ref, semaphore).wait()

    def sib_copy(sweep, g):
        flow, sib = (flow0, sib0) if sweep == 0 else (flow1, sib1)
        at = sweep * CHUNKS + g
        return remote(flow.at[:, :, rows_at(g), :], sib.at[g], sib_ssem.at[sweep], sib_rsem.at[at], sibling)

    def par_copy(sweep, g):
        send, recv = (send0, recv0) if sweep == 0 else (send1, recv1)
        at = sweep * CHUNKS + g
        return remote(send.at[g], recv.at[g], par_ssem.at[sweep], par_rsem.at[at], partner)

    def raw_copy():
        mine = flow0.at[:, :, rows_at(order(0)), :]
        return remote(mine, raw.at[0], raw_ssem.at[0], raw_rsem.at[0], partner)

    def raw_pass():
        return remote(raw.at[0], raw.at[1], raw_ssem.at[1], raw_rsem.at[1], sibling)

    halos_out, halos_in = (halo_out0, halo_out1), (halo_in0, halo_in1)

    def send_row(sweep, row, into, device):
        remote(row, into, halo_ssem.at[sweep], halo_rsem.at[sweep], device).start()

    def start_halos(sweep):
        send_row(sweep, halos_out[sweep].at[0], halos_in[sweep].at[1], above)
        send_row(sweep, halos_out[sweep].at[1], halos_in[sweep].at[0], below)

    first_in_ring, last_in_ring = y == 0, y == SY - 1

    def start_first_halos():
        for side, stays, device in ((0, y > 0, above), (1, y < SY - 1, below)):

            @pl.when(stays)
            def _(side=side, device=device):
                send_row(0, halo_out0.at[side], halo_in0.at[1 - side], device)

            @pl.when(jnp.logical_not(stays))
            def _(side=side):
                other_end = plane_peer(SY - 1 if side == 0 else 1)
                remote(halo_out0.at[side], relay, halo_ssem.at[0], relay_sem.at[0], other_end).start()

    def pass_halos():
        for here, side, device in (
            (last_in_ring, 0, (inst, (space + SPACE - SY) % SPACE)),
            (first_in_ring, 1, (inst, (space + SY) % SPACE)),
        ):

            @pl.when(here)
            def _(side=side, device=device):
                all_done(relay, relay_sem.at[0])
                send_row(0, relay, halo_in0.at[1 - side], device)

    def pack_halos(sweep):
        flow, out = (flow0 if sweep == 0 else flow1), halos_out[sweep]
        for side, row in enumerate((CHUNK, CHUNK + ROWS - 1)):
            for n in range(2):
                for v in range(NV):
                    out[side, n, pl.ds(v, 1), :] = flow[n, v, pl.ds(row, 1), :]

    def unpack_halos(sweep):
        flow, into = (flow0 if sweep == 0 else flow1), halos_in[sweep]
        all_done(into, halo_rsem.at[sweep])
        for side, row in enumerate((CHUNK - 1, CHUNK + ROWS)):
            for n in range(2):
                for v in range(NV):
                    flow[n, v, pl.ds(row, 1), :] = into[side, n, pl.ds(v, 1), :]

    def cross_copy(sweep):
        mine = plane0.at[y, x] if sweep == 0 else cross.at[x]
        return remote(mine, mine, cross_ssem.at[sweep], cross_rsem.at[sweep], across)

    def cross_arrival(sweep):
        theirs = plane0.at[y, 1 - x] if sweep == 0 else cross.at[1 - x]
        return remote(theirs, theirs, cross_ssem.at[sweep], cross_rsem.at[sweep], across)

    def start_planes():
        mine = plane0.at[y]
        for k in range(1, SY):
            remote(mine, mine, plane_ssem.at[0], plane_rsem.at[0], plane_peer(k)).start()

    def start_rings():
        mine = ring0.at[z]
        for k in range(1, SZ):
            remote(mine, mine, ring_ssem.at[0], ring_rsem.at[0], ring_peer(k)).start()

    def start_layer():
        mine = plane1.at[place]

        def start(k, carry):
            other = k + (k >= place).astype(jnp.int32)
            remote(mine, mine, layer_ssem.at[0], layer_rsem.at[0], (inst, x * LAYER + other)).start()
            return carry

        lax.fori_loop(0, LAYER - 1, start, 0)

    def start_columns(sweep):
        mine = plane0.at[y, x] if sweep == 0 else plane1.at[place]
        for k, device in enumerate((sibling, partner, diagonal)):
            into = (columns0, columns1)[sweep].at[k]
            remote(mine, into, column_ssem.at[sweep], column_rsem.at[sweep], device).start()

    def to_lane(tiles, c, total):
        for v, tile in enumerate(tiles):
            q = c * CHUNK + v
            total = jnp.where(lane == q, pltpu.roll(tile, (q + 1) if c == 0 else q, axis=1), total)
        return total

    def corner_rows(n, g):
        return pl.ds(pl.multiple_of(n * ROWS + g * CHUNK, CHUNK), CHUNK)

    def gather(g):
        here = pl.ds(pl.multiple_of(g * CHUNK, CHUNK), CHUNK)
        for n in range(2):
            total = jnp.zeros((CHUNK, LANES), jnp.float32)
            for c in range(2):
                at = pl.ds(c * LANES, LANES)
                total = to_lane([flow0[n, v, rows_at(g), at] for v in range(NV)] + [step[here, at]], c, total)
            corner[corner_rows(n, g), :] = total

    def turn_first():
        turned = corner[...].T
        for c in range(2):
            plane0[y, x, c] = turned[c * CHUNK : c * CHUNK + NV, :]
            pace_lanes[c] = turned[c * CHUNK + NV : c * CHUNK + NV + 1, :]

    def turn_border():
        turned = corner[...].T
        for c in range(2):
            before[c] = turned[c * CHUNK : c * CHUNK + NV, :]

    def donor(c, n):
        return (stator_donor if c == 0 else rotor_donor)[n, 0]

    def halves(first, second, n):
        if n == 0:
            return jnp.where(low, first, pltpu.roll(second, ROWS, axis=1))
        return jnp.where(low, pltpu.roll(first, ROWS, axis=1), second)

    def forward():
        for c in range(2):
            for n in range(2):
                ahead = (donor(c, n) // ROWS + SPACE - space) % SPACE
                found = []
                for d in (ahead, (ahead + 1) % SPACE):
                    dx, dz, dy = d // LAYER, (d // SY) % SZ, d % SY
                    carry = (y + dy) // SY
                    wants = (z + 2 * SZ - dz - carry) % SZ
                    over = (wants + dz + carry) // SZ
                    found.append(plane0[(y + dy) % SY, (x + dx + over) % SX, c])
                ring0[z, c * 2 + n] = halves(*found, n)

    def from_ring(c, n):
        block = donor(c, n) // ROWS
        here = ring0[(block // SY) % SZ, c * 2 + n]
        there = ring0[((block + 1) // SY) % SZ, c * 2 + n]
        return jnp.where(low, here, there)

    def pass_across():
        for c in range(2):
            for n in range(2):
                block = donor(c, n) // ROWS
                cross[x, c * 2 + n] = halves(plane1[block % LAYER, c], plane1[(block + 1) % LAYER, c], n)

    def from_cross(c, n):
        block = donor(c, n) // ROWS
        here = cross[(block // LAYER) % SX, c * 2 + n]
        there = cross[((block + 1) // LAYER) % SX, c * 2 + n]
        return jnp.where(low, here, there)

    def sum_columns(sweep):
        columns = (columns0, columns1)[sweep]
        sums = []
        for c in range(2):
            total = None
            for k, table in enumerate((from_sib, to_own, to_sib)):
                straight = columns[k, c]
                turned = pltpu.roll(straight, ROWS, axis=1)
                same = jnp.where(low, table[0][0], table[1][1])
                crossed = jnp.where(low, table[0][1], table[1][0])
                term = same * straight + crossed * turned
                total = term if total is None else total + term
            sums.append(total)
        return sums

    def settle(sweep, remote_sum):
        entering = []
        for c in range(2):
            weights = stator_weight if c == 0 else rotor_weight
            values = []
            for n in range(2):
                window = from_ring(c, n) if sweep == 0 else from_cross(c, n)
                offset = donor(c, n) % ROWS
                first = pltpu.roll(window, (LANES - offset) % LANES, axis=1)
                second = pltpu.roll(window, LANES - 1 - offset, axis=1)
                weight = weights[pl.ds(n, 1), :]
                weight = jnp.concatenate([weight, weight], axis=1)
                values.append((1.0 - weight) * first + weight * second)
            entering.append(jnp.where(low, values[0], pltpu.roll(values[1], ROWS, axis=1)))
        stator, rotor = entering
        share_lanes[0] = -VISCOSITY * rotor
        share_lanes[1] = -VISCOSITY * stator
        for v in range(NV):
            total = share_lanes[1, pl.ds(v, 1), :]
            for w in range(NV):
                total = total - jac[v, w] * stator[w : w + 1, :]
            share_lanes[1, pl.ds(v, 1), :] = total
        for c in range(2):
            share_lanes[c] = share_lanes[c] + remote_sum[c]

    def turn_share():
        corner[...] = jnp.zeros_like(corner)
        for t in range(2):
            corner[pl.ds(t * CHUNK, NV), :] = share_lanes[t]
        share_rows[...] = corner[...].T

    def spread(own, other, into):
        for v in range(NV):
            for t in range(2):
                at = pl.ds(t * LANES, LANES)
                ours, theirs = [own(n, v, at) for n in range(2)], [other(n, v, at) for n in range(2)]
                for a in range(2):
                    into[a, v, :, at] = (
                        to_own[a][0] * ours[0] + to_own[a][1] * ours[1]
                        + (to_sib[a][0] * theirs[0] + to_sib[a][1] * theirs[1])
                    )

    def mix(sweep, g):
        flow, sib, send = (flow0, sib0, send0) if sweep == 0 else (flow1, sib1, send1)
        spread(lambda n, v, at: flow[n, v, rows_at(g), at], lambda n, v, at: sib[g, n, v, :, at], send.at[g])

    def mix_raw():
        spread(lambda n, v, at: raw[0, n, v, :, at], lambda n, v, at: raw[1, n, v, :, at], recv0.at[order(0)])

    def inner(flow, g, t):
        here = pl.ds(pl.multiple_of(g * CHUNK, CHUNK), CHUNK)
        jacobian = [[jac[v, w] for w in range(NV)] for v in range(NV)]
        at = pl.ds(t * LANES, LANES)
        centre = [[flow[n, v, rows_at(g), at] for v in range(NV)] for n in range(2)]
        parts = []
        for n in range(2):
            diff, smooth = [], []
            for v in range(NV):
                window = flow[n, v, pl.ds(pl.multiple_of(g * CHUNK, CHUNK), 3 * CHUNK), at]
                upper = window[CHUNK - 1 : 2 * CHUNK - 1]
                lower = window[CHUNK + 1 : 2 * CHUNK + 1]
                f = centre[n][v]
                left = jnp.where(lane == 0, 0.0, pltpu.roll(f, 1, axis=1))
                right = jnp.where(lane == LANES - 1, 0.0, pltpu.roll(f, LANES - 1, axis=1))
                diff.append(f - left)
                smooth.append(VISCOSITY * (4.0 * f - left - right - upper - lower))
            row = []
            for v in range(NV):
                convect = jacobian[v][0] * diff[0]
                for w in range(1, NV):
                    convect = convect + jacobian[v][w] * diff[w]
                derivative = from_own[n][0] * centre[0][v] + from_own[n][1] * centre[1][v]
                row.append(convect + smooth[v] + derivative - source[n, v, here, at])
            parts.append(row)
        return centre, parts

    def border(g):
        here = pl.ds(pl.multiple_of(g * CHUNK, CHUNK), CHUNK)
        totals = [jnp.zeros((CHUNK, LANES), jnp.float32) for _ in range(2)]
        for t in range(2):
            pace = step[here, pl.ds(t * LANES, LANES)]
            centre, parts = inner(flow0, g, t)
            for n in range(2):
                totals[n] = to_lane([centre[n][v] - pace * parts[n][v] for v in range(NV)], t, totals[n])
        for n in range(2):
            corner[corner_rows(n, g), :] = totals[n]

    def advance(sweep, g):
        flow, sib, recv = (flow0, sib0, recv0) if sweep == 0 else (flow1, sib1, recv1)
        here = pl.ds(pl.multiple_of(g * CHUNK, CHUNK), CHUNK)
        for t in range(2):
            at = pl.ds(t * LANES, LANES)
            pace = step[here, at]
            edge = lane == (LANES - 1 if t == 0 else 0)
            centre, parts = inner(flow, g, t)
            for n in range(2):
                for v in range(NV):
                    others = (
                        from_sib[n][0] * sib[g, 0, v, :, at] + from_sib[n][1] * sib[g, 1, v, :, at]
                        + recv[g, n, v, :, at]
                    )
                    residual = parts[n][v] + jnp.where(edge, 0.0, others)
                    new = centre[n][v] - pace * residual
                    if sweep == 0:
                        flow1[n, v, rows_at(g), at] = new
                    else:
                        out_state[n, v, here, at] = new
                        out_resid[n, v, here, at] = residual

    def patch(sweep, g):
        here = pl.ds(pl.multiple_of(g * CHUNK, CHUNK), CHUNK)
        for n in range(2):
            shares = share_rows[corner_rows(n, g), :]
            for t in range(2):
                at = pl.ds(t * LANES, LANES)
                edge = lane == (LANES - 1 if t == 0 else 0)
                pace = step[here, at]
                for v in range(NV):
                    share = jnp.where(edge, pltpu.roll(shares, LANES - 1 - v if t == 0 else LANES - CHUNK - v, axis=1), 0.0)
                    if sweep == 0:
                        flow1[n, v, rows_at(g), at] = flow1[n, v, rows_at(g), at] - pace * share
                    else:
                        out_state[n, v, here, at] = out_state[n, v, here, at] - pace * share
                        out_resid[n, v, here, at] = out_resid[n, v, here, at] + share

    def loop(body, begin=0, end=CHUNKS):
        def wrapped(g, carry):
            body(g)
            return carry

        lax.fori_loop(begin, end, wrapped, 0)

    step_in.wait()
    flow_in.wait()
    loop(gather)
    turn_first()
    pack_halos(0)
    hear(barrier, nearest)
    cross_copy(0).start()
    raw_copy().start()
    loop(lambda p: sib_copy(0, order(p)).start())
    tell(known.at[0], rounds[0])
    start_first_halos()

    def first_mix(p):
        g = order(p)
        sib_copy(0, g).wait_recv()
        mix(0, g)
        par_copy(0, g).start()

    loop(first_mix, 1, FIRST)
    start_columns(0)
    hear(known.at[0], rounds[0])
    tell(known.at[1], rounds[1])
    loop(first_mix, FIRST, CHUNKS)
    for copy in small_in:
        copy.wait()
    source_in.wait()
    cross_arrival(0).wait_recv()
    start_planes()
    hear(known.at[1], rounds[1])
    tell(known.at[2], rounds[2])
    loop(border, 1, CHUNKS - 1)
    raw_copy().wait_recv()
    raw_pass().start()

    def when(places):
        low_z, high_z = places
        return (1 - z // (SZ // 2)) * (low_z - high_z) + high_z

    at_rings, at_halos, at_settle, at_layer = (when(a) for a in (AT_RINGS, AT_HALOS, AT_SETTLE, AT_LAYER))
    ahead = when(AHEAD)

    def second_mix(p):
        g = order(p)
        sib_copy(1, g).wait_recv()
        mix(1, g)

        @pl.when(p < ahead)
        def _():
            par_copy(1, g).start()

    def first_sweep(p):
        g = order(p)

        @pl.when(p == at_rings)
        def _():
            hear(known.at[2], rounds[2])
            pass_halos()
            all_done(plane0.at[pl.ds(0, SY - 1)], plane_rsem.at[0])
            forward()
            start_rings()

        @pl.when(p == at_halos)
        def _():
            unpack_halos(0)
            border(0)
            border(CHUNKS - 1)
            turn_border()

        @pl.when(p == at_settle)
        def _():
            all_done(columns0, column_rsem.at[0])
            remote_sum = sum_columns(0)
            all_done(ring0.at[pl.ds(0, SZ - 1)], ring_rsem.at[0])
            settle(0, remote_sum)
            for c in range(2):
                plane1[place, c] = before[c] - pace_lanes[c] * share_lanes[c]
            start_layer()
            start_columns(1)
            turn_share()

        @pl.when(p == 0)
        def _():
            sib_copy(0, g).wait_recv()
            raw_pass().wait_recv()
            mix_raw()

        @pl.when(p > 0)
        def _():
            par_copy(0, g).wait_recv()

        advance(0, g)
        sib_copy(1, g).start()

        @pl.when(p > 0)
        def _():
            second_mix(p - 1)

    loop(first_sweep)
    second_mix(CHUNKS - 1)
    all_done(sib1, sib_ssem.at[1])
    loop(lambda g: patch(0, g))
    pack_halos(1)
    start_halos(1)

    def second_sweep(p):
        g = order(p)

        @pl.when(p == at_layer)
        def _():
            all_done(plane1.at[pl.ds(0, LAYER - 1)], layer_rsem.at[0])
            pass_across()
            cross_copy(1).start()

        @pl.when(p == CHUNKS - 1)
        def _():
            all_done(columns1, column_rsem.at[1])
            remote_sum = sum_columns(1)
            cross_arrival(1).wait_recv()
            settle(1, remote_sum)
            turn_share()
            loop(lambda g: patch(1, g), 1, CHUNKS)

        @pl.when(p == AT_SECOND_HALOS)
        def _():
            unpack_halos(1)

        par_copy(1, g).wait_recv()

        @pl.when(jnp.logical_and(p + PACE >= ahead, p + PACE < CHUNKS))
        def _():
            par_copy(1, order(p + PACE)).start()

        advance(1, g)

    loop(second_sweep)
    patch(1, 0)

    all_done(sib0, sib_ssem.at[0])
    all_done(send0.at[pl.ds(0, CHUNKS - 1)], par_ssem.at[0])
    raw_copy().wait_send()
    raw_pass().wait_send()
    all_done(send1, par_ssem.at[1])
    all_done(columns0, column_ssem.at[0])
    all_done(columns1, column_ssem.at[1])
    all_done(plane0.at[pl.ds(0, SY - 1)], plane_ssem.at[0])
    all_done(ring0.at[pl.ds(0, SZ - 1)], ring_ssem.at[0])
    all_done(plane1.at[pl.ds(0, LAYER - 1)], layer_ssem.at[0])
    for sweep in range(2):
        cross_copy(sweep).wait_send()
        all_done(halos_out[sweep], halo_ssem.at[sweep])

    @pl.when(jnp.logical_or(first_in_ring, last_in_ring))
    def _():
        all_done(relay, halo_ssem.at[0])


def store(state, resid, state_hbm, resid_hbm, sems):
    copies = [
        pltpu.make_async_copy(state, state_hbm, sems.at[0]),
        pltpu.make_async_copy(resid, resid_hbm, sems.at[1]),
    ]
    for copy in copies:
        copy.start()
    for copy in copies:
        copy.wait()


def local(flow_state, flow_source, pseudo_step, flux_jacobian, stator_donor, stator_weight, rotor_donor, rotor_weight):
    f32 = jnp.float32
    block = (2, NV, ROWS, AX)
    padded = (2, NV, ROWS + 2 * CHUNK, AX)
    chunked = (CHUNKS, 2, NV, CHUNK, AX)
    anywhere = pl.BlockSpec(memory_space=pltpu.HBM)
    vmem = pl.BlockSpec(memory_space=pltpu.VMEM)
    dma = pltpu.SemaphoreType.DMA
    regular = pltpu.SemaphoreType.REGULAR
    halo = (2, 2, NV, AX)
    args = (
        flow_state, flow_source, pseudo_step, flux_jacobian, stator_donor, stator_weight, rotor_donor, rotor_weight
    )
    state, resid = pl.pallas_call(
        kernel,
        out_shape=(pltpu.VMEM(block, f32), pltpu.VMEM(block, f32)),
        in_specs=[anywhere] * 8,
        out_specs=(vmem, vmem),
        scratch_shapes=[
            pltpu.SMEM((NV, NV), f32),
            pltpu.SMEM((2, ROWS), jnp.int32),
            pltpu.VMEM((2, ROWS), f32),
            pltpu.SMEM((2, ROWS), jnp.int32),
            pltpu.VMEM((2, ROWS), f32),
            pltpu.VMEM(padded, f32),
            pltpu.VMEM(padded, f32),
            pltpu.VMEM(block, f32),
            pltpu.VMEM((ROWS, AX), f32),
            *[pltpu.VMEM(chunked, f32) for _ in range(6)],
            pltpu.VMEM((LANES, LANES), f32),
            pltpu.VMEM((SY, SX, 2, NV, LANES), f32),
            pltpu.VMEM((SZ * SY, 2, NV, LANES), f32),
            pltpu.VMEM((SZ, 4, NV, LANES), f32),
            pltpu.VMEM((SX, 4, NV, LANES), f32),
            *[pltpu.VMEM((3, 2, NV, LANES), f32) for _ in range(2)],
            pltpu.VMEM((2, NV, LANES), f32),
            pltpu.VMEM((2, 1, LANES), f32),
            pltpu.VMEM((2, NV, LANES), f32),
            pltpu.VMEM((LANES, LANES), f32),
            *[pltpu.VMEM(halo, f32) for _ in range(4)],
            pltpu.VMEM(halo[1:], f32),
            dma((1,)),
            pltpu.VMEM((2, *chunked[1:]), f32),
            dma((2,)),
            dma((2,)),
            regular((3,)),
            dma((8,)),
            dma((2,)),
            dma((2 * CHUNKS,)),
            dma((2,)),
            dma((2 * CHUNKS,)),
            dma((2,)),
            dma((2,)),
            *[dma((1,)) for _ in range(6)],
            dma((2,)),
            dma((2,)),
            dma((2,)),
            dma((2,)),
        ],
        compiler_params=pltpu.CompilerParams(
            collective_id=0, has_side_effects=True, vmem_limit_bytes=24 * 2**20
        ),
    )(*[pltpu.with_memory_space_constraint(arg, pltpu.HBM) for arg in args])
    return pl.pallas_call(
        store,
        out_shape=(pltpu.HBM(block, f32), pltpu.HBM(block, f32)),
        in_specs=[vmem, vmem],
        out_specs=(anywhere, anywhere),
        scratch_shapes=[dma((2,))],
    )(
        pltpu.with_memory_space_constraint(state, pltpu.VMEM), pltpu.with_memory_space_constraint(resid, pltpu.VMEM)
    )


def solution(mesh):
    return jax.shard_map(
        local,
        mesh=mesh,
        in_specs=(
            P("inst", None, "space", None),
            P("inst", None, "space", None),
            P("space", None),
            P(),
            P("inst", "space"),
            P("inst", "space"),
            P("inst", "space"),
            P("inst", "space"),
        ),
        out_specs=(P("inst", None, "space", None), P("inst", None, "space", None)),
        check_vma=False,
    )
```

```python
import math

import jax
import jax.numpy as jnp
from jax import lax
from jax.experimental import pallas as pl
from jax.experimental.pallas import tpu as pltpu
from jax.sharding import PartitionSpec as P

MESH = pl.DeviceIdType.MESH
NT = 8
NV = 5
ROWS = 64
AX = 256
LANES = 128
CHUNK = 8
CHUNKS = ROWS // CHUNK
SX, SZ, SY = 2, 8, 4
SPACE = SX * SZ * SY
LAYER = SZ * SY
VISCOSITY = 0.5
AT_RINGS, AT_HALOS, AT_SETTLE = (3, 1), (5, 3), (6, 5)
AT_LAYER, AT_SECOND_HALOS = (4, 3), 6
AHEAD, PACE = (5, 4), 2
FIRST = 2


def spectral(gap):
    gap = gap % NT
    if gap == 0:
        return 0.0
    return 0.5 * (-1.0) ** gap * math.cos(math.pi * gap / NT) / math.sin(math.pi * gap / NT)


def kernel(
    flow_hbm, source_hbm, step_hbm, *rest,
):
    *small_hbm, out_state, out_resid = rest[:7]
    body(flow_hbm, source_hbm, step_hbm, small_hbm, out_state, out_resid, *rest[7:])


def body(
    flow_hbm, source_hbm, step_hbm, small_hbm, out_state, out_resid,
    jac, stator_donor, stator_weight, rotor_donor, rotor_weight,
    flow0, flow1, source, step, sib0, sib1, send0, send1, recv0, recv1,
    corner, plane0, plane1, ring0, cross, columns0, columns1, before, pace_lanes, share_lanes, share_rows,
    halo_out0, halo_out1, halo_in0, halo_in1, relay, relay_sem, raw, raw_ssem, raw_rsem,
    known, load_sem, sib_ssem, sib_rsem, par_ssem, par_rsem, halo_ssem, halo_rsem,
    plane_ssem, plane_rsem, ring_ssem, ring_rsem, layer_ssem, layer_rsem, cross_ssem, cross_rsem, column_ssem, column_rsem,
):
    inst, space = lax.axis_index("inst"), lax.axis_index("space")
    pair, core = inst // 2, inst % 2
    x, z, y = space // (SZ * SY), (space // SY) % SZ, space % SY
    sibling = (pair * 2 + 1 - core, space)
    partner = ((1 - pair) * 2 + core, space)
    diagonal = ((1 - pair) * 2 + 1 - core, space)
    across = (inst, (space + SPACE // 2) % SPACE)
    above = (inst, (space + SPACE - 1) % SPACE)
    below = (inst, (space + 1) % SPACE)
    place = space % LAYER

    def plane_peer(k):
        return inst, x * LAYER + z * SY + (y + k) % SY

    def ring_peer(k):
        return inst, x * LAYER + ((z + k) % SZ) * SY + y

    flow_in = pltpu.make_async_copy(flow_hbm, flow0.at[:, :, pl.ds(CHUNK, ROWS), :], load_sem.at[0])
    source_in = pltpu.make_async_copy(source_hbm, source, load_sem.at[1])
    step_in = pltpu.make_async_copy(step_hbm, step, load_sem.at[2])
    flow_in.start()
    source_in.start()
    step_in.start()
    small = (jac, stator_donor, stator_weight, rotor_donor, rotor_weight)
    small_in = [
        pltpu.make_async_copy(src, dst, load_sem.at[3 + k]) for k, (src, dst) in enumerate(zip(small_hbm, small))
    ]
    for copy in small_in:
        copy.start()

    def on_line(k):
        return [(z >= k, (inst, space - k * SY)), (z < SZ - k, (inst, space + k * SY))]

    always = space >= 0
    nearest = [(always, sibling), (always, partner), (always, across)]
    nearest += [(always, plane_peer(k)) for k in range(1, SY)] + on_line(1)

    def tell(semaphore, devices):
        for exists, device in devices:

            @pl.when(exists)
            def _(device=device):
                pl.semaphore_signal(semaphore, inc=1, device_id=device, device_id_type=MESH)

    def hear(semaphore, devices):
        count = 0
        for exists, _ in devices:
            count = count + exists.astype(jnp.int32)
        pl.semaphore_wait(semaphore, count)

    rounds = [on_line(1), on_line(2), on_line(4)]
    barrier = pltpu.get_barrier_semaphore()
    tell(barrier, nearest)

    lane = lax.broadcasted_iota(jnp.int32, (CHUNK, LANES), 1)
    low = lax.broadcasted_iota(jnp.int32, (NV, LANES), 1) < ROWS

    def scalars(table):
        return [[table(a - b) for b in range(2)] for a in range(2)]

    from_own = scalars(spectral)
    from_sib = scalars(lambda g: jnp.where(core == 0, spectral(g - 2), spectral(g + 2)).astype(jnp.float32))
    to_own = scalars(lambda g: spectral(g + 4))
    to_sib = scalars(lambda g: jnp.where(core == 0, spectral(g + 2), spectral(g + 6)).astype(jnp.float32))

    def remote(src, dst, ssem, rsem, device):
        return pltpu.make_async_remote_copy(
            src_ref=src, dst_ref=dst, send_sem=ssem, recv_sem=rsem, device_id=device, device_id_type=MESH
        )

    def rows_at(g):
        return pl.ds(pl.multiple_of(CHUNK + g * CHUNK, CHUNK), CHUNK)

    def order(p):
        return (p + 1) % CHUNKS

    def all_done(ref, semaphore):
        pltpu.make_async_copy(ref, ref, semaphore).wait()

    def sib_copy(sweep, g):
        flow, sib = (flow0, sib0) if sweep == 0 else (flow1, sib1)
        at = sweep * CHUNKS + g
        return remote(flow.at[:, :, rows_at(g), :], sib.at[g], sib_ssem.at[sweep], sib_rsem.at[at], sibling)

    def par_copy(sweep, g):
        send, recv = (send0, recv0) if sweep == 0 else (send1, recv1)
        at = sweep * CHUNKS + g
        return remote(send.at[g], recv.at[g], par_ssem.at[sweep], par_rsem.at[at], partner)

    def raw_copy():
        mine = flow0.at[:, :, rows_at(order(0)), :]
        return remote(mine, raw.at[0], raw_ssem.at[0], raw_rsem.at[0], partner)

    def raw_pass():
        return remote(raw.at[0], raw.at[1], raw_ssem.at[1], raw_rsem.at[1], sibling)

    halos_out, halos_in = (halo_out0, halo_out1), (halo_in0, halo_in1)

    def send_row(sweep, row, into, device):
        remote(row, into, halo_ssem.at[sweep], halo_rsem.at[sweep], device).start()

    def start_halos(sweep):
        send_row(sweep, halos_out[sweep].at[0], halos_in[sweep].at[1], above)
        send_row(sweep, halos_out[sweep].at[1], halos_in[sweep].at[0], below)

    first_in_ring, last_in_ring = y == 0, y == SY - 1

    def start_first_halos():
        for side, stays, device in ((0, y > 0, above), (1, y < SY - 1, below)):

            @pl.when(stays)
            def _(side=side, device=device):
                send_row(0, halo_out0.at[side], halo_in0.at[1 - side], device)

            @pl.when(jnp.logical_not(stays))
            def _(side=side):
                other_end = plane_peer(SY - 1 if side == 0 else 1)
                remote(halo_out0.at[side], relay, halo_ssem.at[0], relay_sem.at[0], other_end).start()

    def pass_halos():
        for here, side, device in (
            (last_in_ring, 0, (inst, (space + SPACE - SY) % SPACE)),
            (first_in_ring, 1, (inst, (space + SY) % SPACE)),
        ):

            @pl.when(here)
            def _(side=side, device=device):
                all_done(relay, relay_sem.at[0])
                send_row(0, relay, halo_in0.at[1 - side], device)

    def pack_halos(sweep):
        flow, out = (flow0 if sweep == 0 else flow1), halos_out[sweep]
        for side, row in enumerate((CHUNK, CHUNK + ROWS - 1)):
            for n in range(2):
                for v in range(NV):
                    out[side, n, pl.ds(v, 1), :] = flow[n, v, pl.ds(row, 1), :]

    def unpack_halos(sweep):
        flow, into = (flow0 if sweep == 0 else flow1), halos_in[sweep]
        all_done(into, halo_rsem.at[sweep])
        for side, row in enumerate((CHUNK - 1, CHUNK + ROWS)):
            for n in range(2):
                for v in range(NV):
                    flow[n, v, pl.ds(row, 1), :] = into[side, n, pl.ds(v, 1), :]

    def cross_copy(sweep):
        mine = plane0.at[y, x] if sweep == 0 else cross.at[x]
        return remote(mine, mine, cross_ssem.at[sweep], cross_rsem.at[sweep], across)

    def cross_arrival(sweep):
        theirs = plane0.at[y, 1 - x] if sweep == 0 else cross.at[1 - x]
        return remote(theirs, theirs, cross_ssem.at[sweep], cross_rsem.at[sweep], across)

    def start_planes():
        mine = plane0.at[y]
        for k in range(1, SY):
            remote(mine, mine, plane_ssem.at[0], plane_rsem.at[0], plane_peer(k)).start()

    def start_rings():
        mine = ring0.at[z]
        for k in range(1, SZ):
            remote(mine, mine, ring_ssem.at[0], ring_rsem.at[0], ring_peer(k)).start()

    def start_layer():
        mine = plane1.at[place]

        def start(k, carry):
            other = k + (k >= place).astype(jnp.int32)
            remote(mine, mine, layer_ssem.at[0], layer_rsem.at[0], (inst, x * LAYER + other)).start()
            return carry

        lax.fori_loop(0, LAYER - 1, start, 0)

    def start_columns(sweep):
        mine = plane0.at[y, x] if sweep == 0 else plane1.at[place]
        for k, device in enumerate((sibling, partner, diagonal)):
            into = (columns0, columns1)[sweep].at[k]
            remote(mine, into, column_ssem.at[sweep], column_rsem.at[sweep], device).start()

    def to_lane(tiles, c, total):
        for v, tile in enumerate(tiles):
            q = c * CHUNK + v
            total = jnp.where(lane == q, pltpu.roll(tile, (q + 1) if c == 0 else q, axis=1), total)
        return total

    def corner_rows(n, g):
        return pl.ds(pl.multiple_of(n * ROWS + g * CHUNK, CHUNK), CHUNK)

    def gather(g):
        here = pl.ds(pl.multiple_of(g * CHUNK, CHUNK), CHUNK)
        for n in range(2):
            total = jnp.zeros((CHUNK, LANES), jnp.float32)
            for c in range(2):
                at = pl.ds(c * LANES, LANES)
                total = to_lane([flow0[n, v, rows_at(g), at] for v in range(NV)] + [step[here, at]], c, total)
            corner[corner_rows(n, g), :] = total

    def turn_first():
        turned = corner[...].T
        for c in range(2):
            plane0[y, x, c] = turned[c * CHUNK : c * CHUNK + NV, :]
            pace_lanes[c] = turned[c * CHUNK + NV : c * CHUNK + NV + 1, :]

    def turn_border():
        turned = corner[...].T
        for c in range(2):
            before[c] = turned[c * CHUNK : c * CHUNK + NV, :]

    def donor(c, n):
        return (stator_donor if c == 0 else rotor_donor)[n, 0]

    def halves(first, second, n):
        if n == 0:
            return jnp.where(low, first, pltpu.roll(second, ROWS, axis=1))
        return jnp.where(low, pltpu.roll(first, ROWS, axis=1), second)

    def forward():
        for c in range(2):
            for n in range(2):
                ahead = (donor(c, n) // ROWS + SPACE - space) % SPACE
                found = []
                for d in (ahead, (ahead + 1) % SPACE):
                    dx, dz, dy = d // LAYER, (d // SY) % SZ, d % SY
                    carry = (y + dy) // SY
                    wants = (z + 2 * SZ - dz - carry) % SZ
                    over = (wants + dz + carry) // SZ
                    found.append(plane0[(y + dy) % SY, (x + dx + over) % SX, c])
                ring0[z, c * 2 + n] = halves(*found, n)

    def from_ring(c, n):
        block = donor(c, n) // ROWS
        here = ring0[(block // SY) % SZ, c * 2 + n]
        there = ring0[((block + 1) // SY) % SZ, c * 2 + n]
        return jnp.where(low, here, there)

    def pass_across():
        for c in range(2):
            for n in range(2):
                block = donor(c, n) // ROWS
                cross[x, c * 2 + n] = halves(plane1[block % LAYER, c], plane1[(block + 1) % LAYER, c], n)

    def from_cross(c, n):
        block = donor(c, n) // ROWS
        here = cross[(block // LAYER) % SX, c * 2 + n]
        there = cross[((block + 1) // LAYER) % SX, c * 2 + n]
        return jnp.where(low, here, there)

    def sum_columns(sweep):
        columns = (columns0, columns1)[sweep]
        sums = []
        for c in range(2):
            total = None
            for k, table in enumerate((from_sib, to_own, to_sib)):
                straight = columns[k, c]
                turned = pltpu.roll(straight, ROWS, axis=1)
                same = jnp.where(low, table[0][0], table[1][1])
                crossed = jnp.where(low, table[0][1], table[1][0])
                term = same * straight + crossed * turned
                total = term if total is None else total + term
            sums.append(total)
        return sums

    def settle(sweep, remote_sum):
        entering = []
        for c in range(2):
            weights = stator_weight if c == 0 else rotor_weight
            values = []
            for n in range(2):
                window = from_ring(c, n) if sweep == 0 else from_cross(c, n)
                offset = donor(c, n) % ROWS
                first = pltpu.roll(window, (LANES - offset) % LANES, axis=1)
                second = pltpu.roll(window, LANES - 1 - offset, axis=1)
                weight = weights[pl.ds(n, 1), :]
                weight = jnp.concatenate([weight, weight], axis=1)
                values.append((1.0 - weight) * first + weight * second)
            entering.append(jnp.where(low, values[0], pltpu.roll(values[1], ROWS, axis=1)))
        stator, rotor = entering
        share_lanes[0] = -VISCOSITY * rotor
        share_lanes[1] = -VISCOSITY * stator
        for v in range(NV):
            total = share_lanes[1, pl.ds(v, 1), :]
            for w in range(NV):
                total = total - jac[v, w] * stator[w : w + 1, :]
            share_lanes[1, pl.ds(v, 1), :] = total
        for c in range(2):
            share_lanes[c] = share_lanes[c] + remote_sum[c]

    def turn_share():
        corner[...] = jnp.zeros_like(corner)
        for t in range(2):
            corner[pl.ds(t * CHUNK, NV), :] = share_lanes[t]
        share_rows[...] = corner[...].T

    def spread(own, other, into):
        for v in range(NV):
            for t in range(2):
                at = pl.ds(t * LANES, LANES)
                ours, theirs = [own(n, v, at) for n in range(2)], [other(n, v, at) for n in range(2)]
                for a in range(2):
                    into[a, v, :, at] = (
                        to_own[a][0] * ours[0] + to_own[a][1] * ours[1]
                        + (to_sib[a][0] * theirs[0] + to_sib[a][1] * theirs[1])
                    )

    def mix(sweep, g):
        flow, sib, send = (flow0, sib0, send0) if sweep == 0 else (flow1, sib1, send1)
        spread(lambda n, v, at: flow[n, v, rows_at(g), at], lambda n, v, at: sib[g, n, v, :, at], send.at[g])

    def mix_raw():
        spread(lambda n, v, at: raw[0, n, v, :, at], lambda n, v, at: raw[1, n, v, :, at], recv0.at[order(0)])

    def inner(flow, g, t):
        here = pl.ds(pl.multiple_of(g * CHUNK, CHUNK), CHUNK)
        jacobian = [[jac[v, w] for w in range(NV)] for v in range(NV)]
        at = pl.ds(t * LANES, LANES)
        centre = [[flow[n, v, rows_at(g), at] for v in range(NV)] for n in range(2)]
        parts = []
        for n in range(2):
            diff, smooth = [], []
            for v in range(NV):
                window = flow[n, v, pl.ds(pl.multiple_of(g * CHUNK, CHUNK), 3 * CHUNK), at]
                upper = window[CHUNK - 1 : 2 * CHUNK - 1]
                lower = window[CHUNK + 1 : 2 * CHUNK + 1]
                f = centre[n][v]
                left = jnp.where(lane == 0, 0.0, pltpu.roll(f, 1, axis=1))
                right = jnp.where(lane == LANES - 1, 0.0, pltpu.roll(f, LANES - 1, axis=1))
                diff.append(f - left)
                smooth.append(VISCOSITY * (4.0 * f - left - right - upper - lower))
            row = []
            for v in range(NV):
                convect = jacobian[v][0] * diff[0]
                for w in range(1, NV):
                    convect = convect + jacobian[v][w] * diff[w]
                derivative = from_own[n][0] * centre[0][v] + from_own[n][1] * centre[1][v]
                row.append(convect + smooth[v] + derivative - source[n, v, here, at])
            parts.append(row)
        return centre, parts

    def border(g):
        here = pl.ds(pl.multiple_of(g * CHUNK, CHUNK), CHUNK)
        totals = [jnp.zeros((CHUNK, LANES), jnp.float32) for _ in range(2)]
        for t in range(2):
            pace = step[here, pl.ds(t * LANES, LANES)]
            centre, parts = inner(flow0, g, t)
            for n in range(2):
                totals[n] = to_lane([centre[n][v] - pace * parts[n][v] for v in range(NV)], t, totals[n])
        for n in range(2):
            corner[corner_rows(n, g), :] = totals[n]

    def advance(sweep, g):
        flow, sib, recv = (flow0, sib0, recv0) if sweep == 0 else (flow1, sib1, recv1)
        here = pl.ds(pl.multiple_of(g * CHUNK, CHUNK), CHUNK)
        for t in range(2):
            at = pl.ds(t * LANES, LANES)
            pace = step[here, at]
            edge = lane == (LANES - 1 if t == 0 else 0)
            centre, parts = inner(flow, g, t)
            for n in range(2):
                for v in range(NV):
                    others = (
                        from_sib[n][0] * sib[g, 0, v, :, at] + from_sib[n][1] * sib[g, 1, v, :, at]
                        + recv[g, n, v, :, at]
                    )
                    residual = parts[n][v] + jnp.where(edge, 0.0, others)
                    new = centre[n][v] - pace * residual
                    if sweep == 0:
                        flow1[n, v, rows_at(g), at] = new
                    else:
                        out_state[n, v, here, at] = new
                        out_resid[n, v, here, at] = residual

    def patch(sweep, g):
        here = pl.ds(pl.multiple_of(g * CHUNK, CHUNK), CHUNK)
        for n in range(2):
            shares = share_rows[corner_rows(n, g), :]
            for t in range(2):
                at = pl.ds(t * LANES, LANES)
                edge = lane == (LANES - 1 if t == 0 else 0)
                pace = step[here, at]
                for v in range(NV):
                    share = jnp.where(edge, pltpu.roll(shares, LANES - 1 - v if t == 0 else LANES - CHUNK - v, axis=1), 0.0)
                    if sweep == 0:
                        flow1[n, v, rows_at(g), at] = flow1[n, v, rows_at(g), at] - pace * share
                    else:
                        out_state[n, v, here, at] = out_state[n, v, here, at] - pace * share
                        out_resid[n, v, here, at] = out_resid[n, v, here, at] + share

    def loop(body, begin=0, end=CHUNKS):
        def wrapped(g, carry):
            body(g)
            return carry

        lax.fori_loop(begin, end, wrapped, 0)

    step_in.wait()
    flow_in.wait()
    loop(gather)
    turn_first()
    pack_halos(0)
    hear(barrier, nearest)
    cross_copy(0).start()
    raw_copy().start()
    loop(lambda p: sib_copy(0, order(p)).start())
    tell(known.at[0], rounds[0])
    start_first_halos()

    def first_mix(p):
        g = order(p)
        sib_copy(0, g).wait_recv()
        mix(0, g)
        par_copy(0, g).start()

    loop(first_mix, 1, FIRST)
    start_columns(0)
    hear(known.at[0], rounds[0])
    tell(known.at[1], rounds[1])
    loop(first_mix, FIRST, CHUNKS)
    for copy in small_in:
        copy.wait()
    source_in.wait()
    cross_arrival(0).wait_recv()
    start_planes()
    hear(known.at[1], rounds[1])
    tell(known.at[2], rounds[2])
    loop(border, 1, CHUNKS - 1)
    raw_copy().wait_recv()
    raw_pass().start()

    def when(places):
        low_z, high_z = places
        return (1 - z // (SZ // 2)) * (low_z - high_z) + high_z

    at_rings, at_halos, at_settle, at_layer = (when(a) for a in (AT_RINGS, AT_HALOS, AT_SETTLE, AT_LAYER))
    ahead = when(AHEAD)

    def second_mix(p):
        g = order(p)
        sib_copy(1, g).wait_recv()
        mix(1, g)

        @pl.when(p < ahead)
        def _():
            par_copy(1, g).start()

    def first_sweep(p):
        g = order(p)

        @pl.when(p == at_rings)
        def _():
            hear(known.at[2], rounds[2])
            pass_halos()
            all_done(plane0.at[pl.ds(0, SY - 1)], plane_rsem.at[0])
            forward()
            start_rings()

        @pl.when(p == at_halos)
        def _():
            unpack_halos(0)
            border(0)
            border(CHUNKS - 1)
            turn_border()

        @pl.when(p == at_settle)
        def _():
            all_done(columns0, column_rsem.at[0])
            remote_sum = sum_columns(0)
            all_done(ring0.at[pl.ds(0, SZ - 1)], ring_rsem.at[0])
            settle(0, remote_sum)
            for c in range(2):
                plane1[place, c] = before[c] - pace_lanes[c] * share_lanes[c]
            start_layer()
            start_columns(1)
            turn_share()

        @pl.when(p == 0)
        def _():
            sib_copy(0, g).wait_recv()
            raw_pass().wait_recv()
            mix_raw()

        @pl.when(p > 0)
        def _():
            par_copy(0, g).wait_recv()

        advance(0, g)
        sib_copy(1, g).start()

        @pl.when(p > 0)
        def _():
            second_mix(p - 1)

    loop(first_sweep)
    second_mix(CHUNKS - 1)
    all_done(sib1, sib_ssem.at[1])
    loop(lambda g: patch(0, g))
    pack_halos(1)
    start_halos(1)

    def second_sweep(p):
        g = order(p)

        @pl.when(p == at_layer)
        def _():
            all_done(plane1.at[pl.ds(0, LAYER - 1)], layer_rsem.at[0])
            pass_across()
            cross_copy(1).start()

        @pl.when(p == CHUNKS - 1)
        def _():
            all_done(columns1, column_rsem.at[1])
            remote_sum = sum_columns(1)
            cross_arrival(1).wait_recv()
            settle(1, remote_sum)
            turn_share()
            loop(lambda g: patch(1, g), 1, CHUNKS)

        @pl.when(p == AT_SECOND_HALOS)
        def _():
            unpack_halos(1)

        par_copy(1, g).wait_recv()

        @pl.when(jnp.logical_and(p + PACE >= ahead, p + PACE < CHUNKS))
        def _():
            par_copy(1, order(p + PACE)).start()

        advance(1, g)

    loop(second_sweep)
    patch(1, 0)

    all_done(sib0, sib_ssem.at[0])
    all_done(send0.at[pl.ds(0, CHUNKS - 1)], par_ssem.at[0])
    raw_copy().wait_send()
    raw_pass().wait_send()
    all_done(send1, par_ssem.at[1])
    all_done(columns0, column_ssem.at[0])
    all_done(columns1, column_ssem.at[1])
    all_done(plane0.at[pl.ds(0, SY - 1)], plane_ssem.at[0])
    all_done(ring0.at[pl.ds(0, SZ - 1)], ring_ssem.at[0])
    all_done(plane1.at[pl.ds(0, LAYER - 1)], layer_ssem.at[0])
    for sweep in range(2):
        cross_copy(sweep).wait_send()
        all_done(halos_out[sweep], halo_ssem.at[sweep])

    @pl.when(jnp.logical_or(first_in_ring, last_in_ring))
    def _():
        all_done(relay, halo_ssem.at[0])


def store(state, resid, state_hbm, resid_hbm, sems):
    copies = [
        pltpu.make_async_copy(state, state_hbm, sems.at[0]),
        pltpu.make_async_copy(resid, resid_hbm, sems.at[1]),
    ]
    for copy in copies:
        copy.start()
    for copy in copies:
        copy.wait()


def local(flow_state, flow_source, pseudo_step, flux_jacobian, stator_donor, stator_weight, rotor_donor, rotor_weight):
    f32 = jnp.float32
    block = (2, NV, ROWS, AX)
    padded = (2, NV, ROWS + 2 * CHUNK, AX)
    chunked = (CHUNKS, 2, NV, CHUNK, AX)
    anywhere = pl.BlockSpec(memory_space=pltpu.HBM)
    vmem = pl.BlockSpec(memory_space=pltpu.VMEM)
    dma = pltpu.SemaphoreType.DMA
    regular = pltpu.SemaphoreType.REGULAR
    halo = (2, 2, NV, AX)
    args = (
        flow_state, flow_source, pseudo_step, flux_jacobian, stator_donor, stator_weight, rotor_donor, rotor_weight
    )
    state, resid = pl.pallas_call(
        kernel,
        out_shape=(pltpu.VMEM(block, f32), pltpu.VMEM(block, f32)),
        in_specs=[anywhere] * 8,
        out_specs=(vmem, vmem),
        scratch_shapes=[
            pltpu.SMEM((NV, NV), f32),
            pltpu.SMEM((2, ROWS), jnp.int32),
            pltpu.VMEM((2, ROWS), f32),
            pltpu.SMEM((2, ROWS), jnp.int32),
            pltpu.VMEM((2, ROWS), f32),
            pltpu.VMEM(padded, f32),
            pltpu.VMEM(padded, f32),
            pltpu.VMEM(block, f32),
            pltpu.VMEM((ROWS, AX), f32),
            *[pltpu.VMEM(chunked, f32) for _ in range(6)],
            pltpu.VMEM((LANES, LANES), f32),
            pltpu.VMEM((SY, SX, 2, NV, LANES), f32),
            pltpu.VMEM((SZ * SY, 2, NV, LANES), f32),
            pltpu.VMEM((SZ, 4, NV, LANES), f32),
            pltpu.VMEM((SX, 4, NV, LANES), f32),
            *[pltpu.VMEM((3, 2, NV, LANES), f32) for _ in range(2)],
            pltpu.VMEM((2, NV, LANES), f32),
            pltpu.VMEM((2, 1, LANES), f32),
            pltpu.VMEM((2, NV, LANES), f32),
            pltpu.VMEM((LANES, LANES), f32),
            *[pltpu.VMEM(halo, f32) for _ in range(4)],
            pltpu.VMEM(halo[1:], f32),
            dma((1,)),
            pltpu.VMEM((2, *chunked[1:]), f32),
            dma((2,)),
            dma((2,)),
            regular((3,)),
            dma((8,)),
            dma((2,)),
            dma((2 * CHUNKS,)),
            dma((2,)),
            dma((2 * CHUNKS,)),
            dma((2,)),
            dma((2,)),
            *[dma((1,)) for _ in range(6)],
            dma((2,)),
            dma((2,)),
            dma((2,)),
            dma((2,)),
        ],
        compiler_params=pltpu.CompilerParams(
            collective_id=0, has_side_effects=True, vmem_limit_bytes=24 * 2**20
        ),
    )(*[pltpu.with_memory_space_constraint(arg, pltpu.HBM) for arg in args])
    return pl.pallas_call(
        store,
        out_shape=(pltpu.HBM(block, f32), pltpu.HBM(block, f32)),
        in_specs=[vmem, vmem],
        out_specs=(anywhere, anywhere),
        scratch_shapes=[dma((2,))],
    )(
        pltpu.with_memory_space_constraint(state, pltpu.VMEM), pltpu.with_memory_space_constraint(resid, pltpu.VMEM)
    )


def solution(mesh):
    return jax.shard_map(
        local,
        mesh=mesh,
        in_specs=(
            P("inst", None, "space", None),
            P("inst", None, "space", None),
            P("space", None),
            P(),
            P("inst", "space"),
            P("inst", "space"),
            P("inst", "space"),
            P("inst", "space"),
        ),
        out_specs=(P("inst", None, "space", None), P("inst", None, "space", None)),
        check_vma=False,
    )
```

```python
import math

import jax
import jax.numpy as jnp
from jax import lax
from jax.experimental import pallas as pl
from jax.experimental.pallas import tpu as pltpu
from jax.sharding import PartitionSpec as P

MESH = pl.DeviceIdType.MESH
NT = 8
NV = 5
ROWS = 64
AX = 256
LANES = 128
CHUNK = 8
CHUNKS = ROWS // CHUNK
SX, SZ, SY = 2, 8, 4
SPACE = SX * SZ * SY
LAYER = SZ * SY
VISCOSITY = 0.5
AT_RINGS, AT_HALOS, AT_SETTLE = (3, 1), (5, 3), (6, 5)
AT_LAYER, AT_SECOND_HALOS = (4, 3), 6
AHEAD, PACE = (6, 5), 2
FIRST = 4


def spectral(gap):
    gap = gap % NT
    if gap == 0:
        return 0.0
    return 0.5 * (-1.0) ** gap * math.cos(math.pi * gap / NT) / math.sin(math.pi * gap / NT)


def kernel(
    flow_hbm, source_hbm, step_hbm, *rest,
):
    *small_hbm, out_state, out_resid = rest[:7]
    body(flow_hbm, source_hbm, step_hbm, small_hbm, out_state, out_resid, *rest[7:])


def body(
    flow_hbm, source_hbm, step_hbm, small_hbm, out_state, out_resid,
    jac, stator_donor, stator_weight, rotor_donor, rotor_weight,
    flow0, flow1, source, step, sib0, sib1, send0, send1, recv0, recv1,
    corner, plane0, plane1, ring0, cross, columns0, columns1, before, pace_lanes, share_lanes, share_rows,
    halo_out0, halo_out1, halo_in0, halo_in1, relay, relay_sem, raw, raw_ssem, raw_rsem,
    known, load_sem, sib_ssem, sib_rsem, par_ssem, par_rsem, halo_ssem, halo_rsem,
    plane_ssem, plane_rsem, ring_ssem, ring_rsem, layer_ssem, layer_rsem, cross_ssem, cross_rsem, column_ssem, column_rsem,
):
    inst, space = lax.axis_index("inst"), lax.axis_index("space")
    pair, core = inst // 2, inst % 2
    x, z, y = space // (SZ * SY), (space // SY) % SZ, space % SY
    sibling = (pair * 2 + 1 - core, space)
    partner = ((1 - pair) * 2 + core, space)
    diagonal = ((1 - pair) * 2 + 1 - core, space)
    across = (inst, (space + SPACE // 2) % SPACE)
    above = (inst, (space + SPACE - 1) % SPACE)
    below = (inst, (space + 1) % SPACE)
    place = space % LAYER

    def plane_peer(k):
        return inst, x * LAYER + z * SY + (y + k) % SY

    def ring_peer(k):
        return inst, x * LAYER + ((z + k) % SZ) * SY + y

    flow_in = pltpu.make_async_copy(flow_hbm, flow0.at[:, :, pl.ds(CHUNK, ROWS), :], load_sem.at[0])
    source_in = pltpu.make_async_copy(source_hbm, source, load_sem.at[1])
    step_in = pltpu.make_async_copy(step_hbm, step, load_sem.at[2])
    flow_in.start()
    source_in.start()
    step_in.start()
    small = (jac, stator_donor, stator_weight, rotor_donor, rotor_weight)
    small_in = [
        pltpu.make_async_copy(src, dst, load_sem.at[3 + k]) for k, (src, dst) in enumerate(zip(small_hbm, small))
    ]
    for copy in small_in:
        copy.start()

    def on_line(k):
        return [(z >= k, (inst, space - k * SY)), (z < SZ - k, (inst, space + k * SY))]

    always = space >= 0
    nearest = [(always, sibling), (always, partner), (always, across)]
    nearest += [(always, plane_peer(k)) for k in range(1, SY)] + on_line(1)

    def tell(semaphore, devices):
        for exists, device in devices:

            @pl.when(exists)
            def _(device=device):
                pl.semaphore_signal(semaphore, inc=1, device_id=device, device_id_type=MESH)

    def hear(semaphore, devices):
        count = 0
        for exists, _ in devices:
            count = count + exists.astype(jnp.int32)
        pl.semaphore_wait(semaphore, count)

    rounds = [on_line(1), on_line(2), on_line(4)]
    barrier = pltpu.get_barrier_semaphore()
    tell(barrier, nearest)

    lane = lax.broadcasted_iota(jnp.int32, (CHUNK, LANES), 1)
    low = lax.broadcasted_iota(jnp.int32, (NV, LANES), 1) < ROWS

    def scalars(table):
        return [[table(a - b) for b in range(2)] for a in range(2)]

    from_own = scalars(spectral)
    from_sib = scalars(lambda g: jnp.where(core == 0, spectral(g - 2), spectral(g + 2)).astype(jnp.float32))
    to_own = scalars(lambda g: spectral(g + 4))
    to_sib = scalars(lambda g: jnp.where(core == 0, spectral(g + 2), spectral(g + 6)).astype(jnp.float32))

    def remote(src, dst, ssem, rsem, device):
        return pltpu.make_async_remote_copy(
            src_ref=src, dst_ref=dst, send_sem=ssem, recv_sem=rsem, device_id=device, device_id_type=MESH
        )

    def rows_at(g):
        return pl.ds(pl.multiple_of(CHUNK + g * CHUNK, CHUNK), CHUNK)

    def order(p):
        return (p + 1) % CHUNKS

    def all_done(ref, semaphore):
        pltpu.make_async_copy(ref, ref, semaphore).wait()

    def sib_copy(sweep, g):
        flow, sib = (flow0, sib0) if sweep == 0 else (flow1, sib1)
        at = sweep * CHUNKS + g
        return remote(flow.at[:, :, rows_at(g), :], sib.at[g], sib_ssem.at[sweep], sib_rsem.at[at], sibling)

    def par_copy(sweep, g):
        send, recv = (send0, recv0) if sweep == 0 else (send1, recv1)
        at = sweep * CHUNKS + g
        return remote(send.at[g], recv.at[g], par_ssem.at[sweep], par_rsem.at[at], partner)

    def raw_copy():
        mine = flow0.at[:, :, rows_at(order(0)), :]
        return remote(mine, raw.at[0], raw_ssem.at[0], raw_rsem.at[0], partner)

    def raw_pass():
        return remote(raw.at[0], raw.at[1], raw_ssem.at[1], raw_rsem.at[1], sibling)

    halos_out, halos_in = (halo_out0, halo_out1), (halo_in0, halo_in1)

    def send_row(sweep, row, into, device):
        remote(row, into, halo_ssem.at[sweep], halo_rsem.at[sweep], device).start()

    def start_halos(sweep):
        send_row(sweep, halos_out[sweep].at[0], halos_in[sweep].at[1], above)
        send_row(sweep, halos_out[sweep].at[1], halos_in[sweep].at[0], below)

    first_in_ring, last_in_ring = y == 0, y == SY - 1

    def start_first_halos():
        for side, stays, device in ((0, y > 0, above), (1, y < SY - 1, below)):

            @pl.when(stays)
            def _(side=side, device=device):
                send_row(0, halo_out0.at[side], halo_in0.at[1 - side], device)

            @pl.when(jnp.logical_not(stays))
            def _(side=side):
                other_end = plane_peer(SY - 1 if side == 0 else 1)
                remote(halo_out0.at[side], relay, halo_ssem.at[0], relay_sem.at[0], other_end).start()

    def pass_halos():
        for here, side, device in (
            (last_in_ring, 0, (inst, (space + SPACE - SY) % SPACE)),
            (first_in_ring, 1, (inst, (space + SY) % SPACE)),
        ):

            @pl.when(here)
            def _(side=side, device=device):
                all_done(relay, relay_sem.at[0])
                send_row(0, relay, halo_in0.at[1 - side], device)

    def pack_halos(sweep):
        flow, out = (flow0 if sweep == 0 else flow1), halos_out[sweep]
        for side, row in enumerate((CHUNK, CHUNK + ROWS - 1)):
            for n in range(2):
                for v in range(NV):
                    out[side, n, pl.ds(v, 1), :] = flow[n, v, pl.ds(row, 1), :]

    def unpack_halos(sweep):
        flow, into = (flow0 if sweep == 0 else flow1), halos_in[sweep]
        all_done(into, halo_rsem.at[sweep])
        for side, row in enumerate((CHUNK - 1, CHUNK + ROWS)):
            for n in range(2):
                for v in range(NV):
                    flow[n, v, pl.ds(row, 1), :] = into[side, n, pl.ds(v, 1), :]

    def cross_copy(sweep):
        mine = plane0.at[y, x] if sweep == 0 else cross.at[x]
        return remote(mine, mine, cross_ssem.at[sweep], cross_rsem.at[sweep], across)

    def cross_arrival(sweep):
        theirs = plane0.at[y, 1 - x] if sweep == 0 else cross.at[1 - x]
        return remote(theirs, theirs, cross_ssem.at[sweep], cross_rsem.at[sweep], across)

    def start_planes():
        mine = plane0.at[y]
        for k in range(1, SY):
            remote(mine, mine, plane_ssem.at[0], plane_rsem.at[0], plane_peer(k)).start()

    def start_rings():
        mine = ring0.at[z]
        for k in range(1, SZ):
            remote(mine, mine, ring_ssem.at[0], ring_rsem.at[0], ring_peer(k)).start()

    def start_layer():
        mine = plane1.at[place]

        def start(k, carry):
            other = k + (k >= place).astype(jnp.int32)
            remote(mine, mine, layer_ssem.at[0], layer_rsem.at[0], (inst, x * LAYER + other)).start()
            return carry

        lax.fori_loop(0, LAYER - 1, start, 0)

    def start_columns(sweep):
        mine = plane0.at[y, x] if sweep == 0 else plane1.at[place]
        for k, device in enumerate((sibling, partner, diagonal)):
            into = (columns0, columns1)[sweep].at[k]
            remote(mine, into, column_ssem.at[sweep], column_rsem.at[sweep], device).start()

    def to_lane(tiles, c, total):
        for v, tile in enumerate(tiles):
            q = c * CHUNK + v
            total = jnp.where(lane == q, pltpu.roll(tile, (q + 1) if c == 0 else q, axis=1), total)
        return total

    def corner_rows(n, g):
        return pl.ds(pl.multiple_of(n * ROWS + g * CHUNK, CHUNK), CHUNK)

    def gather(g):
        here = pl.ds(pl.multiple_of(g * CHUNK, CHUNK), CHUNK)
        for n in range(2):
            total = jnp.zeros((CHUNK, LANES), jnp.float32)
            for c in range(2):
                at = pl.ds(c * LANES, LANES)
                total = to_lane([flow0[n, v, rows_at(g), at] for v in range(NV)] + [step[here, at]], c, total)
            corner[corner_rows(n, g), :] = total

    def turn_first():
        turned = corner[...].T
        for c in range(2):
            plane0[y, x, c] = turned[c * CHUNK : c * CHUNK + NV, :]
            pace_lanes[c] = turned[c * CHUNK + NV : c * CHUNK + NV + 1, :]

    def turn_border():
        turned = corner[...].T
        for c in range(2):
            before[c] = turned[c * CHUNK : c * CHUNK + NV, :]

    def donor(c, n):
        return (stator_donor if c == 0 else rotor_donor)[n, 0]

    def halves(first, second, n):
        if n == 0:
            return jnp.where(low, first, pltpu.roll(second, ROWS, axis=1))
        return jnp.where(low, pltpu.roll(first, ROWS, axis=1), second)

    def forward():
        for c in range(2):
            for n in range(2):
                ahead = (donor(c, n) // ROWS + SPACE - space) % SPACE
                found = []
                for d in (ahead, (ahead + 1) % SPACE):
                    dx, dz, dy = d // LAYER, (d // SY) % SZ, d % SY
                    carry = (y + dy) // SY
                    wants = (z + 2 * SZ - dz - carry) % SZ
                    over = (wants + dz + carry) // SZ
                    found.append(plane0[(y + dy) % SY, (x + dx + over) % SX, c])
                ring0[z, c * 2 + n] = halves(*found, n)

    def from_ring(c, n):
        block = donor(c, n) // ROWS
        here = ring0[(block // SY) % SZ, c * 2 + n]
        there = ring0[((block + 1) // SY) % SZ, c * 2 + n]
        return jnp.where(low, here, there)

    def pass_across():
        for c in range(2):
            for n in range(2):
                block = donor(c, n) // ROWS
                cross[x, c * 2 + n] = halves(plane1[block % LAYER, c], plane1[(block + 1) % LAYER, c], n)

    def from_cross(c, n):
        block = donor(c, n) // ROWS
        here = cross[(block // LAYER) % SX, c * 2 + n]
        there = cross[((block + 1) // LAYER) % SX, c * 2 + n]
        return jnp.where(low, here, there)

    def sum_columns(sweep):
        columns = (columns0, columns1)[sweep]
        sums = []
        for c in range(2):
            total = None
            for k, table in enumerate((from_sib, to_own, to_sib)):
                straight = columns[k, c]
                turned = pltpu.roll(straight, ROWS, axis=1)
                same = jnp.where(low, table[0][0], table[1][1])
                crossed = jnp.where(low, table[0][1], table[1][0])
                term = same * straight + crossed * turned
                total = term if total is None else total + term
            sums.append(total)
        return sums

    def settle(sweep, remote_sum):
        entering = []
        for c in range(2):
            weights = stator_weight if c == 0 else rotor_weight
            values = []
            for n in range(2):
                window = from_ring(c, n) if sweep == 0 else from_cross(c, n)
                offset = donor(c, n) % ROWS
                first = pltpu.roll(window, (LANES - offset) % LANES, axis=1)
                second = pltpu.roll(window, LANES - 1 - offset, axis=1)
                weight = weights[pl.ds(n, 1), :]
                weight = jnp.concatenate([weight, weight], axis=1)
                values.append((1.0 - weight) * first + weight * second)
            entering.append(jnp.where(low, values[0], pltpu.roll(values[1], ROWS, axis=1)))
        stator, rotor = entering
        share_lanes[0] = -VISCOSITY * rotor
        share_lanes[1] = -VISCOSITY * stator
        for v in range(NV):
            total = share_lanes[1, pl.ds(v, 1), :]
            for w in range(NV):
                total = total - jac[v, w] * stator[w : w + 1, :]
            share_lanes[1, pl.ds(v, 1), :] = total
        for c in range(2):
            share_lanes[c] = share_lanes[c] + remote_sum[c]

    def turn_share():
        corner[...] = jnp.zeros_like(corner)
        for t in range(2):
            corner[pl.ds(t * CHUNK, NV), :] = share_lanes[t]
        share_rows[...] = corner[...].T

    def spread(own, other, into):
        for v in range(NV):
            for t in range(2):
                at = pl.ds(t * LANES, LANES)
                ours, theirs = [own(n, v, at) for n in range(2)], [other(n, v, at) for n in range(2)]
                for a in range(2):
                    into[a, v, :, at] = (
                        to_own[a][0] * ours[0] + to_own[a][1] * ours[1]
                        + (to_sib[a][0] * theirs[0] + to_sib[a][1] * theirs[1])
                    )

    def mix(sweep, g):
        flow, sib, send = (flow0, sib0, send0) if sweep == 0 else (flow1, sib1, send1)
        spread(lambda n, v, at: flow[n, v, rows_at(g), at], lambda n, v, at: sib[g, n, v, :, at], send.at[g])

    def mix_raw():
        spread(lambda n, v, at: raw[0, n, v, :, at], lambda n, v, at: raw[1, n, v, :, at], recv0.at[order(0)])

    def inner(flow, g, t):
        here = pl.ds(pl.multiple_of(g * CHUNK, CHUNK), CHUNK)
        jacobian = [[jac[v, w] for w in range(NV)] for v in range(NV)]
        at = pl.ds(t * LANES, LANES)
        centre = [[flow[n, v, rows_at(g), at] for v in range(NV)] for n in range(2)]
        parts = []
        for n in range(2):
            diff, smooth = [], []
            for v in range(NV):
                window = flow[n, v, pl.ds(pl.multiple_of(g * CHUNK, CHUNK), 3 * CHUNK), at]
                upper = window[CHUNK - 1 : 2 * CHUNK - 1]
                lower = window[CHUNK + 1 : 2 * CHUNK + 1]
                f = centre[n][v]
                left = jnp.where(lane == 0, 0.0, pltpu.roll(f, 1, axis=1))
                right = jnp.where(lane == LANES - 1, 0.0, pltpu.roll(f, LANES - 1, axis=1))
                diff.append(f - left)
                smooth.append(VISCOSITY * (4.0 * f - left - right - upper - lower))
            row = []
            for v in range(NV):
                convect = jacobian[v][0] * diff[0]
                for w in range(1, NV):
                    convect = convect + jacobian[v][w] * diff[w]
                derivative = from_own[n][0] * centre[0][v] + from_own[n][1] * centre[1][v]
                row.append(convect + smooth[v] + derivative - source[n, v, here, at])
            parts.append(row)
        return centre, parts

    def border(g):
        here = pl.ds(pl.multiple_of(g * CHUNK, CHUNK), CHUNK)
        totals = [jnp.zeros((CHUNK, LANES), jnp.float32) for _ in range(2)]
        for t in range(2):
            pace = step[here, pl.ds(t * LANES, LANES)]
            centre, parts = inner(flow0, g, t)
            for n in range(2):
                totals[n] = to_lane([centre[n][v] - pace * parts[n][v] for v in range(NV)], t, totals[n])
        for n in range(2):
            corner[corner_rows(n, g), :] = totals[n]

    def advance(sweep, g):
        flow, sib, recv = (flow0, sib0, recv0) if sweep == 0 else (flow1, sib1, recv1)
        here = pl.ds(pl.multiple_of(g * CHUNK, CHUNK), CHUNK)
        for t in range(2):
            at = pl.ds(t * LANES, LANES)
            pace = step[here, at]
            edge = lane == (LANES - 1 if t == 0 else 0)
            centre, parts = inner(flow, g, t)
            for n in range(2):
                for v in range(NV):
                    others = (
                        from_sib[n][0] * sib[g, 0, v, :, at] + from_sib[n][1] * sib[g, 1, v, :, at]
                        + recv[g, n, v, :, at]
                    )
                    residual = parts[n][v] + jnp.where(edge, 0.0, others)
                    new = centre[n][v] - pace * residual
                    if sweep == 0:
                        flow1[n, v, rows_at(g), at] = new
                    else:
                        out_state[n, v, here, at] = new
                        out_resid[n, v, here, at] = residual

    def patch(sweep, g):
        here = pl.ds(pl.multiple_of(g * CHUNK, CHUNK), CHUNK)
        for n in range(2):
            shares = share_rows[corner_rows(n, g), :]
            for t in range(2):
                at = pl.ds(t * LANES, LANES)
                edge = lane == (LANES - 1 if t == 0 else 0)
                pace = step[here, at]
                for v in range(NV):
                    share = jnp.where(edge, pltpu.roll(shares, LANES - 1 - v if t == 0 else LANES - CHUNK - v, axis=1), 0.0)
                    if sweep == 0:
                        flow1[n, v, rows_at(g), at] = flow1[n, v, rows_at(g), at] - pace * share
                    else:
                        out_state[n, v, here, at] = out_state[n, v, here, at] - pace * share
                        out_resid[n, v, here, at] = out_resid[n, v, here, at] + share

    def loop(body, begin=0, end=CHUNKS):
        def wrapped(g, carry):
            body(g)
            return carry

        lax.fori_loop(begin, end, wrapped, 0)

    step_in.wait()
    flow_in.wait()
    loop(gather)
    turn_first()
    pack_halos(0)
    hear(barrier, nearest)
    cross_copy(0).start()
    raw_copy().start()
    loop(lambda p: sib_copy(0, order(p)).start())
    tell(known.at[0], rounds[0])
    start_first_halos()

    def first_mix(p):
        g = order(p)
        sib_copy(0, g).wait_recv()
        mix(0, g)
        par_copy(0, g).start()

    loop(first_mix, 1, FIRST)
    start_columns(0)
    hear(known.at[0], rounds[0])
    tell(known.at[1], rounds[1])
    loop(first_mix, FIRST, CHUNKS)
    for copy in small_in:
        copy.wait()
    source_in.wait()
    cross_arrival(0).wait_recv()
    start_planes()
    hear(known.at[1], rounds[1])
    tell(known.at[2], rounds[2])
    loop(border, 1, CHUNKS - 1)
    raw_copy().wait_recv()
    raw_pass().start()

    def when(places):
        low_z, high_z = places
        return (1 - z // (SZ // 2)) * (low_z - high_z) + high_z

    at_rings, at_halos, at_settle, at_layer = (when(a) for a in (AT_RINGS, AT_HALOS, AT_SETTLE, AT_LAYER))
    ahead = when(AHEAD)

    def second_mix(p):
        g = order(p)
        sib_copy(1, g).wait_recv()
        mix(1, g)

        @pl.when(p < ahead)
        def _():
            par_copy(1, g).start()

    def first_sweep(p):
        g = order(p)

        @pl.when(p == at_rings)
        def _():
            hear(known.at[2], rounds[2])
            pass_halos()
            all_done(plane0.at[pl.ds(0, SY - 1)], plane_rsem.at[0])
            forward()
            start_rings()

        @pl.when(p == at_halos)
        def _():
            unpack_halos(0)
            border(0)
            border(CHUNKS - 1)
            turn_border()

        @pl.when(p == at_settle)
        def _():
            all_done(columns0, column_rsem.at[0])
            remote_sum = sum_columns(0)
            all_done(ring0.at[pl.ds(0, SZ - 1)], ring_rsem.at[0])
            settle(0, remote_sum)
            for c in range(2):
                plane1[place, c] = before[c] - pace_lanes[c] * share_lanes[c]
            start_layer()
            start_columns(1)
            turn_share()

        @pl.when(p == 0)
        def _():
            sib_copy(0, g).wait_recv()
            raw_pass().wait_recv()
            mix_raw()

        @pl.when(p > 0)
        def _():
            par_copy(0, g).wait_recv()

        advance(0, g)
        sib_copy(1, g).start()

        @pl.when(p > 0)
        def _():
            second_mix(p - 1)

    loop(first_sweep)
    second_mix(CHUNKS - 1)
    all_done(sib1, sib_ssem.at[1])
    loop(lambda g: patch(0, g))
    pack_halos(1)
    start_halos(1)

    def second_sweep(p):
        g = order(p)

        @pl.when(p == at_layer)
        def _():
            all_done(plane1.at[pl.ds(0, LAYER - 1)], layer_rsem.at[0])
            pass_across()
            cross_copy(1).start()

        @pl.when(p == CHUNKS - 1)
        def _():
            all_done(columns1, column_rsem.at[1])
            remote_sum = sum_columns(1)
            cross_arrival(1).wait_recv()
            settle(1, remote_sum)
            turn_share()
            loop(lambda g: patch(1, g), 1, CHUNKS)

        @pl.when(p == AT_SECOND_HALOS)
        def _():
            unpack_halos(1)

        par_copy(1, g).wait_recv()

        @pl.when(jnp.logical_and(p + PACE >= ahead, p + PACE < CHUNKS))
        def _():
            par_copy(1, order(p + PACE)).start()

        advance(1, g)

    loop(second_sweep)
    patch(1, 0)

    all_done(sib0, sib_ssem.at[0])
    all_done(send0.at[pl.ds(0, CHUNKS - 1)], par_ssem.at[0])
    raw_copy().wait_send()
    raw_pass().wait_send()
    all_done(send1, par_ssem.at[1])
    all_done(columns0, column_ssem.at[0])
    all_done(columns1, column_ssem.at[1])
    all_done(plane0.at[pl.ds(0, SY - 1)], plane_ssem.at[0])
    all_done(ring0.at[pl.ds(0, SZ - 1)], ring_ssem.at[0])
    all_done(plane1.at[pl.ds(0, LAYER - 1)], layer_ssem.at[0])
    for sweep in range(2):
        cross_copy(sweep).wait_send()
        all_done(halos_out[sweep], halo_ssem.at[sweep])

    @pl.when(jnp.logical_or(first_in_ring, last_in_ring))
    def _():
        all_done(relay, halo_ssem.at[0])


def store(state, resid, state_hbm, resid_hbm, sems):
    copies = [
        pltpu.make_async_copy(state, state_hbm, sems.at[0]),
        pltpu.make_async_copy(resid, resid_hbm, sems.at[1]),
    ]
    for copy in copies:
        copy.start()
    for copy in copies:
        copy.wait()


def local(flow_state, flow_source, pseudo_step, flux_jacobian, stator_donor, stator_weight, rotor_donor, rotor_weight):
    f32 = jnp.float32
    block = (2, NV, ROWS, AX)
    padded = (2, NV, ROWS + 2 * CHUNK, AX)
    chunked = (CHUNKS, 2, NV, CHUNK, AX)
    anywhere = pl.BlockSpec(memory_space=pltpu.HBM)
    vmem = pl.BlockSpec(memory_space=pltpu.VMEM)
    dma = pltpu.SemaphoreType.DMA
    regular = pltpu.SemaphoreType.REGULAR
    halo = (2, 2, NV, AX)
    args = (
        flow_state, flow_source, pseudo_step, flux_jacobian, stator_donor, stator_weight, rotor_donor, rotor_weight
    )
    state, resid = pl.pallas_call(
        kernel,
        out_shape=(pltpu.VMEM(block, f32), pltpu.VMEM(block, f32)),
        in_specs=[anywhere] * 8,
        out_specs=(vmem, vmem),
        scratch_shapes=[
            pltpu.SMEM((NV, NV), f32),
            pltpu.SMEM((2, ROWS), jnp.int32),
            pltpu.VMEM((2, ROWS), f32),
            pltpu.SMEM((2, ROWS), jnp.int32),
            pltpu.VMEM((2, ROWS), f32),
            pltpu.VMEM(padded, f32),
            pltpu.VMEM(padded, f32),
            pltpu.VMEM(block, f32),
            pltpu.VMEM((ROWS, AX), f32),
            *[pltpu.VMEM(chunked, f32) for _ in range(6)],
            pltpu.VMEM((LANES, LANES), f32),
            pltpu.VMEM((SY, SX, 2, NV, LANES), f32),
            pltpu.VMEM((SZ * SY, 2, NV, LANES), f32),
            pltpu.VMEM((SZ, 4, NV, LANES), f32),
            pltpu.VMEM((SX, 4, NV, LANES), f32),
            *[pltpu.VMEM((3, 2, NV, LANES), f32) for _ in range(2)],
            pltpu.VMEM((2, NV, LANES), f32),
            pltpu.VMEM((2, 1, LANES), f32),
            pltpu.VMEM((2, NV, LANES), f32),
            pltpu.VMEM((LANES, LANES), f32),
            *[pltpu.VMEM(halo, f32) for _ in range(4)],
            pltpu.VMEM(halo[1:], f32),
            dma((1,)),
            pltpu.VMEM((2, *chunked[1:]), f32),
            dma((2,)),
            dma((2,)),
            regular((3,)),
            dma((8,)),
            dma((2,)),
            dma((2 * CHUNKS,)),
            dma((2,)),
            dma((2 * CHUNKS,)),
            dma((2,)),
            dma((2,)),
            *[dma((1,)) for _ in range(6)],
            dma((2,)),
            dma((2,)),
            dma((2,)),
            dma((2,)),
        ],
        compiler_params=pltpu.CompilerParams(
            collective_id=0, has_side_effects=True, vmem_limit_bytes=24 * 2**20
        ),
    )(*[pltpu.with_memory_space_constraint(arg, pltpu.HBM) for arg in args])
    return pl.pallas_call(
        store,
        out_shape=(pltpu.HBM(block, f32), pltpu.HBM(block, f32)),
        in_specs=[vmem, vmem],
        out_specs=(anywhere, anywhere),
        scratch_shapes=[dma((2,))],
    )(
        pltpu.with_memory_space_constraint(state, pltpu.VMEM), pltpu.with_memory_space_constraint(resid, pltpu.VMEM)
    )


def solution(mesh):
    return jax.shard_map(
        local,
        mesh=mesh,
        in_specs=(
            P("inst", None, "space", None),
            P("inst", None, "space", None),
            P("space", None),
            P(),
            P("inst", "space"),
            P("inst", "space"),
            P("inst", "space"),
            P("inst", "space"),
        ),
        out_specs=(P("inst", None, "space", None), P("inst", None, "space", None)),
        check_vma=False,
    )
```
